128 devices in a mesh: var: 64 (over z, y, x), samp: 2 (over core).
Axes of the slice: x: 4, y: 4, z: 4, core: 2. Of those that a mesh axis runs over, the one named last changes fastest.
Arguments:
- dosages: bfloat16 [8192, 32768], P(('var', 'samp'))
- band_width: int32 [256], P('var'), may hold values from 7 to 8, as said below
Outputs:
- ld_tiles: float32 [256, 9, 128, 128], P('var', None, 'samp')
The draws below stay inside these ranges and needn't reach their ends.
Inputs may be any that keep to these rules, and one draw needn't show every extreme that they name: `band_width`: some panel has band width 8, and some other panel has band width 8 - 1.
All inputs are finite; a program needn't handle non-finite values.
Results may differ from the reference program's by a relative error of at most 0.00092.
Values may be sent and summed in bfloat16 or wider, within the bound.
A program may use at most 128 MiB of HBM per device.

```python
import jax
import jax.numpy as jnp
from jax import lax

PANEL = 128
WMAX = 8
NPANEL = 256
VARIANTS = 32768
SAMPLES = 8192


def draw_dosages(key, part):
    key = jax.random.fold_in(key, 11)
    key_shared, key_noise, key_strength, key_offset = jax.random.split(key, 4)
    shared = jax.random.normal(key_shared, (SAMPLES, PANEL), jnp.float32)
    noise = jax.random.normal(key_noise, (SAMPLES, VARIANTS), jnp.float32)
    strength = jax.random.uniform(key_strength, (VARIANTS,), jnp.float32, 0.3, 2.0)
    offset = jax.random.uniform(key_offset, (VARIANTS,), jnp.float32, -1.5, 1.5)
    latent = jnp.tile(shared, (1, VARIANTS // PANEL))
    values = 2.0 * jax.nn.sigmoid(offset + strength * latent + noise)
    return values.astype(jnp.bfloat16)


def draw_band_width(key, part):
    key = jax.random.fold_in(key, 5)
    key_width, key_spot, key_other = jax.random.split(key, 3)
    widths = jax.random.randint(key_width, (NPANEL,), WMAX - 1, WMAX + 1, dtype=jnp.int32)
    spot = jax.random.randint(key_spot, (), 0, NPANEL, dtype=jnp.int32)
    step = jax.random.randint(key_other, (), 1, NPANEL, dtype=jnp.int32)
    other_spot = (spot + step) % NPANEL
    widths = widths.at[spot].set(WMAX)
    return widths.at[other_spot].set(WMAX - 1)


def setup_inputs(seed: int = 0) -> dict:
    streams_of = jax.random.split(jax.random.key(seed), 3)
    dosages = draw_dosages(jax.random.fold_in(streams_of[2], 71), 0)
    band_width = draw_band_width(jax.random.fold_in(streams_of[2], 71), 0)
    return {"dosages": dosages, "band_width": band_width}


def reference(dosages, band_width):
    panel_ids = jnp.arange(NPANEL, dtype=jnp.int32)

    def panel_moments(index):
        block = lax.dynamic_slice_in_dim(dosages, index * PANEL, PANEL, 1).astype(jnp.float32)
        return (lax.optimization_barrier(jnp.sum(block, 0)), lax.optimization_barrier(jnp.sum(block * block, 0)))
    first_sum, second_sum = lax.map(panel_moments, panel_ids)
    mean_value = first_sum / SAMPLES
    inv_scale = lax.rsqrt(second_sum / SAMPLES - mean_value * mean_value + 1e-05)

    def standardize(index):
        block = lax.dynamic_slice_in_dim(dosages, index * PANEL, PANEL, 1).astype(jnp.float32)
        return ((block - mean_value[index]) * inv_scale[index]).astype(jnp.bfloat16)
    standard = lax.map(standardize, panel_ids)
    offsets = jnp.arange(WMAX + 1, dtype=jnp.int32)

    def band_row(index):

        def one_tile(offset):
            other = jnp.minimum(index + offset, NPANEL - 1)
            tile = jnp.dot(standard[index].T, standard[other], preferred_element_type=jnp.float32)
            keep_tile = (offset <= band_width[index]) & (index + offset < NPANEL)
            return jnp.where(keep_tile, tile, jnp.zeros_like(tile))
        return lax.map(one_tile, offsets)
    return lax.map(band_row, panel_ids) / SAMPLES
```

```python
import jax
import jax.numpy as jnp
from jax import lax
from jax.experimental import pallas as pl
from jax.experimental.pallas import tpu as pltpu
from jax.sharding import PartitionSpec as P

MESH = pl.DeviceIdType.MESH
WMAX = 8
PANEL = 128
SIDE = 4
GROUPS = SIDE * SIDE
OWN = 4
CHUNK = OWN * PANEL
GROUP_COLS = SIDE * CHUNK
HALO_COLS = WMAX * PANEL
COLS = GROUP_COLS + HALO_COLS
CHUNKS = COLS // CHUNK
ROWS = 64
LOCAL = GROUPS * ROWS
SAMPLES = 8192
OFFSETS = [(0, 1), (1, 0), (0, 3), (3, 0), (1, 1), (3, 3), (1, 3), (3, 1),
           (0, 2), (2, 0), (1, 2), (2, 1), (3, 2), (2, 3), (2, 2)]


def position():
    var = lax.axis_index("var")
    return var // SIDE, lax.rem(var, SIDE), lax.axis_index("samp")


def group_at(group, dz, dy):
    z, y = group // SIDE, lax.rem(group, SIDE)
    return lax.rem(z + dz, SIDE) * SIDE + lax.rem(y + dy, SIDE)


def exchange_kernel(dos_ref, out_ref, send_sem, recv_sem, local_sem):
    group, x, core = position()
    barrier = pltpu.get_barrier_semaphore()
    for dz, dy in OFFSETS:
        other = group_at(group, dz, dy)
        pl.semaphore_signal(barrier, inc=1, device_id=(other * SIDE + x, core), device_id_type=MESH)
    pl.semaphore_wait(barrier, len(OFFSETS))

    def parts(other):
        first = pl.multiple_of(other * GROUP_COLS, GROUP_COLS)
        after = pl.multiple_of(lax.rem(other + 1, GROUPS) * GROUP_COLS, GROUP_COLS)
        return ((pl.ds(first, GROUP_COLS), pl.ds(0, GROUP_COLS)), (pl.ds(after, HALO_COLS), pl.ds(GROUP_COLS, HALO_COLS)))

    copies = []
    for index, (dz, dy) in enumerate(OFFSETS):
        other = group_at(group, dz, dy)
        for part, (source, target) in enumerate(parts(other)):
            copy = pltpu.make_async_remote_copy(
                src_ref=dos_ref.at[:, source],
                dst_ref=out_ref.at[index, :, target],
                send_sem=send_sem.at[index, part],
                recv_sem=recv_sem.at[index, part],
                device_id=(other * SIDE + x, core),
                device_id_type=MESH,
            )
            copy.start()
            copies.append(copy)
    own = []
    for part, (source, target) in enumerate(parts(group)):
        copy = pltpu.make_async_copy(
            dos_ref.at[:, source], out_ref.at[len(OFFSETS), :, target], local_sem.at[part]
        )
        copy.start()
        own.append(copy)
    for copy in own + copies:
        copy.wait()


def exchange(dosages):
    count = len(OFFSETS)
    return pl.pallas_call(
        exchange_kernel,
        out_shape=jax.ShapeDtypeStruct((GROUPS, ROWS, COLS), dosages.dtype),
        in_specs=[pl.BlockSpec(memory_space=pl.ANY)],
        out_specs=pl.BlockSpec(memory_space=pl.ANY),
        scratch_shapes=[
            pltpu.SemaphoreType.DMA((count, 2)),
            pltpu.SemaphoreType.DMA((count, 2)),
            pltpu.SemaphoreType.DMA((2,)),
        ],
        compiler_params=pltpu.CompilerParams(collective_id=0, has_side_effects=True),
        name="exchange",
    )(dosages)


RING = [2, 1, 3, 0]
BLOCK = 2 * PANEL


def tiles_kernel(
    dos_ref, out_ref, sums, scale, standard, turned, part, twin, ring,
    stat_send, stat_recv, twin_send, twin_recv, ring_send, ring_recv,
):
    group, x, core = position()
    me = x * 2 + core
    peers = []
    for dx in range(SIDE):
        for dc in range(2):
            if dx or dc:
                peer_x, peer_c = lax.rem(x + dx, SIDE), lax.rem(core + dc, 2)
                peers.append((group * SIDE + peer_x, peer_c))
    barrier = pltpu.get_barrier_semaphore()
    for peer in peers:
        pl.semaphore_signal(barrier, inc=1, device_id=peer, device_id_type=MESH)

    sums[0] = jnp.zeros((16, CHUNK), jnp.float32)

    def chunk_sums(chunk, carry):
        columns = pl.ds(pl.multiple_of(chunk * CHUNK, CHUNK), CHUNK)

        def add(step, totals):
            rows = pl.ds(pl.multiple_of(step * 64, 64), 64)
            values = dos_ref[rows, columns].astype(jnp.float32).reshape(8, 8, CHUNK)
            return totals[0] + jnp.sum(values, 0), totals[1] + jnp.sum(values * values, 0)

        zero = jnp.zeros((8, CHUNK), jnp.float32)
        first, second = lax.fori_loop(0, LOCAL // 64, add, (zero, zero))
        sums[0, pl.ds(chunk, 1), :] = jnp.sum(first, 0, keepdims=True)
        sums[0, pl.ds(chunk + 8, 1), :] = jnp.sum(second, 0, keepdims=True)
        return carry

    lax.fori_loop(0, CHUNKS, chunk_sums, 0)
    pl.semaphore_wait(barrier, len(peers))
    stat_copies = []
    for index, peer in enumerate(peers):
        copy = pltpu.make_async_remote_copy(
            src_ref=sums.at[0],
            dst_ref=sums.at[index + 1],
            send_sem=stat_send.at[index],
            recv_sem=stat_recv.at[index],
            device_id=peer,
            device_id_type=MESH,
        )
        copy.start()
        stat_copies.append(copy)
    for copy in stat_copies:
        copy.wait()
    totals = jnp.sum(sums[...], 0)
    mean = totals[0:8] * (1.0 / SAMPLES)
    inv_scale = lax.rsqrt(totals[8:16] * (1.0 / SAMPLES) - mean * mean + 1e-05)
    scale[0:8, :] = mean
    scale[8:16, :] = inv_scale

    def standardize(chunk, carry):
        columns = pl.ds(pl.multiple_of(chunk * CHUNK, CHUNK), CHUNK)
        mean = scale[pl.ds(chunk, 1), :]
        inv_scale = scale[pl.ds(chunk + 8, 1), :]

        def rows_of(step, carry):
            rows = pl.ds(pl.multiple_of(step * 64, 64), 64)
            values = dos_ref[rows, columns].astype(jnp.float32)
            standard[chunk, rows, :] = ((values - mean) * inv_scale).astype(jnp.bfloat16)
            return carry

        return lax.fori_loop(0, LOCAL // 64, rows_of, carry)

    lax.fori_loop(0, CHUNKS, standardize, 0)

    twin_copies = []
    for slot, distance in enumerate(RING):
        rows_chunk = lax.rem(x + distance, SIDE)
        turned[...] = standard[rows_chunk].T
        for d in range(WMAX // OWN + 1):
            for pp in range(OWN // 2):
                for qq in range(OWN // 2):
                    if d * OWN + 2 * qq + 1 < 2 * pp or d * OWN + 2 * qq - (2 * pp + 1) > WMAX:
                        continue
                    block = jnp.dot(
                        turned[pp * BLOCK:(pp + 1) * BLOCK, :],
                        standard[rows_chunk + d, :, qq * BLOCK:(qq + 1) * BLOCK],
                        preferred_element_type=jnp.float32,
                    )
                    for p in range(2):
                        for q in range(2):
                            row = 2 * pp + p
                            k = d * OWN + 2 * qq + q - row
                            if 0 <= k <= WMAX:
                                for half in range(2):
                                    start = p * PANEL + half * 64
                                    part[slot, half, row, k] = block[start:start + 64, q * PANEL:(q + 1) * PANEL]
        copy = pltpu.make_async_remote_copy(
            src_ref=part.at[slot, 1 - core],
            dst_ref=twin.at[slot],
            send_sem=twin_send.at[slot],
            recv_sem=twin_recv.at[slot],
            device_id=(group * SIDE + x, 1 - core),
            device_id_type=MESH,
        )
        copy.start()
        twin_copies.append(copy)

    ring_copies = []
    for slot, distance in enumerate(RING):
        twin_copies[slot].wait()
        if distance == 0:
            continue
        part[slot, core] = part[slot, core] + twin[slot]
        copy = pltpu.make_async_remote_copy(
            src_ref=part.at[slot, core],
            dst_ref=ring.at[slot],
            send_sem=ring_send.at[slot],
            recv_sem=ring_recv.at[slot],
            device_id=(group * SIDE + lax.rem(x + distance, SIDE), core),
            device_id_type=MESH,
        )
        copy.start()
        ring_copies.append(copy)
    for copy in ring_copies:
        copy.wait()
    last = len(RING) - 1
    out_ref[...] = part[last, core] + twin[last] + (ring[0] + ring[1] + ring[2])


def tiles(received):
    tile_shape = (OWN, WMAX + 1, PANEL // 2, PANEL)
    return pl.pallas_call(
        tiles_kernel,
        out_shape=jax.ShapeDtypeStruct(tile_shape, jnp.float32),
        in_specs=[pl.BlockSpec(memory_space=pltpu.VMEM)],
        out_specs=pl.BlockSpec(memory_space=pltpu.VMEM),
        scratch_shapes=[
            pltpu.VMEM((8, 16, CHUNK), jnp.float32),
            pltpu.VMEM((16, CHUNK), jnp.float32),
            pltpu.VMEM((CHUNKS, LOCAL, CHUNK), jnp.bfloat16),
            pltpu.VMEM((CHUNK, LOCAL), jnp.bfloat16),
            pltpu.VMEM((SIDE, 2) + tile_shape, jnp.float32),
            pltpu.VMEM((SIDE,) + tile_shape, jnp.float32),
            pltpu.VMEM((SIDE - 1,) + tile_shape, jnp.float32),
            pltpu.SemaphoreType.DMA((7,)),
            pltpu.SemaphoreType.DMA((7,)),
            pltpu.SemaphoreType.DMA((SIDE,)),
            pltpu.SemaphoreType.DMA((SIDE,)),
            pltpu.SemaphoreType.DMA((SIDE - 1,)),
            pltpu.SemaphoreType.DMA((SIDE - 1,)),
        ],
        compiler_params=pltpu.CompilerParams(
            collective_id=1, has_side_effects=True, vmem_limit_bytes=56 * 1024 * 1024
        ),
        name="tiles",
    )(received)


def per_device(dosages, band_width):
    received = exchange(dosages)
    band_tiles = tiles(received.reshape(LOCAL, COLS))
    offsets = jnp.arange(WMAX + 1, dtype=jnp.int32)
    panel_count = OWN * lax.axis_size("var")
    global_panel = lax.axis_index("var") * OWN + jnp.arange(OWN, dtype=jnp.int32)
    in_band = (offsets[None, :] <= band_width[:, None]) & (
        global_panel[:, None] + offsets[None, :] < panel_count
    )
    return jnp.where(in_band[:, :, None, None], band_tiles * (1.0 / SAMPLES), 0.0)


def solution(mesh):
    in_specs = (P(("var", "samp"), None), P("var"))
    out_specs = P("var", None, "samp", None)
    return jax.shard_map(
        per_device, mesh=mesh, in_specs=in_specs, out_specs=out_specs, check_vma=False
    )
```

```python
import jax
import jax.numpy as jnp
from jax import lax
from jax.experimental import pallas as pl
from jax.experimental.pallas import tpu as pltpu
from jax.sharding import PartitionSpec as P

MESH = pl.DeviceIdType.MESH
WMAX = 8
PANEL = 128
SIDE = 4
GROUPS = SIDE * SIDE
OWN = 4
CHUNK = OWN * PANEL
GROUP_COLS = SIDE * CHUNK
HALO_COLS = WMAX * PANEL
COLS = GROUP_COLS + HALO_COLS
CHUNKS = COLS // CHUNK
ROWS = 64
LOCAL = GROUPS * ROWS
SAMPLES = 8192
PAIRS = [((2, 2), (3, 3)), ((0, 1), (1, 0)), ((1, 2), (0, 3)), ((2, 1), (3, 0)), ((2, 3), (3, 2)), ((1, 3), (3, 1)),
         ((0, 2), (2, 0)), ((1, 1), (1, 1))]
FIRST = [one for one, _ in PAIRS] + [two for _, two in PAIRS[:-1]]
SECOND = [two for _, two in PAIRS] + [one for one, _ in PAIRS[:-1]]


def position():
    var = lax.axis_index("var")
    return var // SIDE, lax.rem(var, SIDE), lax.axis_index("samp")


def group_at(group, offset):
    z, y = group // SIDE, lax.rem(group, SIDE)
    return lax.rem(z + offset // SIDE, SIDE) * SIDE + lax.rem(y + lax.rem(offset, SIDE), SIDE)


def offset_at(core, step):
    one, two = (dz * SIDE + dy for dz, dy in (FIRST[step], SECOND[step]))
    return one + core * (two - one)


def exchange_kernel(dos_ref, out_ref, send_sem, recv_sem, local_sem):
    group, x, core = position()
    barrier = pltpu.get_barrier_semaphore()
    for offset in range(1, GROUPS):
        pl.semaphore_signal(
            barrier, inc=1, device_id=(group_at(group, offset) * SIDE + x, core), device_id_type=MESH
        )
    pl.semaphore_wait(barrier, GROUPS - 1)

    def parts(other):
        first = pl.multiple_of(other * GROUP_COLS, GROUP_COLS)
        after = pl.multiple_of(lax.rem(other + 1, GROUPS) * GROUP_COLS, GROUP_COLS)
        return ((pl.ds(first, GROUP_COLS), pl.ds(0, GROUP_COLS)), (pl.ds(after, HALO_COLS), pl.ds(GROUP_COLS, HALO_COLS)))

    copies = []
    for step in range(GROUPS - 1):
        offset = offset_at(core, step)
        other = group_at(group, offset)
        for part, (source, target) in enumerate(parts(other)):
            copy = pltpu.make_async_remote_copy(
                src_ref=dos_ref.at[:, source],
                dst_ref=out_ref.at[offset, :, target],
                send_sem=send_sem.at[offset, part],
                recv_sem=recv_sem.at[offset, part],
                device_id=(other * SIDE + x, core),
                device_id_type=MESH,
            )
            copy.start()
            copies.append(copy)
    own = []
    for part, (source, target) in enumerate(parts(group)):
        copy = pltpu.make_async_copy(dos_ref.at[:, source], out_ref.at[0, :, target], local_sem.at[part])
        copy.start()
        own.append(copy)
    for copy in own + copies:
        copy.wait()


def exchange(dosages):
    return pl.pallas_call(
        exchange_kernel,
        out_shape=jax.ShapeDtypeStruct((GROUPS, ROWS, COLS), dosages.dtype),
        in_specs=[pl.BlockSpec(memory_space=pl.ANY)],
        out_specs=pl.BlockSpec(memory_space=pl.ANY),
        scratch_shapes=[
            pltpu.SemaphoreType.DMA((GROUPS, 2)),
            pltpu.SemaphoreType.DMA((GROUPS, 2)),
            pltpu.SemaphoreType.DMA((2,)),
        ],
        compiler_params=pltpu.CompilerParams(collective_id=0, has_side_effects=True),
        name="exchange",
    )(dosages)


RING = [2, 1, 3, 0]
BLOCK = 2 * PANEL


def tiles_kernel(
    dos_ref, out_ref, sums, scale, standard, turned, part, twin, relay, ring,
    stat_send, stat_recv, twin_send, twin_recv, ring_send, ring_recv,
):
    group, x, core = position()
    me = x * 2 + core
    peers = []
    for dx in range(SIDE):
        for dc in range(2):
            if dx or dc:
                peer_x, peer_c = lax.rem(x + dx, SIDE), lax.rem(core + dc, 2)
                peers.append((group * SIDE + peer_x, peer_c))
    barrier = pltpu.get_barrier_semaphore()
    for peer in peers:
        pl.semaphore_signal(barrier, inc=1, device_id=peer, device_id_type=MESH)

    sums[0] = jnp.zeros((16, CHUNK), jnp.float32)

    def chunk_sums(chunk, carry):
        columns = pl.ds(pl.multiple_of(chunk * CHUNK, CHUNK), CHUNK)

        def add(step, totals):
            rows = pl.ds(pl.multiple_of(step * 64, 64), 64)
            values = dos_ref[rows, columns].astype(jnp.float32).reshape(8, 8, CHUNK)
            return totals[0] + jnp.sum(values, 0), totals[1] + jnp.sum(values * values, 0)

        zero = jnp.zeros((8, CHUNK), jnp.float32)
        first, second = lax.fori_loop(0, LOCAL // 64, add, (zero, zero))
        sums[0, pl.ds(chunk, 1), :] = jnp.sum(first, 0, keepdims=True)
        sums[0, pl.ds(chunk + 8, 1), :] = jnp.sum(second, 0, keepdims=True)
        return carry

    lax.fori_loop(0, CHUNKS, chunk_sums, 0)
    pl.semaphore_wait(barrier, len(peers))
    stat_copies = []
    for index, peer in enumerate(peers):
        copy = pltpu.make_async_remote_copy(
            src_ref=sums.at[0],
            dst_ref=sums.at[index + 1],
            send_sem=stat_send.at[index],
            recv_sem=stat_recv.at[index],
            device_id=peer,
            device_id_type=MESH,
        )
        copy.start()
        stat_copies.append(copy)
    for copy in stat_copies:
        copy.wait()
    totals = jnp.sum(sums[...], 0)
    mean = totals[0:8] * (1.0 / SAMPLES)
    inv_scale = lax.rsqrt(totals[8:16] * (1.0 / SAMPLES) - mean * mean + 1e-05)
    scale[0:8, :] = mean
    scale[8:16, :] = inv_scale

    def standardize(chunk, carry):
        columns = pl.ds(pl.multiple_of(chunk * CHUNK, CHUNK), CHUNK)
        mean = scale[pl.ds(chunk, 1), :]
        inv_scale = scale[pl.ds(chunk + 8, 1), :]

        def rows_of(step, carry):
            rows = pl.ds(pl.multiple_of(step * 64, 64), 64)
            values = dos_ref[rows, columns].astype(jnp.float32)
            standard[chunk, rows, :] = ((values - mean) * inv_scale).astype(jnp.bfloat16)
            return carry

        return lax.fori_loop(0, LOCAL // 64, rows_of, carry)

    lax.fori_loop(0, CHUNKS, standardize, 0)

    def chip_at(distance):
        return group * SIDE + lax.rem(x + distance, SIDE)

    def multiply(slot):
        rows_chunk = lax.rem(x + RING[slot], SIDE)
        turned[...] = standard[rows_chunk].T
        for d in range(WMAX // OWN + 1):
            for pp in range(OWN // 2):
                for qq in range(OWN // 2):
                    if d * OWN + 2 * qq + 1 < 2 * pp or d * OWN + 2 * qq - (2 * pp + 1) > WMAX:
                        continue
                    block = jnp.dot(
                        turned[pp * BLOCK:(pp + 1) * BLOCK, :],
                        standard[rows_chunk + d, :, qq * BLOCK:(qq + 1) * BLOCK],
                        preferred_element_type=jnp.float32,
                    )
                    for p in range(2):
                        for q in range(2):
                            row = 2 * pp + p
                            k = d * OWN + 2 * qq + q - row
                            if 0 <= k <= WMAX:
                                for half in range(2):
                                    start = p * PANEL + half * 64
                                    part[slot, half, row, k] = block[start:start + 64, q * PANEL:(q + 1) * PANEL]
        copy = pltpu.make_async_remote_copy(
            src_ref=part.at[slot, 1 - core],
            dst_ref=twin.at[slot],
            send_sem=twin_send.at[slot],
            recv_sem=twin_recv.at[slot],
            device_id=(group * SIDE + x, 1 - core),
            device_id_type=MESH,
        )
        copy.start()
        return copy

    def send(slot, half, target, index, distance):
        copy = pltpu.make_async_remote_copy(
            src_ref=part.at[slot, core, pl.ds(2 * half, 2)],
            dst_ref=target,
            send_sem=ring_send.at[index],
            recv_sem=ring_recv.at[index],
            device_id=(chip_at(distance), core),
            device_id_type=MESH,
        )
        copy.start()
        return copy

    twins = [multiply(0), multiply(1)]
    twins[0].wait()
    part[0, core] = part[0, core] + twin[0]
    forth = send(0, 0, relay.at[0], 0, 1)
    back = send(0, 1, relay.at[1], 1, 3)
    twins.append(multiply(2))
    twins[1].wait()
    part[1, core] = part[1, core] + twin[1]
    sent = [send(1, 1, ring.at[0, pl.ds(2, 2)], 2, 1)]
    twins.append(multiply(3))
    twins[2].wait()
    part[2, core] = part[2, core] + twin[2]
    sent.append(send(2, 0, ring.at[1, pl.ds(0, 2)], 3, 3))
    forth.wait()
    part[1, core, 0:2] = part[1, core, 0:2] + relay[0]
    sent.append(send(1, 0, ring.at[0, pl.ds(0, 2)], 4, 1))
    back.wait()
    part[2, core, 2:4] = part[2, core, 2:4] + relay[1]
    sent.append(send(2, 1, ring.at[1, pl.ds(2, 2)], 5, 3))
    twins[3].wait()
    part[3, core] = part[3, core] + twin[3]
    for copy in sent:
        copy.wait()
    out_ref[...] = part[3, core] + (ring[0] + ring[1])


def tiles(received):
    tile_shape = (OWN, WMAX + 1, PANEL // 2, PANEL)
    return pl.pallas_call(
        tiles_kernel,
        out_shape=jax.ShapeDtypeStruct(tile_shape, jnp.float32),
        in_specs=[pl.BlockSpec(memory_space=pltpu.VMEM)],
        out_specs=pl.BlockSpec(memory_space=pltpu.VMEM),
        scratch_shapes=[
            pltpu.VMEM((8, 16, CHUNK), jnp.float32),
            pltpu.VMEM((16, CHUNK), jnp.float32),
            pltpu.VMEM((CHUNKS, LOCAL, CHUNK), jnp.bfloat16),
            pltpu.VMEM((CHUNK, LOCAL), jnp.bfloat16),
            pltpu.VMEM((SIDE, 2) + tile_shape, jnp.float32),
            pltpu.VMEM((SIDE,) + tile_shape, jnp.float32),
            pltpu.VMEM((2, 2) + tile_shape[1:], jnp.float32),
            pltpu.VMEM((2,) + tile_shape, jnp.float32),
            pltpu.SemaphoreType.DMA((7,)),
            pltpu.SemaphoreType.DMA((7,)),
            pltpu.SemaphoreType.DMA((SIDE,)),
            pltpu.SemaphoreType.DMA((SIDE,)),
            pltpu.SemaphoreType.DMA((6,)),
            pltpu.SemaphoreType.DMA((6,)),
        ],
        compiler_params=pltpu.CompilerParams(
            collective_id=1, has_side_effects=True, vmem_limit_bytes=56 * 1024 * 1024
        ),
        name="tiles",
    )(received)


def per_device(dosages, band_width):
    received = exchange(dosages)
    band_tiles = tiles(received.reshape(LOCAL, COLS))
    offsets = jnp.arange(WMAX + 1, dtype=jnp.int32)
    panel_count = OWN * lax.axis_size("var")
    global_panel = lax.axis_index("var") * OWN + jnp.arange(OWN, dtype=jnp.int32)
    in_band = (offsets[None, :] <= band_width[:, None]) & (
        global_panel[:, None] + offsets[None, :] < panel_count
    )
    return jnp.where(in_band[:, :, None, None], band_tiles * (1.0 / SAMPLES), 0.0)


def solution(mesh):
    in_specs = (P(("var", "samp"), None), P("var"))
    out_specs = P("var", None, "samp", None)
    return jax.shard_map(
        per_device, mesh=mesh, in_specs=in_specs, out_specs=out_specs, check_vma=False
    )
```

```python
import jax
import jax.numpy as jnp
from jax import lax
from jax.experimental import pallas as pl
from jax.experimental.pallas import tpu as pltpu
from jax.sharding import PartitionSpec as P

MESH = pl.DeviceIdType.MESH
WMAX = 8
PANEL = 128
SIDE = 4
GROUPS = SIDE * SIDE
OWN = 4
CHUNK = OWN * PANEL
GROUP_COLS = SIDE * CHUNK
HALO_COLS = WMAX * PANEL
COLS = GROUP_COLS + HALO_COLS
CHUNKS = COLS // CHUNK
ROWS = 64
LOCAL = GROUPS * ROWS
SAMPLES = 8192
PAIRS = [((2, 2), (3, 3)), ((0, 1), (1, 0)), ((1, 2), (0, 3)), ((2, 1), (3, 0)), ((2, 3), (3, 2)), ((1, 3), (3, 1)),
         ((0, 2), (2, 0)), ((1, 1), (1, 1))]
FIRST = [one for one, _ in PAIRS] + [two for _, two in PAIRS[:-1]]
SECOND = [two for _, two in PAIRS] + [one for one, _ in PAIRS[:-1]]


def position():
    var = lax.axis_index("var")
    return var // SIDE, lax.rem(var, SIDE), lax.axis_index("samp")


def group_at(group, offset):
    z, y = group // SIDE, lax.rem(group, SIDE)
    return lax.rem(z + offset // SIDE, SIDE) * SIDE + lax.rem(y + lax.rem(offset, SIDE), SIDE)


def offset_at(core, step):
    one, two = (dz * SIDE + dy for dz, dy in (FIRST[step], SECOND[step]))
    return one + core * (two - one)


RING = [2, 1, 3, 0]
BLOCK = 2 * PANEL


def tiles_kernel(
    dos_ref, out_ref, local, received, adds, sums, scale, standard, turned, part, twin, relay, ring,
    stage_sem, own_sem, swap_send, swap_recv, stat_send, stat_recv, twin_send, twin_recv, ring_send, ring_recv,
):
    group, x, core = position()
    stage = pltpu.make_async_copy(dos_ref, local, stage_sem)
    stage.start()
    peers = []
    for dx in range(SIDE):
        for dc in range(2):
            if dx or dc:
                peer_x, peer_c = lax.rem(x + dx, SIDE), lax.rem(core + dc, 2)
                peers.append((group * SIDE + peer_x, peer_c))
    barrier = pltpu.get_barrier_semaphore()
    for offset in range(1, GROUPS):
        pl.semaphore_signal(
            barrier, inc=1, device_id=(group_at(group, offset) * SIDE + x, core), device_id_type=MESH
        )
    for peer in peers:
        pl.semaphore_signal(barrier, inc=1, device_id=peer, device_id_type=MESH)
    adds[...] = jnp.zeros(adds.shape, jnp.float32)
    sums[0] = jnp.zeros((16, CHUNK), jnp.float32)
    stage.wait()
    pl.semaphore_wait(barrier, GROUPS - 1 + len(peers))

    def parts(other):
        first = pl.multiple_of(other * GROUP_COLS, GROUP_COLS)
        after = pl.multiple_of(lax.rem(other + 1, GROUPS) * GROUP_COLS, GROUP_COLS)
        return (
            (local.at[:, pl.ds(first, GROUP_COLS)], pl.ds(0, GROUP_COLS)),
            (local.at[:, pl.ds(after, HALO_COLS)], pl.ds(GROUP_COLS, HALO_COLS)),
        )

    swaps = []
    for step in range(GROUPS - 1):
        offset = offset_at(core, step)
        other = group_at(group, offset)
        for index, (source, target) in enumerate(parts(other)):
            copy = pltpu.make_async_remote_copy(
                src_ref=source,
                dst_ref=received.at[offset, :, target],
                send_sem=swap_send.at[offset, index],
                recv_sem=swap_recv.at[offset, index],
                device_id=(other * SIDE + x, core),
                device_id_type=MESH,
            )
            copy.start()
            swaps.append(copy)
    own = []
    for index, (source, target) in enumerate(parts(group)):
        copy = pltpu.make_async_copy(source, received.at[0, :, target], own_sem.at[index])
        copy.start()
        own.append(copy)

    def add_moments(slot):
        def chunk_moments(chunk, carry):
            columns = pl.ds(pl.multiple_of(chunk * CHUNK, CHUNK), CHUNK)
            values = received[slot, :, columns].astype(jnp.float32).reshape(8, ROWS // 8, CHUNK)
            adds[0, :, columns] = adds[0, :, columns] + jnp.sum(values, 0)
            adds[1, :, columns] = adds[1, :, columns] + jnp.sum(values * values, 0)
            return carry

        lax.fori_loop(0, CHUNKS, chunk_moments, 0)

    for copy in own:
        copy.wait()
    add_moments(0)
    for step in range(GROUPS - 1):
        for copy in swaps[2 * step:2 * step + 2]:
            copy.wait()
        add_moments(offset_at(core, step))
    for chunk in range(CHUNKS):
        columns = slice(chunk * CHUNK, (chunk + 1) * CHUNK)
        sums[0, chunk:chunk + 1, :] = jnp.sum(adds[0, :, columns], 0, keepdims=True)
        sums[0, chunk + 8:chunk + 9, :] = jnp.sum(adds[1, :, columns], 0, keepdims=True)
    stat_copies = []
    for index, peer in enumerate(peers):
        copy = pltpu.make_async_remote_copy(
            src_ref=sums.at[0],
            dst_ref=sums.at[index + 1],
            send_sem=stat_send.at[index],
            recv_sem=stat_recv.at[index],
            device_id=peer,
            device_id_type=MESH,
        )
        copy.start()
        stat_copies.append(copy)
    for copy in stat_copies:
        copy.wait()
    totals = jnp.sum(sums[...], 0)
    mean = totals[0:8] * (1.0 / SAMPLES)
    inv_scale = lax.rsqrt(totals[8:16] * (1.0 / SAMPLES) - mean * mean + 1e-05)
    scale[0:8, :] = mean
    scale[8:16, :] = inv_scale

    def standardize(chunk, carry):
        columns = pl.ds(pl.multiple_of(chunk * CHUNK, CHUNK), CHUNK)
        mean = scale[pl.ds(chunk, 1), :]
        inv_scale = scale[pl.ds(chunk + 8, 1), :]

        def rows_of(step, carry):
            rows = pl.ds(pl.multiple_of(step * ROWS, ROWS), ROWS)
            values = received[step, :, columns].astype(jnp.float32)
            standard[chunk, rows, :] = ((values - mean) * inv_scale).astype(jnp.bfloat16)
            return carry

        return lax.fori_loop(0, GROUPS, rows_of, carry)

    lax.fori_loop(0, CHUNKS, standardize, 0)

    def chip_at(distance):
        return group * SIDE + lax.rem(x + distance, SIDE)

    def multiply(slot):
        rows_chunk = lax.rem(x + RING[slot], SIDE)
        turned[...] = standard[rows_chunk].T
        for d in range(WMAX // OWN + 1):
            for pp in range(OWN // 2):
                for qq in range(OWN // 2):
                    if d * OWN + 2 * qq + 1 < 2 * pp or d * OWN + 2 * qq - (2 * pp + 1) > WMAX:
                        continue
                    block = jnp.dot(
                        turned[pp * BLOCK:(pp + 1) * BLOCK, :],
                        standard[rows_chunk + d, :, qq * BLOCK:(qq + 1) * BLOCK],
                        preferred_element_type=jnp.float32,
                    )
                    for p in range(2):
                        for q in range(2):
                            row = 2 * pp + p
                            k = d * OWN + 2 * qq + q - row
                            if 0 <= k <= WMAX:
                                for half in range(2):
                                    start = p * PANEL + half * 64
                                    part[slot, half, row, k] = block[start:start + 64, q * PANEL:(q + 1) * PANEL]
        copy = pltpu.make_async_remote_copy(
            src_ref=part.at[slot, 1 - core],
            dst_ref=twin.at[slot],
            send_sem=twin_send.at[slot],
            recv_sem=twin_recv.at[slot],
            device_id=(group * SIDE + x, 1 - core),
            device_id_type=MESH,
        )
        copy.start()
        return copy

    def send(slot, half, target, index, distance):
        copy = pltpu.make_async_remote_copy(
            src_ref=part.at[slot, core, pl.ds(2 * half, 2)],
            dst_ref=target,
            send_sem=ring_send.at[index],
            recv_sem=ring_recv.at[index],
            device_id=(chip_at(distance), core),
            device_id_type=MESH,
        )
        copy.start()
        return copy

    twins = [multiply(0), multiply(1)]
    twins[0].wait()
    part[0, core] = part[0, core] + twin[0]
    forth = send(0, 0, relay.at[0], 0, 1)
    back = send(0, 1, relay.at[1], 1, 3)
    twins.append(multiply(2))
    twins[1].wait()
    part[1, core] = part[1, core] + twin[1]
    sent = [send(1, 1, ring.at[0, pl.ds(2, 2)], 2, 1)]
    twins.append(multiply(3))
    twins[2].wait()
    part[2, core] = part[2, core] + twin[2]
    sent.append(send(2, 0, ring.at[1, pl.ds(0, 2)], 3, 3))
    forth.wait()
    part[1, core, 0:2] = part[1, core, 0:2] + relay[0]
    sent.append(send(1, 0, ring.at[0, pl.ds(0, 2)], 4, 1))
    back.wait()
    part[2, core, 2:4] = part[2, core, 2:4] + relay[1]
    sent.append(send(2, 1, ring.at[1, pl.ds(2, 2)], 5, 3))
    twins[3].wait()
    part[3, core] = part[3, core] + twin[3]
    for copy in sent:
        copy.wait()
    out_ref[...] = part[3, core] + (ring[0] + ring[1])


def tiles(dosages):
    tile_shape = (OWN, WMAX + 1, PANEL // 2, PANEL)
    return pl.pallas_call(
        tiles_kernel,
        out_shape=jax.ShapeDtypeStruct(tile_shape, jnp.float32),
        in_specs=[pl.BlockSpec(memory_space=pl.ANY)],
        out_specs=pl.BlockSpec(memory_space=pltpu.VMEM),
        scratch_shapes=[
            pltpu.VMEM(dosages.shape, jnp.bfloat16),
            pltpu.VMEM((GROUPS, ROWS, COLS), jnp.bfloat16),
            pltpu.VMEM((2, 8, COLS), jnp.float32),
            pltpu.VMEM((8, 16, CHUNK), jnp.float32),
            pltpu.VMEM((16, CHUNK), jnp.float32),
            pltpu.VMEM((CHUNKS, LOCAL, CHUNK), jnp.bfloat16),
            pltpu.VMEM((CHUNK, LOCAL), jnp.bfloat16),
            pltpu.VMEM((SIDE, 2) + tile_shape, jnp.float32),
            pltpu.VMEM((SIDE,) + tile_shape, jnp.float32),
            pltpu.VMEM((2, 2) + tile_shape[1:], jnp.float32),
            pltpu.VMEM((2,) + tile_shape, jnp.float32),
            pltpu.SemaphoreType.DMA,
            pltpu.SemaphoreType.DMA((2,)),
            pltpu.SemaphoreType.DMA((GROUPS, 2)),
            pltpu.SemaphoreType.DMA((GROUPS, 2)),
            pltpu.SemaphoreType.DMA((7,)),
            pltpu.SemaphoreType.DMA((7,)),
            pltpu.SemaphoreType.DMA((SIDE,)),
            pltpu.SemaphoreType.DMA((SIDE,)),
            pltpu.SemaphoreType.DMA((6,)),
            pltpu.SemaphoreType.DMA((6,)),
        ],
        compiler_params=pltpu.CompilerParams(
            collective_id=0, has_side_effects=True, vmem_limit_bytes=56 * 1024 * 1024
        ),
        name="tiles",
    )(dosages)


def per_device(dosages, band_width):
    band_tiles = tiles(dosages)
    offsets = jnp.arange(WMAX + 1, dtype=jnp.int32)
    panel_count = OWN * lax.axis_size("var")
    global_panel = lax.axis_index("var") * OWN + jnp.arange(OWN, dtype=jnp.int32)
    in_band = (offsets[None, :] <= band_width[:, None]) & (
        global_panel[:, None] + offsets[None, :] < panel_count
    )
    return jnp.where(in_band[:, :, None, None], band_tiles * (1.0 / SAMPLES), 0.0)


def solution(mesh):
    in_specs = (P(("var", "samp"), None), P("var"))
    out_specs = P("var", None, "samp", None)
    return jax.shard_map(
        per_device, mesh=mesh, in_specs=in_specs, out_specs=out_specs, check_vma=False
    )
```

```python
import jax
import jax.numpy as jnp
from jax import lax
from jax.experimental import pallas as pl
from jax.experimental.pallas import tpu as pltpu
from jax.sharding import PartitionSpec as P

MESH = pl.DeviceIdType.MESH
WMAX = 8
PANEL = 128
SIDE = 4
GROUPS = SIDE * SIDE
OWN = 4
CHUNK = OWN * PANEL
GROUP_COLS = SIDE * CHUNK
HALO_COLS = WMAX * PANEL
COLS = GROUP_COLS + HALO_COLS
CHUNKS = COLS // CHUNK
ROWS = 64
LOCAL = GROUPS * ROWS
SAMPLES = 8192
HALF = ROWS // 2


def position():
    var = lax.axis_index("var")
    return var // SIDE, lax.rem(var, SIDE), lax.axis_index("samp")


RING = [2, 1, 3, 0]
BLOCK = 2 * PANEL


def tiles_kernel(
    dos_ref, out_ref, staged, middle, passing, received, adds, sums, scale, standard, turned, part, twin, relay, ring,
    stage_sem, own_sem, swap_send, swap_recv, stat_send, stat_recv, twin_send, twin_recv, ring_send, ring_recv,
):
    group, x, core = position()
    z, y = group // SIDE, lax.rem(group, SIDE)
    stages = []
    for other in range(GROUPS):
        after = (other + 1) % GROUPS * GROUP_COLS
        block = staged.at[other // SIDE, other % SIDE]
        for index, (source, target) in enumerate((
            (pl.ds(other * GROUP_COLS, GROUP_COLS), pl.ds(0, GROUP_COLS)),
            (pl.ds(after, HALO_COLS), pl.ds(GROUP_COLS, HALO_COLS)),
        )):
            copy = pltpu.make_async_copy(dos_ref.at[:, source], block.at[:, target], stage_sem.at[other, index])
            copy.start()
            stages.append(copy)
    peers = []
    for dx in range(SIDE):
        for dc in range(2):
            if dx or dc:
                peer_x, peer_c = lax.rem(x + dx, SIDE), lax.rem(core + dc, 2)
                peers.append((group * SIDE + peer_x, peer_c))
    def along_y(step):
        return (z * SIDE + lax.rem(y + step, SIDE)) * SIDE + x, core

    def along_z(step):
        return (lax.rem(z + step, SIDE) * SIDE + y) * SIDE + x, core

    neighbours = [along_y(1), along_y(3), along_z(1), along_z(3)]
    barrier = pltpu.get_barrier_semaphore()
    for peer in neighbours + peers:
        pl.semaphore_signal(barrier, inc=1, device_id=peer, device_id_type=MESH)
    adds[...] = jnp.zeros(adds.shape, jnp.float32)
    sums[0] = jnp.zeros((16, CHUNK), jnp.float32)
    for copy in stages:
        copy.wait()
    pl.semaphore_wait(barrier, len(neighbours) + len(peers))

    places = ((y, z), (z, y))
    routes = ((along_y, along_z), (along_z, along_y))
    EVERY = pl.ds(0, SIDE)

    def rows_of_half(half):
        return pl.ds(half * HALF, HALF)

    def staged_for(half, place, others):
        if half == 0:
            return staged.at[others, place, rows_of_half(half)]
        return staged.at[place, others, rows_of_half(half)]

    def received_from(half, distance, others):
        if half == 0:
            return received.at[distance, others, rows_of_half(half)]
        return received.at[others, distance, rows_of_half(half)]

    def begin(half, phase, kind, way, source, target):
        copy = pltpu.make_async_remote_copy(
            src_ref=source,
            dst_ref=target,
            send_sem=swap_send.at[half, phase, kind, way],
            recv_sem=swap_recv.at[half, phase, kind, way],
            device_id=routes[half][phase](1 + 2 * way),
            device_id_type=MESH,
        )
        copy.start()
        return copy

    def keep(half, phase, source, target):
        copy = pltpu.make_async_copy(source, target, own_sem.at[half, phase])
        copy.start()
        return copy

    both = [(half, way) for way in range(2) for half in range(2)]

    def place_at(half, phase, step):
        return lax.rem(places[half][phase] + step, SIDE)

    far = {
        (half, way): begin(
            half, 0, 0, way, staged_for(half, place_at(half, 0, 2), pl.ds(2 * way, 2)), passing.at[half, 0, way]
        )
        for half, way in both
    }
    near = {
        (half, way): begin(
            half, 0, 1, way, staged_for(half, place_at(half, 0, 1 + 2 * way), EVERY), middle.at[half, 1 + 2 * way]
        )
        for half, way in both
    }
    kept = [keep(half, 0, staged_for(half, places[half][0], EVERY), middle.at[half, 0]) for half in range(2)]
    passed = {}
    for half, way in both:
        far[half, way].wait()
        passed[half, way] = begin(
            half, 0, 2, way, passing.at[half, 0, way], middle.at[half, 2, pl.ds(2 * way, 2)]
        )
    for copy in kept:
        copy.wait()
    for key in both:
        near[key].wait()
    far = {}
    for half, way in both:
        if way == 1:
            passed[half, 0].wait()
            passed[half, 1].wait()
        far[half, way] = begin(
            half, 1, 0, way, middle.at[half, pl.ds(2 * way, 2), place_at(half, 1, 2)], passing.at[half, 1, way]
        )
    near = {
        (half, way): begin(
            half, 1, 1, way,
            middle.at[half, EVERY, place_at(half, 1, 1 + 2 * way)],
            received_from(half, 1 + 2 * way, EVERY),
        )
        for half, way in both
    }
    kept = [
        keep(half, 1, middle.at[half, EVERY, places[half][1]], received_from(half, 0, EVERY)) for half in range(2)
    ]

    def add_moments(half, distance):
        def block_moments(step, carry):
            other, chunk = step // CHUNKS, lax.rem(step, CHUNKS)
            columns = pl.ds(pl.multiple_of(chunk * CHUNK, CHUNK), CHUNK)
            block = received_from(half, distance, other)
            values = block[:, columns].astype(jnp.float32).reshape(HALF // 8, 8, CHUNK)
            adds[0, :, columns] = adds[0, :, columns] + jnp.sum(values, 0)
            adds[1, :, columns] = adds[1, :, columns] + jnp.sum(values * values, 0)
            return carry

        lax.fori_loop(0, SIDE * CHUNKS, block_moments, 0)

    for half in range(2):
        kept[half].wait()
        add_moments(half, 0)
    passed = {}
    for half, way in both:
        far[half, way].wait()
        passed[half, way] = begin(
            half, 1, 2, way, passing.at[half, 1, way], received_from(half, 2, pl.ds(2 * way, 2))
        )
    for half, way in both:
        near[half, way].wait()
        add_moments(half, 1 + 2 * way)
    for half in range(2):
        passed[half, 0].wait()
        passed[half, 1].wait()
        add_moments(half, 2)
    for chunk in range(CHUNKS):
        columns = slice(chunk * CHUNK, (chunk + 1) * CHUNK)
        sums[0, chunk:chunk + 1, :] = jnp.sum(adds[0, :, columns], 0, keepdims=True)
        sums[0, chunk + 8:chunk + 9, :] = jnp.sum(adds[1, :, columns], 0, keepdims=True)
    stat_copies = []
    for index, peer in enumerate(peers):
        copy = pltpu.make_async_remote_copy(
            src_ref=sums.at[0],
            dst_ref=sums.at[index + 1],
            send_sem=stat_send.at[index],
            recv_sem=stat_recv.at[index],
            device_id=peer,
            device_id_type=MESH,
        )
        copy.start()
        stat_copies.append(copy)
    for copy in stat_copies:
        copy.wait()
    totals = jnp.sum(sums[...], 0)
    mean = totals[0:8] * (1.0 / SAMPLES)
    inv_scale = lax.rsqrt(totals[8:16] * (1.0 / SAMPLES) - mean * mean + 1e-05)
    scale[0:8, :] = mean
    scale[8:16, :] = inv_scale

    def standardize(chunk, carry):
        columns = pl.ds(pl.multiple_of(chunk * CHUNK, CHUNK), CHUNK)
        mean = scale[pl.ds(chunk, 1), :]
        inv_scale = scale[pl.ds(chunk + 8, 1), :]

        def rows_of(step, carry):
            rows = pl.ds(pl.multiple_of(step * ROWS, ROWS), ROWS)
            values = received[step // SIDE, lax.rem(step, SIDE), :, columns].astype(jnp.float32)
            standard[chunk, rows, :] = ((values - mean) * inv_scale).astype(jnp.bfloat16)
            return carry

        return lax.fori_loop(0, GROUPS, rows_of, carry)

    lax.fori_loop(0, CHUNKS, standardize, 0)

    def chip_at(distance):
        return group * SIDE + lax.rem(x + distance, SIDE)

    def multiply(slot):
        rows_chunk = lax.rem(x + RING[slot], SIDE)
        turned[...] = standard[rows_chunk].T
        for d in range(WMAX // OWN + 1):
            for pp in range(OWN // 2):
                for qq in range(OWN // 2):
                    if d * OWN + 2 * qq + 1 < 2 * pp or d * OWN + 2 * qq - (2 * pp + 1) > WMAX:
                        continue
                    block = jnp.dot(
                        turned[pp * BLOCK:(pp + 1) * BLOCK, :],
                        standard[rows_chunk + d, :, qq * BLOCK:(qq + 1) * BLOCK],
                        preferred_element_type=jnp.float32,
                    )
                    for p in range(2):
                        for q in range(2):
                            row = 2 * pp + p
                            k = d * OWN + 2 * qq + q - row
                            if 0 <= k <= WMAX:
                                for half in range(2):
                                    start = p * PANEL + half * 64
                                    part[slot, half, row, k] = block[start:start + 64, q * PANEL:(q + 1) * PANEL]
        copy = pltpu.make_async_remote_copy(
            src_ref=part.at[slot, 1 - core],
            dst_ref=twin.at[slot],
            send_sem=twin_send.at[slot],
            recv_sem=twin_recv.at[slot],
            device_id=(group * SIDE + x, 1 - core),
            device_id_type=MESH,
        )
        copy.start()
        return copy

    def send(slot, half, target, index, distance):
        copy = pltpu.make_async_remote_copy(
            src_ref=part.at[slot, core, pl.ds(2 * half, 2)],
            dst_ref=target,
            send_sem=ring_send.at[index],
            recv_sem=ring_recv.at[index],
            device_id=(chip_at(distance), core),
            device_id_type=MESH,
        )
        copy.start()
        return copy

    twins = [multiply(0), multiply(1)]
    twins[0].wait()
    part[0, core] = part[0, core] + twin[0]
    forth = send(0, 0, relay.at[0], 0, 1)
    back = send(0, 1, relay.at[1], 1, 3)
    twins.append(multiply(2))
    twins[1].wait()
    part[1, core] = part[1, core] + twin[1]
    sent = [send(1, 1, ring.at[0, pl.ds(2, 2)], 2, 1)]
    twins.append(multiply(3))
    twins[2].wait()
    part[2, core] = part[2, core] + twin[2]
    sent.append(send(2, 0, ring.at[1, pl.ds(0, 2)], 3, 3))
    forth.wait()
    part[1, core, 0:2] = part[1, core, 0:2] + relay[0]
    sent.append(send(1, 0, ring.at[0, pl.ds(0, 2)], 4, 1))
    back.wait()
    part[2, core, 2:4] = part[2, core, 2:4] + relay[1]
    sent.append(send(2, 1, ring.at[1, pl.ds(2, 2)], 5, 3))
    twins[3].wait()
    part[3, core] = part[3, core] + twin[3]
    for copy in sent:
        copy.wait()
    out_ref[...] = part[3, core] + (ring[0] + ring[1])


def tiles(dosages):
    tile_shape = (OWN, WMAX + 1, PANEL // 2, PANEL)
    return pl.pallas_call(
        tiles_kernel,
        out_shape=jax.ShapeDtypeStruct(tile_shape, jnp.float32),
        in_specs=[pl.BlockSpec(memory_space=pl.ANY)],
        out_specs=pl.BlockSpec(memory_space=pltpu.VMEM),
        scratch_shapes=[
            pltpu.VMEM((SIDE, SIDE, ROWS, COLS), jnp.bfloat16),
            pltpu.VMEM((2, SIDE, SIDE, HALF, COLS), jnp.bfloat16),
            pltpu.VMEM((2, 2, 2, 2, HALF, COLS), jnp.bfloat16),
            pltpu.VMEM((SIDE, SIDE, ROWS, COLS), jnp.bfloat16),
            pltpu.VMEM((2, 8, COLS), jnp.float32),
            pltpu.VMEM((8, 16, CHUNK), jnp.float32),
            pltpu.VMEM((16, CHUNK), jnp.float32),
            pltpu.VMEM((CHUNKS, LOCAL, CHUNK), jnp.bfloat16),
            pltpu.VMEM((CHUNK, LOCAL), jnp.bfloat16),
            pltpu.VMEM((SIDE, 2) + tile_shape, jnp.float32),
            pltpu.VMEM((SIDE,) + tile_shape, jnp.float32),
            pltpu.VMEM((2, 2) + tile_shape[1:], jnp.float32),
            pltpu.VMEM((2,) + tile_shape, jnp.float32),
            pltpu.SemaphoreType.DMA((GROUPS, 2)),
            pltpu.SemaphoreType.DMA((2, 2)),
            pltpu.SemaphoreType.DMA((2, 2, 3, 2)),
            pltpu.SemaphoreType.DMA((2, 2, 3, 2)),
            pltpu.SemaphoreType.DMA((7,)),
            pltpu.SemaphoreType.DMA((7,)),
            pltpu.SemaphoreType.DMA((SIDE,)),
            pltpu.SemaphoreType.DMA((SIDE,)),
            pltpu.SemaphoreType.DMA((6,)),
            pltpu.SemaphoreType.DMA((6,)),
        ],
        compiler_params=pltpu.CompilerParams(
            collective_id=0, has_side_effects=True, vmem_limit_bytes=60 * 1024 * 1024
        ),
        name="tiles",
    )(dosages)


def per_device(dosages, band_width):
    band_tiles = tiles(dosages)
    offsets = jnp.arange(WMAX + 1, dtype=jnp.int32)
    panel_count = OWN * lax.axis_size("var")
    global_panel = lax.axis_index("var") * OWN + jnp.arange(OWN, dtype=jnp.int32)
    in_band = (offsets[None, :] <= band_width[:, None]) & (
        global_panel[:, None] + offsets[None, :] < panel_count
    )
    return jnp.where(in_band[:, :, None, None], band_tiles * (1.0 / SAMPLES), 0.0)


def solution(mesh):
    in_specs = (P(("var", "samp"), None), P("var"))
    out_specs = P("var", None, "samp", None)
    return jax.shard_map(
        per_device, mesh=mesh, in_specs=in_specs, out_specs=out_specs, check_vma=False
    )
```

```python
import jax
import jax.numpy as jnp
from jax import lax
from jax.experimental import pallas as pl
from jax.experimental.pallas import tpu as pltpu
from jax.sharding import PartitionSpec as P

MESH = pl.DeviceIdType.MESH
WMAX = 8
PANEL = 128
SIDE = 4
GROUPS = SIDE * SIDE
OWN = 4
CHUNK = OWN * PANEL
REACH = WMAX // OWN
CHUNKS = SIDE + REACH
ROWS = 64
HALF = ROWS // 2
LOCAL = GROUPS * ROWS
SAMPLES = 8192
BLOCK = 2 * PANEL
PLACES = [
    [(p, q) for p in range(OWN) for q in range(OWN) if 0 <= d * OWN + q - p <= WMAX] for d in range(REACH + 1)
]
STARTS = [sum(len(places) for places in PLACES[:d]) for d in range(REACH + 2)]
TILES = STARTS[-1]


def position():
    var = lax.axis_index("var")
    return var // SIDE, lax.rem(var, SIDE), lax.axis_index("samp")


def tiles_kernel(
    dos_ref, out_ref, staged, middle, passing, received, sums, standard, turned, part, twin, ring,
    stage_sem, own_sem, swap_send, swap_recv, stat_send, stat_recv, twin_send, twin_recv, ring_send, ring_recv,
):
    group, x, core = position()
    z, y = group // SIDE, lax.rem(group, SIDE)

    def stage(chunk):
        def begin_block(other, carry):
            first = pl.multiple_of(lax.rem(other * SIDE + chunk, GROUPS * SIDE) * CHUNK, CHUNK)
            pltpu.make_async_copy(
                dos_ref.at[:, pl.ds(first, CHUNK)],
                staged.at[chunk, other // SIDE, lax.rem(other, SIDE)],
                stage_sem.at[chunk, other],
            ).start()
            return carry

        lax.fori_loop(0, GROUPS, begin_block, 0)

    def stage_wait(chunk):
        def wait_block(other, carry):
            first = pl.multiple_of(lax.rem(other * SIDE + chunk, GROUPS * SIDE) * CHUNK, CHUNK)
            pltpu.make_async_copy(
                dos_ref.at[:, pl.ds(first, CHUNK)],
                staged.at[chunk, other // SIDE, lax.rem(other, SIDE)],
                stage_sem.at[chunk, other],
            ).wait()
            return carry

        lax.fori_loop(0, GROUPS, wait_block, 0)

    for chunk in range(CHUNKS):
        stage(chunk)

    peers = []
    for dx in range(SIDE):
        for dc in range(2):
            if dx or dc:
                peer_x, peer_c = lax.rem(x + dx, SIDE), lax.rem(core + dc, 2)
                peers.append((group * SIDE + peer_x, peer_c))

    def along_y(step):
        return (z * SIDE + lax.rem(y + step, SIDE)) * SIDE + x, core

    def along_z(step):
        return (lax.rem(z + step, SIDE) * SIDE + y) * SIDE + x, core

    neighbours = [along_y(1), along_y(3), along_z(1), along_z(3)]
    barrier = pltpu.get_barrier_semaphore()
    for peer in neighbours + peers:
        pl.semaphore_signal(barrier, inc=1, device_id=peer, device_id_type=MESH)
    stage_wait(0)
    pl.semaphore_wait(barrier, len(neighbours) + len(peers))

    places = ((y, z), (z, y))
    routes = ((along_y, along_z), (along_z, along_y))
    every = pl.ds(0, SIDE)
    both = [(half, way) for way in range(2) for half in range(2)]

    def pick(ref, chunk, half, place, others):
        rows = pl.ds(half * HALF, HALF)
        return ref.at[chunk, others, place, rows] if half == 0 else ref.at[chunk, place, others, rows]

    def landed(chunk, half, distance, others):
        rows = pl.ds(half * HALF, HALF)
        return (
            received.at[chunk, distance, others, rows] if half == 0 else received.at[chunk, others, distance, rows]
        )

    def begin(chunk, half, phase, kind, way, source, target):
        copy = pltpu.make_async_remote_copy(
            src_ref=source,
            dst_ref=target,
            send_sem=swap_send.at[chunk, half, phase, kind, way],
            recv_sem=swap_recv.at[chunk, half, phase, kind, way],
            device_id=routes[half][phase](1 + 2 * way),
            device_id_type=MESH,
        )
        copy.start()
        return copy

    def keep(chunk, half, phase, source, target):
        copy = pltpu.make_async_copy(source, target, own_sem.at[chunk, half, phase])
        copy.start()
        return copy

    def place_at(half, phase, step):
        return lax.rem(places[half][phase] + step, SIDE)

    far, near, passed, kept = {}, {}, {}, {}

    def first_begin(chunk):
        for half, way in both:
            far[chunk, 0, half, way] = begin(
                chunk, half, 0, 0, way,
                pick(staged, chunk, half, place_at(half, 0, 2), pl.ds(2 * way, 2)),
                passing.at[chunk, half, 0, way],
            )
        for half, way in both:
            near[chunk, 0, half, way] = begin(
                chunk, half, 0, 1, way,
                pick(staged, chunk, half, place_at(half, 0, 1 + 2 * way), every),
                middle.at[chunk, half, 1 + 2 * way],
            )
        for half in range(2):
            kept[chunk, 0, half] = keep(
                chunk, half, 0, pick(staged, chunk, half, places[half][0], every), middle.at[chunk, half, 0]
            )

    def first_pass(chunk):
        for half, way in both:
            far[chunk, 0, half, way].wait()
            passed[chunk, 0, half, way] = begin(
                chunk, half, 0, 2, way,
                passing.at[chunk, half, 0, way],
                middle.at[chunk, half, 2, pl.ds(2 * way, 2)],
            )

    def second_begin(chunk):
        for half in range(2):
            kept[chunk, 0, half].wait()
        for half, way in both:
            near[chunk, 0, half, way].wait()
        for half, way in both:
            passed[chunk, 0, half, way].wait()
        for half, way in both:
            far[chunk, 1, half, way] = begin(
                chunk, half, 1, 0, way,
                middle.at[chunk, half, pl.ds(2 * way, 2), place_at(half, 1, 2)],
                passing.at[chunk, half, 1, way],
            )
        for half, way in both:
            near[chunk, 1, half, way] = begin(
                chunk, half, 1, 1, way,
                middle.at[chunk, half, every, place_at(half, 1, 1 + 2 * way)],
                landed(chunk, half, 1 + 2 * way, every),
            )
        for half in range(2):
            kept[chunk, 1, half] = keep(
                chunk, half, 1, middle.at[chunk, half, every, places[half][1]], landed(chunk, half, 0, every)
            )

    def second_pass(chunk):
        for half, way in both:
            far[chunk, 1, half, way].wait()
            passed[chunk, 1, half, way] = begin(
                chunk, half, 1, 2, way,
                passing.at[chunk, half, 1, way],
                landed(chunk, half, 2, pl.ds(2 * way, 2)),
            )

    def second_wait(chunk):
        for half in range(2):
            kept[chunk, 1, half].wait()
        for half, way in both:
            near[chunk, 1, half, way].wait()
        for half, way in both:
            passed[chunk, 1, half, way].wait()

    def block_of(chunk, step):
        return received[chunk, step // SIDE, lax.rem(step, SIDE)].astype(jnp.float32)

    stats = {}

    def moments(chunk):
        def add(step, totals):
            values = block_of(chunk, step).reshape(ROWS // 8, 8, CHUNK)
            return totals[0] + jnp.sum(values, 0), totals[1] + jnp.sum(values * values, 0)

        zero = jnp.zeros((8, CHUNK), jnp.float32)
        totals = lax.fori_loop(0, GROUPS, add, (zero, zero))
        for row, total in enumerate(totals):
            total = jnp.sum(total, 0, keepdims=True)
            for q in range(OWN):
                sums[0, chunk, row * OWN + q:row * OWN + q + 1, :] = total[:, q * PANEL:(q + 1) * PANEL]
        stats[chunk] = []
        for index, peer in enumerate(peers):
            copy = pltpu.make_async_remote_copy(
                src_ref=sums.at[0, chunk],
                dst_ref=sums.at[index + 1, chunk],
                send_sem=stat_send.at[chunk, index],
                recv_sem=stat_recv.at[chunk, index],
                device_id=peer,
                device_id_type=MESH,
            )
            copy.start()
            stats[chunk].append(copy)

    def standardize(chunk):
        for copy in stats[chunk]:
            copy.wait()
        totals = jnp.sum(sums[:, chunk], 0)
        mean = totals[0:OWN] * (1.0 / SAMPLES)
        inv_scale = lax.rsqrt(totals[OWN:2 * OWN] * (1.0 / SAMPLES) - mean * mean + 1e-05)
        mean = jnp.concatenate([mean[q:q + 1] for q in range(OWN)], axis=1)
        inv_scale = jnp.concatenate([inv_scale[q:q + 1] for q in range(OWN)], axis=1)

        def block_standard(step, carry):
            rows = pl.ds(pl.multiple_of(step * ROWS, ROWS), ROWS)
            standard[chunk, rows, :] = ((block_of(chunk, step) - mean) * inv_scale).astype(jnp.bfloat16)
            return carry

        lax.fori_loop(0, GROUPS, block_standard, 0)
        if chunk < SIDE:
            turned[chunk] = standard[chunk].T

    def pieces_of(chunk):
        return [(chunk - d, d) for d in range(REACH + 1) if 0 <= chunk - d < SIDE]

    twins = {}

    def multiply(chunk):
        for rows_chunk, d in pieces_of(chunk):
            for pp in range(OWN // 2):
                for qq in range(OWN // 2):
                    inside = [
                        (p, q) for p in range(2) for q in range(2) if (2 * pp + p, 2 * qq + q) in PLACES[d]
                    ]
                    if not inside:
                        continue
                    block = jnp.dot(
                        turned[rows_chunk, pp * BLOCK:(pp + 1) * BLOCK, :],
                        standard[chunk, :, qq * BLOCK:(qq + 1) * BLOCK],
                        preferred_element_type=jnp.float32,
                    )
                    for p, q in inside:
                        tile = STARTS[d] + PLACES[d].index((2 * pp + p, 2 * qq + q))
                        for half in range(2):
                            first = p * PANEL + half * (PANEL // 2)
                            part[rows_chunk, half, tile] = block[
                                first:first + PANEL // 2, q * PANEL:(q + 1) * PANEL
                            ]
            which = pl.ds(STARTS[d], len(PLACES[d]))
            copy = pltpu.make_async_remote_copy(
                src_ref=part.at[rows_chunk, 1 - core, which],
                dst_ref=twin.at[rows_chunk, which],
                send_sem=twin_send.at[rows_chunk, d],
                recv_sem=twin_recv.at[rows_chunk, d],
                device_id=(group * SIDE + x, 1 - core),
                device_id_type=MESH,
            )
            copy.start()
            twins[rows_chunk, d] = copy

    def ring_copy(rows_chunk, d, slot):
        which = pl.ds(STARTS[d], len(PLACES[d]))
        return pltpu.make_async_remote_copy(
            src_ref=part.at[rows_chunk, core, which],
            dst_ref=ring.at[slot, which],
            send_sem=ring_send.at[rows_chunk, d],
            recv_sem=ring_recv.at[slot, d],
            device_id=(group * SIDE + rows_chunk, core),
            device_id_type=MESH,
        )

    def reduce(chunk):
        for rows_chunk, d in pieces_of(chunk):
            which = pl.ds(STARTS[d], len(PLACES[d]))
            twins[rows_chunk, d].wait()
            part[rows_chunk, core, which] = part[rows_chunk, core, which] + twin[rows_chunk, which]

            @pl.when(x != rows_chunk)
            def _():
                ring_copy(rows_chunk, d, lax.rem(rows_chunk - x + 2 * SIDE - 1, SIDE)).start()

    first_begin(0)
    for chunk in range(1, CHUNKS):
        stage_wait(chunk)
    first_begin(1)
    first_pass(0)
    first_begin(2)
    second_begin(0)
    first_pass(1)
    second_pass(0)
    second_begin(1)
    for chunk in range(CHUNKS):
        second_wait(chunk)
        moments(chunk)
        if chunk + 2 < CHUNKS:
            first_pass(chunk + 2)
        if chunk + 1 < CHUNKS:
            second_pass(chunk + 1)
        standardize(chunk)
        multiply(chunk)
        if chunk + 3 < CHUNKS:
            first_begin(chunk + 3)
        if chunk + 2 < CHUNKS:
            second_begin(chunk + 2)
        reduce(chunk)

    for rows_chunk in range(SIDE):
        for d in range(REACH + 1):

            @pl.when(x != rows_chunk)
            def _():
                ring_copy(rows_chunk, d, lax.rem(rows_chunk - x + 2 * SIDE - 1, SIDE)).wait_send()

            @pl.when(x == rows_chunk)
            def _():
                for slot in range(SIDE - 1):
                    ring_copy(rows_chunk, d, slot).wait_recv()

    for d in range(REACH + 1):
        for index, (p, q) in enumerate(PLACES[d]):
            tile = STARTS[d] + index
            out_ref[p, d * OWN + q - p] = part[x, core, tile] + (ring[0, tile] + ring[1, tile] + ring[2, tile])


def tiles(dosages):
    half_tile = (PANEL // 2, PANEL)
    block = (CHUNKS, SIDE, SIDE, ROWS, CHUNK)
    dma = pltpu.SemaphoreType.DMA
    return pl.pallas_call(
        tiles_kernel,
        out_shape=jax.ShapeDtypeStruct((OWN, WMAX + 1) + half_tile, jnp.float32),
        in_specs=[pl.BlockSpec(memory_space=pl.ANY)],
        out_specs=pl.BlockSpec(memory_space=pltpu.VMEM),
        scratch_shapes=[
            pltpu.VMEM(block, jnp.bfloat16),
            pltpu.VMEM((CHUNKS, 2, SIDE, SIDE, HALF, CHUNK), jnp.bfloat16),
            pltpu.VMEM((CHUNKS, 2, 2, 2, 2, HALF, CHUNK), jnp.bfloat16),
            pltpu.VMEM(block, jnp.bfloat16),
            pltpu.VMEM((8, CHUNKS, 2 * OWN, PANEL), jnp.float32),
            pltpu.VMEM((CHUNKS, LOCAL, CHUNK), jnp.bfloat16),
            pltpu.VMEM((SIDE, CHUNK, LOCAL), jnp.bfloat16),
            pltpu.VMEM((SIDE, 2, TILES) + half_tile, jnp.float32),
            pltpu.VMEM((SIDE, TILES) + half_tile, jnp.float32),
            pltpu.VMEM((SIDE - 1, TILES) + half_tile, jnp.float32),
            dma((CHUNKS, GROUPS)),
            dma((CHUNKS, 2, 2)),
            dma((CHUNKS, 2, 2, 3, 2)),
            dma((CHUNKS, 2, 2, 3, 2)),
            dma((CHUNKS, 7)),
            dma((CHUNKS, 7)),
            dma((SIDE, REACH + 1)),
            dma((SIDE, REACH + 1)),
            dma((SIDE, REACH + 1)),
            dma((SIDE - 1, REACH + 1)),
        ],
        compiler_params=pltpu.CompilerParams(
            collective_id=0, has_side_effects=True, vmem_limit_bytes=60 * 1024 * 1024
        ),
        name="tiles",
    )(dosages)


def per_device(dosages, band_width):
    band_tiles = tiles(dosages)
    offsets = jnp.arange(WMAX + 1, dtype=jnp.int32)
    panel_count = OWN * lax.axis_size("var")
    global_panel = lax.axis_index("var") * OWN + jnp.arange(OWN, dtype=jnp.int32)
    in_band = (offsets[None, :] <= band_width[:, None]) & (
        global_panel[:, None] + offsets[None, :] < panel_count
    )
    return jnp.where(in_band[:, :, None, None], band_tiles * (1.0 / SAMPLES), 0.0)


def solution(mesh):
    in_specs = (P(("var", "samp"), None), P("var"))
    out_specs = P("var", None, "samp", None)
    return jax.shard_map(
        per_device, mesh=mesh, in_specs=in_specs, out_specs=out_specs, check_vma=False
    )
```

```python
import jax
import jax.numpy as jnp
from jax import lax
from jax.experimental import pallas as pl
from jax.experimental.pallas import tpu as pltpu
from jax.sharding import PartitionSpec as P

MESH = pl.DeviceIdType.MESH
WMAX = 8
PANEL = 128
SIDE = 4
GROUPS = SIDE * SIDE
OWN = 4
CHUNK = OWN * PANEL
REACH = WMAX // OWN
CHUNKS = SIDE + REACH
ROWS = 64
HALF = ROWS // 2
LOCAL = GROUPS * ROWS
SAMPLES = 8192
BLOCK = 2 * PANEL
PLACES = [
    [(p, q) for p in range(OWN) for q in range(OWN) if 0 <= d * OWN + q - p <= WMAX] for d in range(REACH + 1)
]
STARTS = [sum(len(places) for places in PLACES[:d]) for d in range(REACH + 2)]
TILES = STARTS[-1]


def position():
    var = lax.axis_index("var")
    return var // SIDE, lax.rem(var, SIDE), lax.axis_index("samp")


def tiles_kernel(
    dos_ref, out_ref, staged, middle, passing, received, moments, gathered, sums, totals, standard, turned, part, twin, ring,
    stage_sem, own_sem, swap_send, swap_recv, group_send, group_recv, stat_send, stat_recv, twin_send, twin_recv, ring_send, ring_recv,
):
    group, x, core = position()
    z, y = group // SIDE, lax.rem(group, SIDE)

    def stage(chunk):
        def begin_block(other, carry):
            first = pl.multiple_of(lax.rem(other * SIDE + chunk, GROUPS * SIDE) * CHUNK, CHUNK)
            pltpu.make_async_copy(
                dos_ref.at[:, pl.ds(first, CHUNK)],
                staged.at[chunk, other // SIDE, lax.rem(other, SIDE)],
                stage_sem.at[chunk, other],
            ).start()
            return carry

        lax.fori_loop(0, GROUPS, begin_block, 0)

    def stage_wait(chunk):
        def wait_block(other, carry):
            first = pl.multiple_of(lax.rem(other * SIDE + chunk, GROUPS * SIDE) * CHUNK, CHUNK)
            pltpu.make_async_copy(
                dos_ref.at[:, pl.ds(first, CHUNK)],
                staged.at[chunk, other // SIDE, lax.rem(other, SIDE)],
                stage_sem.at[chunk, other],
            ).wait()
            return carry

        lax.fori_loop(0, GROUPS, wait_block, 0)

    for chunk in range(CHUNKS):
        stage(chunk)

    peers = []
    for dx in range(SIDE):
        for dc in range(2):
            if dx or dc:
                peer_x, peer_c = lax.rem(x + dx, SIDE), lax.rem(core + dc, 2)
                peers.append((group * SIDE + peer_x, peer_c))

    def along_y(step):
        return (z * SIDE + lax.rem(y + step, SIDE)) * SIDE + x, core

    def along_z(step):
        return (lax.rem(z + step, SIDE) * SIDE + y) * SIDE + x, core

    def group_at(offset):
        return lax.rem(z + offset // SIDE, SIDE) * SIDE + lax.rem(y + offset % SIDE, SIDE)

    barrier = pltpu.get_barrier_semaphore()
    for offset in range(1, GROUPS):
        pl.semaphore_signal(
            barrier, inc=1, device_id=(group_at(offset) * SIDE + x, core), device_id_type=MESH
        )
    for peer in peers:
        pl.semaphore_signal(barrier, inc=1, device_id=peer, device_id_type=MESH)
    stage_wait(0)
    pl.semaphore_wait(barrier, GROUPS - 1 + len(peers))

    places = ((y, z), (z, y))
    routes = ((along_y, along_z), (along_z, along_y))
    every = pl.ds(0, SIDE)
    both = [(half, way) for way in range(2) for half in range(2)]

    def pick(ref, chunk, half, place, others):
        rows = pl.ds(half * HALF, HALF)
        return ref.at[chunk, others, place, rows] if half == 0 else ref.at[chunk, place, others, rows]

    def landed(chunk, half, distance, others):
        rows = pl.ds(half * HALF, HALF)
        return (
            received.at[chunk, distance, others, rows] if half == 0 else received.at[chunk, others, distance, rows]
        )

    def begin(chunk, half, phase, kind, way, source, target):
        copy = pltpu.make_async_remote_copy(
            src_ref=source,
            dst_ref=target,
            send_sem=swap_send.at[chunk, half, phase, kind, way],
            recv_sem=swap_recv.at[chunk, half, phase, kind, way],
            device_id=routes[half][phase](1 + 2 * way),
            device_id_type=MESH,
        )
        copy.start()
        return copy

    def keep(chunk, half, phase, source, target):
        copy = pltpu.make_async_copy(source, target, own_sem.at[chunk, half, phase])
        copy.start()
        return copy

    def place_at(half, phase, step):
        return lax.rem(places[half][phase] + step, SIDE)

    far, near, passed, kept = {}, {}, {}, {}

    def first_begin(chunk):
        for half, way in both:
            far[chunk, 0, half, way] = begin(
                chunk, half, 0, 0, way,
                pick(staged, chunk, half, place_at(half, 0, 2), pl.ds(2 * way, 2)),
                passing.at[chunk, half, 0, way],
            )
        for half, way in both:
            near[chunk, 0, half, way] = begin(
                chunk, half, 0, 1, way,
                pick(staged, chunk, half, place_at(half, 0, 1 + 2 * way), every),
                middle.at[chunk, half, 1 + 2 * way],
            )
        for half in range(2):
            kept[chunk, 0, half] = keep(
                chunk, half, 0, pick(staged, chunk, half, places[half][0], every), middle.at[chunk, half, 0]
            )

    def first_pass(chunk):
        for half, way in both:
            far[chunk, 0, half, way].wait()
            passed[chunk, 0, half, way] = begin(
                chunk, half, 0, 2, way,
                passing.at[chunk, half, 0, way],
                middle.at[chunk, half, 2, pl.ds(2 * way, 2)],
            )

    def second_begin(chunk):
        for half in range(2):
            kept[chunk, 0, half].wait()
        for half, way in both:
            near[chunk, 0, half, way].wait()
        for half, way in both:
            passed[chunk, 0, half, way].wait()
        for half, way in both:
            far[chunk, 1, half, way] = begin(
                chunk, half, 1, 0, way,
                middle.at[chunk, half, pl.ds(2 * way, 2), place_at(half, 1, 2)],
                passing.at[chunk, half, 1, way],
            )
        for half, way in both:
            near[chunk, 1, half, way] = begin(
                chunk, half, 1, 1, way,
                middle.at[chunk, half, every, place_at(half, 1, 1 + 2 * way)],
                landed(chunk, half, 1 + 2 * way, every),
            )
        for half in range(2):
            kept[chunk, 1, half] = keep(
                chunk, half, 1, middle.at[chunk, half, every, places[half][1]], landed(chunk, half, 0, every)
            )

    def second_pass(chunk):
        for half, way in both:
            far[chunk, 1, half, way].wait()
            passed[chunk, 1, half, way] = begin(
                chunk, half, 1, 2, way,
                passing.at[chunk, half, 1, way],
                landed(chunk, half, 2, pl.ds(2 * way, 2)),
            )

    def second_wait(chunk):
        for half in range(2):
            kept[chunk, 1, half].wait()
        for half, way in both:
            near[chunk, 1, half, way].wait()
        for half, way in both:
            passed[chunk, 1, half, way].wait()

    def block_of(chunk, step):
        return received[chunk, step // SIDE, lax.rem(step, SIDE)].astype(jnp.float32)

    def local_moments():
        def chunk_moments(index, carry):
            other = index // SIDE
            values = staged[lax.rem(index, SIDE), other // SIDE, lax.rem(other, SIDE)]
            values = values.astype(jnp.float32).reshape(ROWS // 8, 8, CHUNK)
            for row, total in enumerate((jnp.sum(values, 0), jnp.sum(values * values, 0))):
                total = jnp.sum(total, 0, keepdims=True)
                for q in range(OWN):
                    moments[index, row * OWN + q:row * OWN + q + 1, :] = total[:, q * PANEL:(q + 1) * PANEL]
            return carry

        lax.fori_loop(0, GROUPS * SIDE, chunk_moments, 0)
        for extra in range(REACH):
            moments[GROUPS * SIDE + extra] = moments[extra]

    def group_moments_begin():
        gathered[0] = moments[pl.ds(group * SIDE, CHUNKS)]
        copies = []
        for offset in range(1, GROUPS):
            other = group_at(offset)
            copy = pltpu.make_async_remote_copy(
                src_ref=moments.at[pl.ds(other * SIDE, CHUNKS)],
                dst_ref=gathered.at[offset],
                send_sem=group_send.at[offset],
                recv_sem=group_recv.at[offset],
                device_id=(other * SIDE + x, core),
                device_id_type=MESH,
            )
            copy.start()
            copies.append(copy)
        return copies

    def ring_moments_begin(copies):
        for copy in copies:
            copy.wait()
        sums[0] = jnp.sum(gathered[...], 0)
        copies = []
        for index, peer in enumerate(peers):
            copy = pltpu.make_async_remote_copy(
                src_ref=sums.at[0],
                dst_ref=sums.at[index + 1],
                send_sem=stat_send.at[index],
                recv_sem=stat_recv.at[index],
                device_id=peer,
                device_id_type=MESH,
            )
            copy.start()
            copies.append(copy)
        return copies

    def ring_moments_end(copies):
        for copy in copies:
            copy.wait()
        totals[...] = jnp.sum(sums[...], 0)

    def standardize(chunk):
        first, second = totals[chunk, 0:OWN], totals[chunk, OWN:2 * OWN]
        mean = first * (1.0 / SAMPLES)
        inv_scale = lax.rsqrt(second * (1.0 / SAMPLES) - mean * mean + 1e-05)
        mean = jnp.concatenate([mean[q:q + 1] for q in range(OWN)], axis=1)
        inv_scale = jnp.concatenate([inv_scale[q:q + 1] for q in range(OWN)], axis=1)

        def block_standard(step, carry):
            rows = pl.ds(pl.multiple_of(step * ROWS, ROWS), ROWS)
            standard[chunk, rows, :] = ((block_of(chunk, step) - mean) * inv_scale).astype(jnp.bfloat16)
            return carry

        lax.fori_loop(0, GROUPS, block_standard, 0)
        if chunk < SIDE:
            turned[chunk] = standard[chunk].T

    def pieces_of(chunk):
        return [(chunk - d, d) for d in range(REACH + 1) if 0 <= chunk - d < SIDE]

    twins = {}

    def multiply(chunk):
        for rows_chunk, d in pieces_of(chunk):
            for pp in range(OWN // 2):
                for qq in range(OWN // 2):
                    inside = [
                        (p, q) for p in range(2) for q in range(2) if (2 * pp + p, 2 * qq + q) in PLACES[d]
                    ]
                    if not inside:
                        continue
                    block = jnp.dot(
                        turned[rows_chunk, pp * BLOCK:(pp + 1) * BLOCK, :],
                        standard[chunk, :, qq * BLOCK:(qq + 1) * BLOCK],
                        preferred_element_type=jnp.float32,
                    )
                    for p, q in inside:
                        tile = STARTS[d] + PLACES[d].index((2 * pp + p, 2 * qq + q))
                        for half in range(2):
                            first = p * PANEL + half * (PANEL // 2)
                            part[rows_chunk, half, tile] = block[
                                first:first + PANEL // 2, q * PANEL:(q + 1) * PANEL
                            ]
            which = pl.ds(STARTS[d], len(PLACES[d]))
            copy = pltpu.make_async_remote_copy(
                src_ref=part.at[rows_chunk, 1 - core, which],
                dst_ref=twin.at[rows_chunk, which],
                send_sem=twin_send.at[rows_chunk, d],
                recv_sem=twin_recv.at[rows_chunk, d],
                device_id=(group * SIDE + x, 1 - core),
                device_id_type=MESH,
            )
            copy.start()
            twins[rows_chunk, d] = copy

    def ring_copy(rows_chunk, d, slot):
        which = pl.ds(STARTS[d], len(PLACES[d]))
        return pltpu.make_async_remote_copy(
            src_ref=part.at[rows_chunk, core, which],
            dst_ref=ring.at[slot, which],
            send_sem=ring_send.at[rows_chunk, d],
            recv_sem=ring_recv.at[slot, d],
            device_id=(group * SIDE + rows_chunk, core),
            device_id_type=MESH,
        )

    def reduce(chunk):
        for rows_chunk, d in pieces_of(chunk):
            which = pl.ds(STARTS[d], len(PLACES[d]))
            twins[rows_chunk, d].wait()
            part[rows_chunk, core, which] = part[rows_chunk, core, which] + twin[rows_chunk, which]

            @pl.when(x != rows_chunk)
            def _():
                ring_copy(rows_chunk, d, lax.rem(rows_chunk - x + 2 * SIDE - 1, SIDE)).start()

    first_begin(0)
    for chunk in range(1, CHUNKS):
        stage_wait(chunk)
    first_begin(1)
    local_moments()
    copies = group_moments_begin()
    first_pass(0)
    first_begin(2)
    second_begin(0)
    copies = ring_moments_begin(copies)
    first_pass(1)
    second_pass(0)
    second_begin(1)
    ring_moments_end(copies)
    for chunk in range(CHUNKS):
        second_wait(chunk)
        if chunk + 2 < CHUNKS:
            first_pass(chunk + 2)
        if chunk + 1 < CHUNKS:
            second_pass(chunk + 1)
        standardize(chunk)
        multiply(chunk)
        if chunk + 3 < CHUNKS:
            first_begin(chunk + 3)
        if chunk + 2 < CHUNKS:
            second_begin(chunk + 2)
        if chunk >= 1:
            reduce(chunk - 1)
    reduce(CHUNKS - 1)

    for rows_chunk in range(SIDE):
        for d in range(REACH + 1):

            @pl.when(x != rows_chunk)
            def _():
                ring_copy(rows_chunk, d, lax.rem(rows_chunk - x + 2 * SIDE - 1, SIDE)).wait_send()

            @pl.when(x == rows_chunk)
            def _():
                for slot in range(SIDE - 1):
                    ring_copy(rows_chunk, d, slot).wait_recv()

    for d in range(REACH + 1):
        for index, (p, q) in enumerate(PLACES[d]):
            tile = STARTS[d] + index
            out_ref[p, d * OWN + q - p] = part[x, core, tile] + (ring[0, tile] + ring[1, tile] + ring[2, tile])


def tiles(dosages):
    half_tile = (PANEL // 2, PANEL)
    block = (CHUNKS, SIDE, SIDE, ROWS, CHUNK)
    dma = pltpu.SemaphoreType.DMA
    return pl.pallas_call(
        tiles_kernel,
        out_shape=jax.ShapeDtypeStruct((OWN, WMAX + 1) + half_tile, jnp.float32),
        in_specs=[pl.BlockSpec(memory_space=pl.ANY)],
        out_specs=pl.BlockSpec(memory_space=pltpu.VMEM),
        scratch_shapes=[
            pltpu.VMEM(block, jnp.bfloat16),
            pltpu.VMEM((CHUNKS, 2, SIDE, SIDE, HALF, CHUNK), jnp.bfloat16),
            pltpu.VMEM((CHUNKS, 2, 2, 2, 2, HALF, CHUNK), jnp.bfloat16),
            pltpu.VMEM(block, jnp.bfloat16),
            pltpu.VMEM((GROUPS * SIDE + REACH, 2 * OWN, PANEL), jnp.float32),
            pltpu.VMEM((GROUPS, CHUNKS, 2 * OWN, PANEL), jnp.float32),
            pltpu.VMEM((8, CHUNKS, 2 * OWN, PANEL), jnp.float32),
            pltpu.VMEM((CHUNKS, 2 * OWN, PANEL), jnp.float32),
            pltpu.VMEM((CHUNKS, LOCAL, CHUNK), jnp.bfloat16),
            pltpu.VMEM((SIDE, CHUNK, LOCAL), jnp.bfloat16),
            pltpu.VMEM((SIDE, 2, TILES) + half_tile, jnp.float32),
            pltpu.VMEM((SIDE, TILES) + half_tile, jnp.float32),
            pltpu.VMEM((SIDE - 1, TILES) + half_tile, jnp.float32),
            dma((CHUNKS, GROUPS)),
            dma((CHUNKS, 2, 2)),
            dma((CHUNKS, 2, 2, 3, 2)),
            dma((CHUNKS, 2, 2, 3, 2)),
            dma((GROUPS,)),
            dma((GROUPS,)),
            dma((7,)),
            dma((7,)),
            dma((SIDE, REACH + 1)),
            dma((SIDE, REACH + 1)),
            dma((SIDE, REACH + 1)),
            dma((SIDE - 1, REACH + 1)),
        ],
        compiler_params=pltpu.CompilerParams(
            collective_id=0, has_side_effects=True, vmem_limit_bytes=60 * 1024 * 1024
        ),
        name="tiles",
    )(dosages)


def per_device(dosages, band_width):
    band_tiles = tiles(dosages)
    offsets = jnp.arange(WMAX + 1, dtype=jnp.int32)
    panel_count = OWN * lax.axis_size("var")
    global_panel = lax.axis_index("var") * OWN + jnp.arange(OWN, dtype=jnp.int32)
    in_band = (offsets[None, :] <= band_width[:, None]) & (
        global_panel[:, None] + offsets[None, :] < panel_count
    )
    return jnp.where(in_band[:, :, None, None], band_tiles * (1.0 / SAMPLES), 0.0)


def solution(mesh):
    in_specs = (P(("var", "samp"), None), P("var"))
    out_specs = P("var", None, "samp", None)
    return jax.shard_map(
        per_device, mesh=mesh, in_specs=in_specs, out_specs=out_specs, check_vma=False
    )
```

```python
import jax
import jax.numpy as jnp
from jax import lax
from jax.experimental import pallas as pl
from jax.experimental.pallas import tpu as pltpu
from jax.sharding import PartitionSpec as P

MESH = pl.DeviceIdType.MESH
WMAX = 8
PANEL = 128
SIDE = 4
GROUPS = SIDE * SIDE
OWN = 4
CHUNK = OWN * PANEL
REACH = WMAX // OWN
CHUNKS = SIDE + REACH
ROWS = 64
ORDER = [10, 15, 1, 4, 6, 3, 9, 12, 11, 14, 7, 13, 2, 8, 5]
LOCAL = GROUPS * ROWS
SAMPLES = 8192
BLOCK = 2 * PANEL
PLACES = [
    [(p, q) for p in range(OWN) for q in range(OWN) if 0 <= d * OWN + q - p <= WMAX] for d in range(REACH + 1)
]
STARTS = [sum(len(places) for places in PLACES[:d]) for d in range(REACH + 2)]
TILES = STARTS[-1]


def position():
    var = lax.axis_index("var")
    return var // SIDE, lax.rem(var, SIDE), lax.axis_index("samp")


def tiles_kernel(
    dos_ref, out_ref, staged, received, moments, gathered, sums, totals, standard, turned, part, twin, ring,
    stage_sem, own_sem, swap_send, swap_recv, group_send, group_recv, stat_send, stat_recv, twin_send, twin_recv, ring_send, ring_recv,
):
    group, x, core = position()
    z, y = group // SIDE, lax.rem(group, SIDE)

    def stage(index):
        first = pl.multiple_of(index * CHUNK, CHUNK)
        return pltpu.make_async_copy(dos_ref.at[:, pl.ds(first, CHUNK)], staged.at[index], stage_sem.at[index])

    def stage_begin(index, carry):
        stage(index).start()
        return carry

    def stage_end(index, carry):
        stage(index).wait()
        return carry

    lax.fori_loop(0, GROUPS * SIDE, stage_begin, 0)

    peers = []
    for dx in range(SIDE):
        for dc in range(2):
            if dx or dc:
                peer_x, peer_c = lax.rem(x + dx, SIDE), lax.rem(core + dc, 2)
                peers.append((group * SIDE + peer_x, peer_c))

    def group_at(offset):
        return lax.rem(z + offset // SIDE, SIDE) * SIDE + lax.rem(y + offset % SIDE, SIDE)

    barrier = pltpu.get_barrier_semaphore()
    for offset in range(1, GROUPS):
        pl.semaphore_signal(
            barrier, inc=1, device_id=(group_at(offset) * SIDE + x, core), device_id_type=MESH
        )
    for peer in peers:
        pl.semaphore_signal(barrier, inc=1, device_id=peer, device_id_type=MESH)
    lax.fori_loop(0, GROUPS * SIDE, stage_end, 0)
    pl.semaphore_wait(barrier, GROUPS - 1 + len(peers))

    swaps = {}

    def swap_begin(chunk):
        swaps[chunk] = []
        for offset in ORDER:
            other = group_at(offset)
            copy = pltpu.make_async_remote_copy(
                src_ref=staged.at[lax.rem(other * SIDE + chunk, GROUPS * SIDE)],
                dst_ref=received.at[chunk, offset],
                send_sem=swap_send.at[chunk, offset],
                recv_sem=swap_recv.at[chunk, offset],
                device_id=(other * SIDE + x, core),
                device_id_type=MESH,
            )
            copy.start()
            swaps[chunk].append(copy)
        copy = pltpu.make_async_copy(
            staged.at[lax.rem(group * SIDE + chunk, GROUPS * SIDE)], received.at[chunk, 0], own_sem.at[chunk]
        )
        copy.start()
        swaps[chunk].append(copy)

    def swap_end(chunk):
        for copy in swaps[chunk]:
            copy.wait()

    def block_of(chunk, step):
        return received[chunk, step].astype(jnp.float32)

    def local_moments():
        def chunk_moments(index, carry):
            values = staged[index].astype(jnp.float32).reshape(ROWS // 8, 8, CHUNK)
            for row, total in enumerate((jnp.sum(values, 0), jnp.sum(values * values, 0))):
                total = jnp.sum(total, 0, keepdims=True)
                for q in range(OWN):
                    moments[index, row * OWN + q:row * OWN + q + 1, :] = total[:, q * PANEL:(q + 1) * PANEL]
            return carry

        lax.fori_loop(0, GROUPS * SIDE, chunk_moments, 0)
        for extra in range(REACH):
            moments[GROUPS * SIDE + extra] = moments[extra]

    def group_moments_begin():
        gathered[0] = moments[pl.ds(group * SIDE, CHUNKS)]
        copies = []
        for offset in range(1, GROUPS):
            other = group_at(offset)
            copy = pltpu.make_async_remote_copy(
                src_ref=moments.at[pl.ds(other * SIDE, CHUNKS)],
                dst_ref=gathered.at[offset],
                send_sem=group_send.at[offset],
                recv_sem=group_recv.at[offset],
                device_id=(other * SIDE + x, core),
                device_id_type=MESH,
            )
            copy.start()
            copies.append(copy)
        return copies

    def ring_moments_begin(copies):
        for copy in copies:
            copy.wait()
        sums[0] = jnp.sum(gathered[...], 0)
        copies = []
        for index, peer in enumerate(peers):
            copy = pltpu.make_async_remote_copy(
                src_ref=sums.at[0],
                dst_ref=sums.at[index + 1],
                send_sem=stat_send.at[index],
                recv_sem=stat_recv.at[index],
                device_id=peer,
                device_id_type=MESH,
            )
            copy.start()
            copies.append(copy)
        return copies

    def ring_moments_end(copies):
        for copy in copies:
            copy.wait()
        totals[...] = jnp.sum(sums[...], 0)

    def standardize(chunk):
        first, second = totals[chunk, 0:OWN], totals[chunk, OWN:2 * OWN]
        mean = first * (1.0 / SAMPLES)
        inv_scale = lax.rsqrt(second * (1.0 / SAMPLES) - mean * mean + 1e-05)
        mean = jnp.concatenate([mean[q:q + 1] for q in range(OWN)], axis=1)
        inv_scale = jnp.concatenate([inv_scale[q:q + 1] for q in range(OWN)], axis=1)

        def block_standard(step, carry):
            rows = pl.ds(pl.multiple_of(step * ROWS, ROWS), ROWS)
            standard[chunk, rows, :] = ((block_of(chunk, step) - mean) * inv_scale).astype(jnp.bfloat16)
            return carry

        lax.fori_loop(0, GROUPS, block_standard, 0)
        if chunk < SIDE:
            turned[chunk] = standard[chunk].T

    def pieces_of(chunk):
        return [(chunk - d, d) for d in range(REACH + 1) if 0 <= chunk - d < SIDE]

    twins = {}

    def multiply(chunk):
        for rows_chunk, d in pieces_of(chunk):
            for pp in range(OWN // 2):
                for qq in range(OWN // 2):
                    inside = [
                        (p, q) for p in range(2) for q in range(2) if (2 * pp + p, 2 * qq + q) in PLACES[d]
                    ]
                    if not inside:
                        continue
                    block = jnp.dot(
                        turned[rows_chunk, pp * BLOCK:(pp + 1) * BLOCK, :],
                        standard[chunk, :, qq * BLOCK:(qq + 1) * BLOCK],
                        preferred_element_type=jnp.float32,
                    )
                    for p, q in inside:
                        tile = STARTS[d] + PLACES[d].index((2 * pp + p, 2 * qq + q))
                        for half in range(2):
                            first = p * PANEL + half * (PANEL // 2)
                            part[rows_chunk, half, tile] = block[
                                first:first + PANEL // 2, q * PANEL:(q + 1) * PANEL
                            ]
            which = pl.ds(STARTS[d], len(PLACES[d]))
            copy = pltpu.make_async_remote_copy(
                src_ref=part.at[rows_chunk, 1 - core, which],
                dst_ref=twin.at[rows_chunk, which],
                send_sem=twin_send.at[rows_chunk, d],
                recv_sem=twin_recv.at[rows_chunk, d],
                device_id=(group * SIDE + x, 1 - core),
                device_id_type=MESH,
            )
            copy.start()
            twins[rows_chunk, d] = copy

    def ring_copy(rows_chunk, d, slot):
        which = pl.ds(STARTS[d], len(PLACES[d]))
        return pltpu.make_async_remote_copy(
            src_ref=part.at[rows_chunk, core, which],
            dst_ref=ring.at[slot, which],
            send_sem=ring_send.at[rows_chunk, d],
            recv_sem=ring_recv.at[slot, d],
            device_id=(group * SIDE + rows_chunk, core),
            device_id_type=MESH,
        )

    def reduce(chunk):
        for rows_chunk, d in pieces_of(chunk):
            which = pl.ds(STARTS[d], len(PLACES[d]))
            twins[rows_chunk, d].wait()
            part[rows_chunk, core, which] = part[rows_chunk, core, which] + twin[rows_chunk, which]

            @pl.when(x != rows_chunk)
            def _():
                ring_copy(rows_chunk, d, lax.rem(rows_chunk - x + 2 * SIDE - 1, SIDE)).start()

    swap_begin(0)
    swap_begin(1)
    local_moments()
    copies = group_moments_begin()
    swap_begin(2)
    copies = ring_moments_begin(copies)
    ring_moments_end(copies)
    for chunk in range(CHUNKS):
        swap_end(chunk)
        if chunk + 3 < CHUNKS:
            swap_begin(chunk + 3)
        standardize(chunk)
        multiply(chunk)
        if chunk >= 1:
            reduce(chunk - 1)
    reduce(CHUNKS - 1)

    for rows_chunk in range(SIDE):
        for d in range(REACH + 1):

            @pl.when(x != rows_chunk)
            def _():
                ring_copy(rows_chunk, d, lax.rem(rows_chunk - x + 2 * SIDE - 1, SIDE)).wait_send()

            @pl.when(x == rows_chunk)
            def _():
                for slot in range(SIDE - 1):
                    ring_copy(rows_chunk, d, slot).wait_recv()

    for d in range(REACH + 1):
        for index, (p, q) in enumerate(PLACES[d]):
            tile = STARTS[d] + index
            out_ref[p, d * OWN + q - p] = part[x, core, tile] + (ring[0, tile] + ring[1, tile] + ring[2, tile])


def tiles(dosages):
    half_tile = (PANEL // 2, PANEL)
    dma = pltpu.SemaphoreType.DMA
    return pl.pallas_call(
        tiles_kernel,
        out_shape=jax.ShapeDtypeStruct((OWN, WMAX + 1) + half_tile, jnp.float32),
        in_specs=[pl.BlockSpec(memory_space=pl.ANY)],
        out_specs=pl.BlockSpec(memory_space=pltpu.VMEM),
        scratch_shapes=[
            pltpu.VMEM((GROUPS * SIDE, ROWS, CHUNK), jnp.bfloat16),
            pltpu.VMEM((CHUNKS, GROUPS, ROWS, CHUNK), jnp.bfloat16),
            pltpu.VMEM((GROUPS * SIDE + REACH, 2 * OWN, PANEL), jnp.float32),
            pltpu.VMEM((GROUPS, CHUNKS, 2 * OWN, PANEL), jnp.float32),
            pltpu.VMEM((8, CHUNKS, 2 * OWN, PANEL), jnp.float32),
            pltpu.VMEM((CHUNKS, 2 * OWN, PANEL), jnp.float32),
            pltpu.VMEM((CHUNKS, LOCAL, CHUNK), jnp.bfloat16),
            pltpu.VMEM((SIDE, CHUNK, LOCAL), jnp.bfloat16),
            pltpu.VMEM((SIDE, 2, TILES) + half_tile, jnp.float32),
            pltpu.VMEM((SIDE, TILES) + half_tile, jnp.float32),
            pltpu.VMEM((SIDE - 1, TILES) + half_tile, jnp.float32),
            dma((GROUPS * SIDE,)),
            dma((CHUNKS,)),
            dma((CHUNKS, GROUPS)),
            dma((CHUNKS, GROUPS)),
            dma((GROUPS,)),
            dma((GROUPS,)),
            dma((7,)),
            dma((7,)),
            dma((SIDE, REACH + 1)),
            dma((SIDE, REACH + 1)),
            dma((SIDE, REACH + 1)),
            dma((SIDE - 1, REACH + 1)),
        ],
        compiler_params=pltpu.CompilerParams(
            collective_id=0, has_side_effects=True, vmem_limit_bytes=60 * 1024 * 1024
        ),
        name="tiles",
    )(dosages)


def per_device(dosages, band_width):
    band_tiles = tiles(dosages)
    offsets = jnp.arange(WMAX + 1, dtype=jnp.int32)
    panel_count = OWN * lax.axis_size("var")
    global_panel = lax.axis_index("var") * OWN + jnp.arange(OWN, dtype=jnp.int32)
    in_band = (offsets[None, :] <= band_width[:, None]) & (
        global_panel[:, None] + offsets[None, :] < panel_count
    )
    return jnp.where(in_band[:, :, None, None], band_tiles * (1.0 / SAMPLES), 0.0)


def solution(mesh):
    in_specs = (P(("var", "samp"), None), P("var"))
    out_specs = P("var", None, "samp", None)
    return jax.shard_map(
        per_device, mesh=mesh, in_specs=in_specs, out_specs=out_specs, check_vma=False
    )
```

```python
import jax
import jax.numpy as jnp
from jax import lax
from jax.experimental import pallas as pl
from jax.experimental.pallas import tpu as pltpu
from jax.sharding import PartitionSpec as P

MESH = pl.DeviceIdType.MESH
WMAX = 8
PANEL = 128
SIDE = 4
GROUPS = SIDE * SIDE
OWN = 4
CHUNK = OWN * PANEL
REACH = WMAX // OWN
CHUNKS = SIDE + REACH
ROWS = 64
AHEAD = 8
ORDER = [10, 15, 1, 4, 6, 3, 9, 12, 11, 14, 7, 13, 2, 8, 5]
LOCAL = GROUPS * ROWS
SAMPLES = 8192
BLOCK = 2 * PANEL
PLACES = [
    [(p, q) for p in range(OWN) for q in range(OWN) if 0 <= d * OWN + q - p <= WMAX] for d in range(REACH + 1)
]
STARTS = [sum(len(places) for places in PLACES[:d]) for d in range(REACH + 2)]
TILES = STARTS[-1]


def position():
    var = lax.axis_index("var")
    return var // SIDE, lax.rem(var, SIDE), lax.axis_index("samp")


def tiles_kernel(
    dos_ref, out_ref, staged, received, moments, gathered, sums, totals, standard, turned, part, twin, ring,
    stage_sem, own_sem, swap_send, swap_recv, group_send, group_recv, stat_send, stat_recv, twin_send, twin_recv, ring_send, ring_recv,
):
    group, x, core = position()
    z, y = group // SIDE, lax.rem(group, SIDE)

    def stage(index):
        first = pl.multiple_of(index * CHUNK, CHUNK)
        return pltpu.make_async_copy(dos_ref.at[:, pl.ds(first, CHUNK)], staged.at[index], stage_sem.at[index])

    def stage_begin(index, carry):
        stage(index).start()
        return carry

    def stage_end(index, carry):
        stage(index).wait()
        return carry

    lax.fori_loop(0, GROUPS * SIDE, stage_begin, 0)

    peers = []
    for dx in range(SIDE):
        for dc in range(2):
            if dx or dc:
                peer_x, peer_c = lax.rem(x + dx, SIDE), lax.rem(core + dc, 2)
                peers.append((group * SIDE + peer_x, peer_c))

    def group_at(offset):
        return lax.rem(z + offset // SIDE, SIDE) * SIDE + lax.rem(y + offset % SIDE, SIDE)

    barrier = pltpu.get_barrier_semaphore()
    for offset in range(1, GROUPS):
        pl.semaphore_signal(
            barrier, inc=1, device_id=(group_at(offset) * SIDE + x, core), device_id_type=MESH
        )
    for peer in peers:
        pl.semaphore_signal(barrier, inc=1, device_id=peer, device_id_type=MESH)
    lax.fori_loop(0, GROUPS * SIDE, stage_end, 0)
    pl.semaphore_wait(barrier, GROUPS - 1 + len(peers))

    def swap(step):
        chunk, index = divmod(step, GROUPS - 1)
        offset = ORDER[index]
        other = group_at(offset)
        return pltpu.make_async_remote_copy(
            src_ref=staged.at[lax.rem(other * SIDE + chunk, GROUPS * SIDE)],
            dst_ref=received.at[chunk, offset],
            send_sem=swap_send.at[chunk, offset],
            recv_sem=swap_recv.at[chunk, offset],
            device_id=(other * SIDE + x, core),
            device_id_type=MESH,
        )

    swaps = [swap(step) for step in range(CHUNKS * (GROUPS - 1))]
    started = [0]

    def pump(count):
        for step in range(started[0], min(started[0] + count, len(swaps))):
            if step >= AHEAD:
                swaps[step - AHEAD].wait_send()
            swaps[step].start()
            started[0] = step + 1

    def own_copy(chunk):
        return pltpu.make_async_copy(
            staged.at[lax.rem(group * SIDE + chunk, GROUPS * SIDE)], received.at[chunk, 0], own_sem.at[chunk]
        )

    def swap_end(chunk):
        own_copy(chunk).wait()
        for copy in swaps[chunk * (GROUPS - 1):(chunk + 1) * (GROUPS - 1)]:
            copy.wait_recv()

    def block_of(chunk, step):
        return received[chunk, step].astype(jnp.float32)

    def local_moments():
        def chunk_moments(index, carry):
            values = staged[index].astype(jnp.float32).reshape(ROWS // 8, 8, CHUNK)
            for row, total in enumerate((jnp.sum(values, 0), jnp.sum(values * values, 0))):
                total = jnp.sum(total, 0, keepdims=True)
                for q in range(OWN):
                    moments[index, row * OWN + q:row * OWN + q + 1, :] = total[:, q * PANEL:(q + 1) * PANEL]
            return carry

        lax.fori_loop(0, GROUPS * SIDE, chunk_moments, 0)
        for extra in range(REACH):
            moments[GROUPS * SIDE + extra] = moments[extra]

    def group_moments_begin():
        gathered[0] = moments[pl.ds(group * SIDE, CHUNKS)]
        copies = []
        for offset in range(1, GROUPS):
            other = group_at(offset)
            copy = pltpu.make_async_remote_copy(
                src_ref=moments.at[pl.ds(other * SIDE, CHUNKS)],
                dst_ref=gathered.at[offset],
                send_sem=group_send.at[offset],
                recv_sem=group_recv.at[offset],
                device_id=(other * SIDE + x, core),
                device_id_type=MESH,
            )
            copy.start()
            copies.append(copy)
        return copies

    def ring_moments_begin(copies):
        for copy in copies:
            copy.wait()
        sums[0] = jnp.sum(gathered[...], 0)
        copies = []
        for index, peer in enumerate(peers):
            copy = pltpu.make_async_remote_copy(
                src_ref=sums.at[0],
                dst_ref=sums.at[index + 1],
                send_sem=stat_send.at[index],
                recv_sem=stat_recv.at[index],
                device_id=peer,
                device_id_type=MESH,
            )
            copy.start()
            copies.append(copy)
        return copies

    def ring_moments_end(copies):
        for copy in copies:
            copy.wait()
        totals[...] = jnp.sum(sums[...], 0)

    def standardize(chunk):
        first, second = totals[chunk, 0:OWN], totals[chunk, OWN:2 * OWN]
        mean = first * (1.0 / SAMPLES)
        inv_scale = lax.rsqrt(second * (1.0 / SAMPLES) - mean * mean + 1e-05)
        mean = jnp.concatenate([mean[q:q + 1] for q in range(OWN)], axis=1)
        inv_scale = jnp.concatenate([inv_scale[q:q + 1] for q in range(OWN)], axis=1)

        def block_standard(step, carry):
            rows = pl.ds(pl.multiple_of(step * ROWS, ROWS), ROWS)
            standard[chunk, rows, :] = ((block_of(chunk, step) - mean) * inv_scale).astype(jnp.bfloat16)
            return carry

        lax.fori_loop(0, GROUPS, block_standard, 0)
        if chunk < SIDE:
            turned[chunk] = standard[chunk].T

    def pieces_of(chunk):
        return [(chunk - d, d) for d in range(REACH + 1) if 0 <= chunk - d < SIDE]

    twins = {}

    def multiply(chunk):
        for rows_chunk, d in pieces_of(chunk):
            pump(3)
            for pp in range(OWN // 2):
                for qq in range(OWN // 2):
                    inside = [
                        (p, q) for p in range(2) for q in range(2) if (2 * pp + p, 2 * qq + q) in PLACES[d]
                    ]
                    if not inside:
                        continue
                    block = jnp.dot(
                        turned[rows_chunk, pp * BLOCK:(pp + 1) * BLOCK, :],
                        standard[chunk, :, qq * BLOCK:(qq + 1) * BLOCK],
                        preferred_element_type=jnp.float32,
                    )
                    for p, q in inside:
                        tile = STARTS[d] + PLACES[d].index((2 * pp + p, 2 * qq + q))
                        for half in range(2):
                            first = p * PANEL + half * (PANEL // 2)
                            part[rows_chunk, half, tile] = block[
                                first:first + PANEL // 2, q * PANEL:(q + 1) * PANEL
                            ]
            which = pl.ds(STARTS[d], len(PLACES[d]))
            copy = pltpu.make_async_remote_copy(
                src_ref=part.at[rows_chunk, 1 - core, which],
                dst_ref=twin.at[rows_chunk, which],
                send_sem=twin_send.at[rows_chunk, d],
                recv_sem=twin_recv.at[rows_chunk, d],
                device_id=(group * SIDE + x, 1 - core),
                device_id_type=MESH,
            )
            copy.start()
            twins[rows_chunk, d] = copy

    def ring_copy(rows_chunk, d, slot):
        which = pl.ds(STARTS[d], len(PLACES[d]))
        return pltpu.make_async_remote_copy(
            src_ref=part.at[rows_chunk, core, which],
            dst_ref=ring.at[slot, which],
            send_sem=ring_send.at[rows_chunk, d],
            recv_sem=ring_recv.at[slot, d],
            device_id=(group * SIDE + rows_chunk, core),
            device_id_type=MESH,
        )

    def reduce(chunk):
        for rows_chunk, d in pieces_of(chunk):
            which = pl.ds(STARTS[d], len(PLACES[d]))
            twins[rows_chunk, d].wait()
            part[rows_chunk, core, which] = part[rows_chunk, core, which] + twin[rows_chunk, which]

            @pl.when(x != rows_chunk)
            def _():
                ring_copy(rows_chunk, d, lax.rem(rows_chunk - x + 2 * SIDE - 1, SIDE)).start()

    pump(AHEAD)
    for chunk in range(CHUNKS):
        own_copy(chunk).start()
    local_moments()
    copies = group_moments_begin()
    pump(7)
    copies = ring_moments_begin(copies)
    pump(4)
    ring_moments_end(copies)
    for chunk in range(CHUNKS):
        pump((chunk + 1) * (GROUPS - 1) + AHEAD - started[0])
        swap_end(chunk)
        standardize(chunk)
        multiply(chunk)
        pump(3)
        if chunk >= 1:
            reduce(chunk - 1)
    reduce(CHUNKS - 1)
    for copy in swaps[-AHEAD:]:
        copy.wait_send()

    for rows_chunk in range(SIDE):
        for d in range(REACH + 1):

            @pl.when(x != rows_chunk)
            def _():
                ring_copy(rows_chunk, d, lax.rem(rows_chunk - x + 2 * SIDE - 1, SIDE)).wait_send()

            @pl.when(x == rows_chunk)
            def _():
                for slot in range(SIDE - 1):
                    ring_copy(rows_chunk, d, slot).wait_recv()

    for d in range(REACH + 1):
        for index, (p, q) in enumerate(PLACES[d]):
            tile = STARTS[d] + index
            out_ref[p, d * OWN + q - p] = part[x, core, tile] + (ring[0, tile] + ring[1, tile] + ring[2, tile])


def tiles(dosages):
    half_tile = (PANEL // 2, PANEL)
    dma = pltpu.SemaphoreType.DMA
    return pl.pallas_call(
        tiles_kernel,
        out_shape=jax.ShapeDtypeStruct((OWN, WMAX + 1) + half_tile, jnp.float32),
        in_specs=[pl.BlockSpec(memory_space=pl.ANY)],
        out_specs=pl.BlockSpec(memory_space=pltpu.VMEM),
        scratch_shapes=[
            pltpu.VMEM((GROUPS * SIDE, ROWS, CHUNK), jnp.bfloat16),
            pltpu.VMEM((CHUNKS, GROUPS, ROWS, CHUNK), jnp.bfloat16),
            pltpu.VMEM((GROUPS * SIDE + REACH, 2 * OWN, PANEL), jnp.float32),
            pltpu.VMEM((GROUPS, CHUNKS, 2 * OWN, PANEL), jnp.float32),
            pltpu.VMEM((8, CHUNKS, 2 * OWN, PANEL), jnp.float32),
            pltpu.VMEM((CHUNKS, 2 * OWN, PANEL), jnp.float32),
            pltpu.VMEM((CHUNKS, LOCAL, CHUNK), jnp.bfloat16),
            pltpu.VMEM((SIDE, CHUNK, LOCAL), jnp.bfloat16),
            pltpu.VMEM((SIDE, 2, TILES) + half_tile, jnp.float32),
            pltpu.VMEM((SIDE, TILES) + half_tile, jnp.float32),
            pltpu.VMEM((SIDE - 1, TILES) + half_tile, jnp.float32),
            dma((GROUPS * SIDE,)),
            dma((CHUNKS,)),
            dma((CHUNKS, GROUPS)),
            dma((CHUNKS, GROUPS)),
            dma((GROUPS,)),
            dma((GROUPS,)),
            dma((7,)),
            dma((7,)),
            dma((SIDE, REACH + 1)),
            dma((SIDE, REACH + 1)),
            dma((SIDE, REACH + 1)),
            dma((SIDE - 1, REACH + 1)),
        ],
        compiler_params=pltpu.CompilerParams(
            collective_id=0, has_side_effects=True, vmem_limit_bytes=60 * 1024 * 1024
        ),
        name="tiles",
    )(dosages)


def per_device(dosages, band_width):
    band_tiles = tiles(dosages)
    offsets = jnp.arange(WMAX + 1, dtype=jnp.int32)
    panel_count = OWN * lax.axis_size("var")
    global_panel = lax.axis_index("var") * OWN + jnp.arange(OWN, dtype=jnp.int32)
    in_band = (offsets[None, :] <= band_width[:, None]) & (
        global_panel[:, None] + offsets[None, :] < panel_count
    )
    return jnp.where(in_band[:, :, None, None], band_tiles * (1.0 / SAMPLES), 0.0)


def solution(mesh):
    in_specs = (P(("var", "samp"), None), P("var"))
    out_specs = P("var", None, "samp", None)
    return jax.shard_map(
        per_device, mesh=mesh, in_specs=in_specs, out_specs=out_specs, check_vma=False
    )
```

```python
import jax
import jax.numpy as jnp
from jax import lax
from jax.experimental import pallas as pl
from jax.experimental.pallas import tpu as pltpu
from jax.sharding import PartitionSpec as P

MESH = pl.DeviceIdType.MESH
WMAX = 8
PANEL = 128
SIDE = 4
GROUPS = SIDE * SIDE
OWN = 4
CHUNK = OWN * PANEL
REACH = WMAX // OWN
CHUNKS = SIDE + REACH
COLS = CHUNKS * CHUNK
GROUP_COLS = SIDE * CHUNK
HALO_COLS = REACH * CHUNK
ROWS = 64
HALF = ROWS // 2
LOCAL = GROUPS * ROWS
SAMPLES = 8192
BLOCK = 2 * PANEL
PLACES = [
    [(p, q) for p in range(OWN) for q in range(OWN) if 0 <= d * OWN + q - p <= WMAX] for d in range(REACH + 1)
]
STARTS = [sum(len(places) for places in PLACES[:d]) for d in range(REACH + 2)]
TILES = STARTS[-1]
HALF_TILE = (PANEL // 2, PANEL)


def position():
    var = lax.axis_index("var")
    return var // SIDE, lax.rem(var, SIDE), lax.axis_index("samp")


def line_peers(group, x, core):
    return [
        (group * SIDE + lax.rem(x + dx, SIDE), lax.rem(core + dc, 2))
        for dx in range(SIDE) for dc in range(2) if dx or dc
    ]


def exchange_kernel(
    dos_ref, received, totals, staged, middle, passing, moments, gathered, sums,
    stage_sem, own_sem, swap_send, swap_recv, group_send, group_recv, stat_send, stat_recv,
):
    group, x, core = position()
    z, y = group // SIDE, lax.rem(group, SIDE)
    stages = []
    for other in range(GROUPS):
        after = (other + 1) % GROUPS * GROUP_COLS
        block = staged.at[other // SIDE, other % SIDE]
        for index, (source, target) in enumerate((
            (pl.ds(other * GROUP_COLS, GROUP_COLS), pl.ds(0, GROUP_COLS)),
            (pl.ds(after, HALO_COLS), pl.ds(GROUP_COLS, HALO_COLS)),
        )):
            copy = pltpu.make_async_copy(dos_ref.at[:, source], block.at[:, target], stage_sem.at[other, index])
            copy.start()
            stages.append(copy)
    peers = line_peers(group, x, core)

    def along_y(step):
        return (z * SIDE + lax.rem(y + step, SIDE)) * SIDE + x, core

    def along_z(step):
        return (lax.rem(z + step, SIDE) * SIDE + y) * SIDE + x, core

    def group_at(offset):
        return lax.rem(z + offset // SIDE, SIDE) * SIDE + lax.rem(y + offset % SIDE, SIDE)

    barrier = pltpu.get_barrier_semaphore()
    for offset in range(1, GROUPS):
        pl.semaphore_signal(
            barrier, inc=1, device_id=(group_at(offset) * SIDE + x, core), device_id_type=MESH
        )
    for peer in peers:
        pl.semaphore_signal(barrier, inc=1, device_id=peer, device_id_type=MESH)
    for copy in stages:
        copy.wait()
    pl.semaphore_wait(barrier, GROUPS - 1 + len(peers))

    places = ((y, z), (z, y))
    routes = ((along_y, along_z), (along_z, along_y))
    every = pl.ds(0, SIDE)
    both = [(half, way) for way in range(2) for half in range(2)]

    def rows_of_half(half):
        return pl.ds(half * HALF, HALF)

    def staged_for(half, place, others):
        if half == 0:
            return staged.at[others, place, rows_of_half(half)]
        return staged.at[place, others, rows_of_half(half)]

    def received_from(half, distance, others):
        if half == 0:
            return received.at[distance, others, rows_of_half(half)]
        return received.at[others, distance, rows_of_half(half)]

    def begin(half, phase, kind, way, source, target):
        copy = pltpu.make_async_remote_copy(
            src_ref=source,
            dst_ref=target,
            send_sem=swap_send.at[half, phase, kind, way],
            recv_sem=swap_recv.at[half, phase, kind, way],
            device_id=routes[half][phase](1 + 2 * way),
            device_id_type=MESH,
        )
        copy.start()
        return copy

    def keep(half, phase, source, target):
        copy = pltpu.make_async_copy(source, target, own_sem.at[half, phase])
        copy.start()
        return copy

    def place_at(half, phase, step):
        return lax.rem(places[half][phase] + step, SIDE)

    far = {
        (half, way): begin(
            half, 0, 0, way, staged_for(half, place_at(half, 0, 2), pl.ds(2 * way, 2)), passing.at[half, 0, way]
        )
        for half, way in both
    }
    near = {
        (half, way): begin(
            half, 0, 1, way, staged_for(half, place_at(half, 0, 1 + 2 * way), every), middle.at[half, 1 + 2 * way]
        )
        for half, way in both
    }
    kept = [keep(half, 0, staged_for(half, places[half][0], every), middle.at[half, 0]) for half in range(2)]

    def chunk_moments(index, carry):
        other = index // SIDE
        columns = pl.ds(pl.multiple_of(lax.rem(index, SIDE) * CHUNK, CHUNK), CHUNK)
        values = staged[other // SIDE, lax.rem(other, SIDE), :, columns]
        values = values.astype(jnp.float32).reshape(ROWS // 8, 8, CHUNK)
        for row, total in enumerate((jnp.sum(values, 0), jnp.sum(values * values, 0))):
            total = jnp.sum(total, 0, keepdims=True)
            for q in range(OWN):
                moments[index, row * OWN + q:row * OWN + q + 1, :] = total[:, q * PANEL:(q + 1) * PANEL]
        return carry

    lax.fori_loop(0, GROUPS * SIDE, chunk_moments, 0)
    for extra in range(REACH):
        moments[GROUPS * SIDE + extra] = moments[extra]
    gathered[0] = moments[pl.ds(group * SIDE, CHUNKS)]
    group_copies = []
    for offset in range(1, GROUPS):
        other = group_at(offset)
        copy = pltpu.make_async_remote_copy(
            src_ref=moments.at[pl.ds(other * SIDE, CHUNKS)],
            dst_ref=gathered.at[offset],
            send_sem=group_send.at[offset],
            recv_sem=group_recv.at[offset],
            device_id=(other * SIDE + x, core),
            device_id_type=MESH,
        )
        copy.start()
        group_copies.append(copy)

    passed = {}
    for half, way in both:
        far[half, way].wait()
        passed[half, way] = begin(
            half, 0, 2, way, passing.at[half, 0, way], middle.at[half, 2, pl.ds(2 * way, 2)]
        )
    for copy in kept:
        copy.wait()
    for key in both:
        near[key].wait()
    far = {}
    for half, way in both:
        if way == 1:
            passed[half, 0].wait()
            passed[half, 1].wait()
        far[half, way] = begin(
            half, 1, 0, way, middle.at[half, pl.ds(2 * way, 2), place_at(half, 1, 2)], passing.at[half, 1, way]
        )
    near = {
        (half, way): begin(
            half, 1, 1, way,
            middle.at[half, every, place_at(half, 1, 1 + 2 * way)],
            received_from(half, 1 + 2 * way, every),
        )
        for half, way in both
    }
    kept = [
        keep(half, 1, middle.at[half, every, places[half][1]], received_from(half, 0, every)) for half in range(2)
    ]
    for copy in group_copies:
        copy.wait()
    sums[0] = jnp.sum(gathered[...], 0)
    line_copies = []
    for index, peer in enumerate(peers):
        copy = pltpu.make_async_remote_copy(
            src_ref=sums.at[0],
            dst_ref=sums.at[index + 1],
            send_sem=stat_send.at[index],
            recv_sem=stat_recv.at[index],
            device_id=peer,
            device_id_type=MESH,
        )
        copy.start()
        line_copies.append(copy)
    passed = {}
    for half, way in both:
        far[half, way].wait()
        passed[half, way] = begin(
            half, 1, 2, way, passing.at[half, 1, way], received_from(half, 2, pl.ds(2 * way, 2))
        )
    for copy in line_copies:
        copy.wait()
    totals[...] = jnp.sum(sums[...], 0)
    for copy in kept + [near[key] for key in both] + [passed[key] for key in both]:
        copy.wait()


def exchange(dosages):
    dma = pltpu.SemaphoreType.DMA
    whole = (SIDE, SIDE, ROWS, COLS)
    moment = (2 * OWN, PANEL)
    return pl.pallas_call(
        exchange_kernel,
        out_shape=(
            jax.ShapeDtypeStruct(whole, jnp.bfloat16),
            jax.ShapeDtypeStruct((CHUNKS,) + moment, jnp.float32),
        ),
        in_specs=[pl.BlockSpec(memory_space=pl.ANY)],
        out_specs=(pl.BlockSpec(memory_space=pl.ANY), pl.BlockSpec(memory_space=pltpu.VMEM)),
        scratch_shapes=[
            pltpu.VMEM(whole, jnp.bfloat16),
            pltpu.VMEM((2, SIDE, SIDE, HALF, COLS), jnp.bfloat16),
            pltpu.VMEM((2, 2, 2, 2, HALF, COLS), jnp.bfloat16),
            pltpu.VMEM((GROUPS * SIDE + REACH,) + moment, jnp.float32),
            pltpu.VMEM((GROUPS, CHUNKS) + moment, jnp.float32),
            pltpu.VMEM((8, CHUNKS) + moment, jnp.float32),
            dma((GROUPS, 2)),
            dma((2, 2)),
            dma((2, 2, 3, 2)),
            dma((2, 2, 3, 2)),
            dma((GROUPS,)),
            dma((GROUPS,)),
            dma((7,)),
            dma((7,)),
        ],
        compiler_params=pltpu.CompilerParams(
            collective_id=0, has_side_effects=True, vmem_limit_bytes=40 * 1024 * 1024
        ),
        name="exchange",
    )(dosages)


def multiply_kernel(received, totals, part, standard, turned):
    step = pl.program_id(0)

    def standardize(chunk):
        moment = totals[chunk]
        mean = moment[0:OWN] * (1.0 / SAMPLES)
        inv_scale = lax.rsqrt(moment[OWN:2 * OWN] * (1.0 / SAMPLES) - mean * mean + 1e-05)
        mean = jnp.concatenate([mean[q:q + 1] for q in range(OWN)], axis=1)
        inv_scale = jnp.concatenate([inv_scale[q:q + 1] for q in range(OWN)], axis=1)
        columns = pl.ds(pl.multiple_of(chunk * CHUNK, CHUNK), CHUNK)

        def block_standard(block, carry):
            rows = pl.ds(pl.multiple_of(block * 128, 128), 128)
            values = received[rows, columns].astype(jnp.float32)
            standard[chunk, rows, :] = ((values - mean) * inv_scale).astype(jnp.bfloat16)
            return carry

        lax.fori_loop(0, LOCAL // 128, block_standard, 0)

    @pl.when(step == 0)
    def _():
        for chunk in range(REACH):
            standardize(chunk)

    standardize(step + REACH)
    turned[...] = standard[step].T
    for d in range(REACH + 1):
        for pp in range(OWN // 2):
            for qq in range(OWN // 2):
                inside = [(p, q) for p in range(2) for q in range(2) if (2 * pp + p, 2 * qq + q) in PLACES[d]]
                if not inside:
                    continue
                block = jnp.dot(
                    turned[pp * BLOCK:(pp + 1) * BLOCK, :],
                    standard[step + d, :, qq * BLOCK:(qq + 1) * BLOCK],
                    preferred_element_type=jnp.float32,
                )
                for p, q in inside:
                    tile = STARTS[d] + PLACES[d].index((2 * pp + p, 2 * qq + q))
                    for half in range(2):
                        first = p * PANEL + half * (PANEL // 2)
                        part[0, half, tile] = block[first:first + PANEL // 2, q * PANEL:(q + 1) * PANEL]


def multiply(received, totals):
    return pl.pallas_call(
        multiply_kernel,
        grid=(SIDE,),
        out_shape=jax.ShapeDtypeStruct((SIDE, 2, TILES) + HALF_TILE, jnp.float32),
        in_specs=[pl.BlockSpec(memory_space=pltpu.VMEM), pl.BlockSpec(memory_space=pltpu.VMEM)],
        out_specs=pl.BlockSpec((1, 2, TILES) + HALF_TILE, lambda step: (step, 0, 0, 0, 0)),
        scratch_shapes=[
            pltpu.VMEM((CHUNKS, LOCAL, CHUNK), jnp.bfloat16),
            pltpu.VMEM((CHUNK, LOCAL), jnp.bfloat16),
        ],
        compiler_params=pltpu.CompilerParams(vmem_limit_bytes=40 * 1024 * 1024),
        name="multiply",
    )(received, totals)


LINE = [2, 1, 3, 0]
MIDDLE = TILES // 2


def reduce_kernel(
    part, out_ref, mine, twin, relay, ring, part_sem, twin_send, twin_recv, ring_send, ring_recv,
):
    group, x, core = position()
    barrier = pltpu.get_barrier_semaphore()
    others = [(group * SIDE + lax.rem(x + step, SIDE), core) for step in (1, 3)] + [(group * SIDE + x, 1 - core)]
    for other in others:
        pl.semaphore_signal(barrier, inc=1, device_id=other, device_id_type=MESH)
    loads = []
    for slot, distance in enumerate(LINE):
        copy = pltpu.make_async_copy(part.at[lax.rem(x + distance, SIDE), core], mine.at[slot], part_sem.at[slot])
        copy.start()
        loads.append(copy)
    pl.semaphore_wait(barrier, len(others))
    twins = []
    for slot, distance in enumerate(LINE):
        copy = pltpu.make_async_remote_copy(
            src_ref=part.at[lax.rem(x + distance, SIDE), 1 - core],
            dst_ref=twin.at[slot],
            send_sem=twin_send.at[slot],
            recv_sem=twin_recv.at[slot],
            device_id=(group * SIDE + x, 1 - core),
            device_id_type=MESH,
        )
        copy.start()
        twins.append(copy)
    halves = (pl.ds(0, MIDDLE), pl.ds(MIDDLE, MIDDLE))

    def add_twin(slot):
        loads[slot].wait()
        twins[slot].wait()
        mine[slot] = mine[slot] + twin[slot]

    def send(slot, half, target, index, distance):
        copy = pltpu.make_async_remote_copy(
            src_ref=mine.at[slot, halves[half]],
            dst_ref=target,
            send_sem=ring_send.at[index],
            recv_sem=ring_recv.at[index],
            device_id=(group * SIDE + lax.rem(x + distance, SIDE), core),
            device_id_type=MESH,
        )
        copy.start()
        return copy

    add_twin(0)
    forth = send(0, 0, relay.at[0], 0, 1)
    back = send(0, 1, relay.at[1], 1, 3)
    add_twin(1)
    sent = [send(1, 1, ring.at[0, halves[1]], 2, 1)]
    add_twin(2)
    sent.append(send(2, 0, ring.at[1, halves[0]], 3, 3))
    forth.wait()
    mine[1, halves[0]] = mine[1, halves[0]] + relay[0]
    sent.append(send(1, 0, ring.at[0, halves[0]], 4, 1))
    back.wait()
    mine[2, halves[1]] = mine[2, halves[1]] + relay[1]
    sent.append(send(2, 1, ring.at[1, halves[1]], 5, 3))
    add_twin(3)
    for copy in sent:
        copy.wait()
    for d in range(REACH + 1):
        for index, (p, q) in enumerate(PLACES[d]):
            tile = STARTS[d] + index
            out_ref[p, d * OWN + q - p] = mine[3, tile] + (ring[0, tile] + ring[1, tile])


def reduce(part):
    dma = pltpu.SemaphoreType.DMA
    return pl.pallas_call(
        reduce_kernel,
        out_shape=jax.ShapeDtypeStruct((OWN, WMAX + 1) + HALF_TILE, jnp.float32),
        in_specs=[pl.BlockSpec(memory_space=pl.ANY)],
        out_specs=pl.BlockSpec(memory_space=pltpu.VMEM),
        scratch_shapes=[
            pltpu.VMEM((SIDE, TILES) + HALF_TILE, jnp.float32),
            pltpu.VMEM((SIDE, TILES) + HALF_TILE, jnp.float32),
            pltpu.VMEM((2, MIDDLE) + HALF_TILE, jnp.float32),
            pltpu.VMEM((2, TILES) + HALF_TILE, jnp.float32),
            dma((SIDE,)),
            dma((SIDE,)),
            dma((SIDE,)),
            dma((6,)),
            dma((6,)),
        ],
        compiler_params=pltpu.CompilerParams(
            collective_id=1, has_side_effects=True, vmem_limit_bytes=30 * 1024 * 1024
        ),
        name="ring",
    )(part)


def per_device(dosages, band_width):
    received, totals = exchange(dosages)
    band_tiles = reduce(multiply(received.reshape(LOCAL, COLS), totals))
    offsets = jnp.arange(WMAX + 1, dtype=jnp.int32)
    panel_count = OWN * lax.axis_size("var")
    global_panel = lax.axis_index("var") * OWN + jnp.arange(OWN, dtype=jnp.int32)
    in_band = (offsets[None, :] <= band_width[:, None]) & (
        global_panel[:, None] + offsets[None, :] < panel_count
    )
    return jnp.where(in_band[:, :, None, None], band_tiles * (1.0 / SAMPLES), 0.0)


def solution(mesh):
    in_specs = (P(("var", "samp"), None), P("var"))
    out_specs = P("var", None, "samp", None)
    return jax.shard_map(
        per_device, mesh=mesh, in_specs=in_specs, out_specs=out_specs, check_vma=False
    )
```

```python
import jax
import jax.numpy as jnp
from jax import lax
from jax.experimental import pallas as pl
from jax.experimental.pallas import tpu as pltpu
from jax.sharding import PartitionSpec as P

MESH = pl.DeviceIdType.MESH
WMAX = 8
PANEL = 128
SIDE = 4
GROUPS = SIDE * SIDE
OWN = 4
CHUNK = OWN * PANEL
REACH = WMAX // OWN
CHUNKS = SIDE + REACH
ROWS = 64
LOCAL = GROUPS * ROWS
BLOCK = 2 * PANEL
STEPS = [(chunk, 0, CHUNK) for chunk in range(CHUNKS - 1)] + [(CHUNKS - 1, first, BLOCK) for first in (0, BLOCK)]
ORDER = [10, 15, 1, 4, 6, 3, 9, 12, 11, 14, 7, 13, 2, 8, 5]
SAMPLES = 8192
PLACES = [
    [(p, q) for q in range(OWN) for p in range(OWN) if 0 <= d * OWN + q - p <= WMAX] for d in range(REACH + 1)
]
STARTS = [sum(len(places) for places in PLACES[:d]) for d in range(REACH + 2)]
TILES = STARTS[-1]


def position():
    var = lax.axis_index("var")
    return var // SIDE, lax.rem(var, SIDE), lax.axis_index("samp")


def tiles_kernel(
    dos_ref, out_ref, staged, received, moments, gathered, sums, totals, standard, turned, part, twin, relay, ring,
    stage_sem, own_sem, swap_send, swap_recv, group_send, group_recv, stat_send, stat_recv, twin_send, twin_recv, relay_recv, ring_send, ring_recv,
):
    group, x, core = position()
    z, y = group // SIDE, lax.rem(group, SIDE)

    def stage(index):
        first = pl.multiple_of(index * CHUNK, CHUNK)
        return pltpu.make_async_copy(dos_ref.at[:, pl.ds(first, CHUNK)], staged.at[index], stage_sem.at[index])

    def stage_begin(index, carry):
        stage(index).start()
        return carry

    def stage_end(index, carry):
        stage(index).wait()
        return carry

    lax.fori_loop(0, GROUPS * SIDE, stage_begin, 0)

    peers = []
    for dx in range(SIDE):
        for dc in range(2):
            if dx or dc:
                peer_x, peer_c = lax.rem(x + dx, SIDE), lax.rem(core + dc, 2)
                peers.append((group * SIDE + peer_x, peer_c))

    def group_at(offset):
        return lax.rem(z + offset // SIDE, SIDE) * SIDE + lax.rem(y + offset % SIDE, SIDE)

    barrier = pltpu.get_barrier_semaphore()
    for offset in range(1, GROUPS):
        pl.semaphore_signal(
            barrier, inc=1, device_id=(group_at(offset) * SIDE + x, core), device_id_type=MESH
        )
    for peer in peers:
        pl.semaphore_signal(barrier, inc=1, device_id=peer, device_id_type=MESH)
    lax.fori_loop(0, GROUPS * SIDE, stage_end, 0)
    pl.semaphore_wait(barrier, GROUPS - 1 + len(peers))

    swaps = {}

    def swap_begin(step):
        chunk, first, count = STEPS[step]
        columns = pl.ds(first, count)
        swaps[step] = []
        for offset in ORDER:
            other = group_at(offset)
            copy = pltpu.make_async_remote_copy(
                src_ref=staged.at[lax.rem(other * SIDE + chunk, GROUPS * SIDE), :, columns],
                dst_ref=received.at[chunk, offset, :, columns],
                send_sem=swap_send.at[step, offset],
                recv_sem=swap_recv.at[step, offset],
                device_id=(other * SIDE + x, core),
                device_id_type=MESH,
            )
            copy.start()
            swaps[step].append(copy)
        copy = pltpu.make_async_copy(
            staged.at[lax.rem(group * SIDE + chunk, GROUPS * SIDE), :, columns],
            received.at[chunk, 0, :, columns],
            own_sem.at[step],
        )
        copy.start()
        swaps[step].append(copy)

    def swap_end(step):
        for copy in swaps[step]:
            copy.wait()

    def local_moments():
        def chunk_moments(index, carry):
            values = staged[index].astype(jnp.float32).reshape(ROWS // 8, 8, CHUNK)
            for row, total in enumerate((jnp.sum(values, 0), jnp.sum(values * values, 0))):
                total = jnp.sum(total, 0, keepdims=True)
                for q in range(OWN):
                    moments[index, row * OWN + q:row * OWN + q + 1, :] = total[:, q * PANEL:(q + 1) * PANEL]
            return carry

        lax.fori_loop(0, GROUPS * SIDE, chunk_moments, 0)
        for extra in range(REACH):
            moments[GROUPS * SIDE + extra] = moments[extra]

    def group_moments_begin():
        gathered[0] = moments[pl.ds(group * SIDE, CHUNKS)]
        copies = []
        for offset in range(1, GROUPS):
            other = group_at(offset)
            copy = pltpu.make_async_remote_copy(
                src_ref=moments.at[pl.ds(other * SIDE, CHUNKS)],
                dst_ref=gathered.at[offset],
                send_sem=group_send.at[offset],
                recv_sem=group_recv.at[offset],
                device_id=(other * SIDE + x, core),
                device_id_type=MESH,
            )
            copy.start()
            copies.append(copy)
        return copies

    def ring_moments_begin(copies):
        for copy in copies:
            copy.wait()
        sums[0] = jnp.sum(gathered[...], 0)
        copies = []
        for index, peer in enumerate(peers):
            copy = pltpu.make_async_remote_copy(
                src_ref=sums.at[0],
                dst_ref=sums.at[index + 1],
                send_sem=stat_send.at[index],
                recv_sem=stat_recv.at[index],
                device_id=peer,
                device_id_type=MESH,
            )
            copy.start()
            copies.append(copy)
        return copies

    def ring_moments_end(copies):
        for copy in copies:
            copy.wait()
        totals[...] = jnp.sum(sums[...], 0)

    def standardize(step):
        chunk, start, count = STEPS[step]
        columns = pl.ds(start, count)
        panels = range(start // PANEL, (start + count) // PANEL)
        first, second = totals[chunk, 0:OWN], totals[chunk, OWN:2 * OWN]
        mean = first * (1.0 / SAMPLES)
        inv_scale = lax.rsqrt(second * (1.0 / SAMPLES) - mean * mean + 1e-05)
        mean = jnp.concatenate([mean[q:q + 1] for q in panels], axis=1)
        inv_scale = jnp.concatenate([inv_scale[q:q + 1] for q in panels], axis=1)

        def block_standard(block, carry):
            rows = pl.ds(pl.multiple_of(block * ROWS, ROWS), ROWS)
            values = received[chunk, block, :, columns].astype(jnp.float32)
            standard[chunk, rows, columns] = ((values - mean) * inv_scale).astype(jnp.bfloat16)
            return carry

        lax.fori_loop(0, GROUPS, block_standard, 0)
        if chunk < SIDE:
            turned[chunk] = standard[chunk].T

    def pieces_of(step):
        chunk, start, count = STEPS[step]
        pieces = []
        for d in range(REACH + 1):
            if 0 <= chunk - d < SIDE:
                inside = [
                    index for index, (p, q) in enumerate(PLACES[d])
                    if start // PANEL <= q < (start + count) // PANEL
                ]
                pieces.append((chunk - d, d, d + (start > 0), STARTS[d] + inside[0], len(inside)))
        return pieces

    def twin_copy(rows_chunk, number, first, count):
        which = pl.ds(first, count)
        return pltpu.make_async_remote_copy(
            src_ref=part.at[rows_chunk, 1 - core, which],
            dst_ref=twin.at[rows_chunk, which],
            send_sem=twin_send.at[rows_chunk, number],
            recv_sem=twin_recv.at[rows_chunk, number],
            device_id=(group * SIDE + x, 1 - core),
            device_id_type=MESH,
        )

    def multiply(step):
        chunk, start, columns = STEPS[step]
        for rows_chunk, d, number, first, count in pieces_of(step):
            for pp in range(OWN // 2):
                for qq in range(start // BLOCK, (start + columns) // BLOCK):
                    inside = [
                        (p, q) for p in range(2) for q in range(2) if (2 * pp + p, 2 * qq + q) in PLACES[d]
                    ]
                    if not inside:
                        continue
                    block = jnp.dot(
                        turned[rows_chunk, pp * BLOCK:(pp + 1) * BLOCK, :],
                        standard[chunk, :, qq * BLOCK:(qq + 1) * BLOCK],
                        preferred_element_type=jnp.float32,
                    )
                    for p, q in inside:
                        tile = STARTS[d] + PLACES[d].index((2 * pp + p, 2 * qq + q))
                        for half in range(2):
                            top = p * PANEL + half * (PANEL // 2)
                            part[rows_chunk, half, tile] = block[
                                top:top + PANEL // 2, q * PANEL:(q + 1) * PANEL
                            ]
            twin_copy(rows_chunk, number, first, count).start()

    def halves_of(first, count):
        upper = (count + 1) // 2
        return pl.ds(first, upper), pl.ds(first + upper, count - upper)

    def line_copy(rows_chunk, number, halves, half, way, relayed):
        which = halves[half]
        return pltpu.make_async_remote_copy(
            src_ref=part.at[rows_chunk, core, which],
            dst_ref=(relay if relayed else ring).at[way, which],
            send_sem=ring_send.at[rows_chunk, number, half],
            recv_sem=relay_recv.at[way, number] if relayed else ring_recv.at[way, number, half],
            device_id=(group * SIDE + lax.rem(x + 1 + 2 * way, SIDE), core),
            device_id_type=MESH,
        )

    def reduce(step):
        for rows_chunk, d, number, first, count in pieces_of(step):
            which = pl.ds(first, count)
            halves = halves_of(first, count)
            twin_copy(rows_chunk, number, first, count).wait()
            part[rows_chunk, core, which] = part[rows_chunk, core, which] + twin[rows_chunk, which]
            distance = lax.rem(rows_chunk - x + SIDE, SIDE)

            @pl.when(distance == 2)
            def _():
                line_copy(rows_chunk, number, halves, 0, 0, True).start()
                line_copy(rows_chunk, number, halves, 1, 1, True).start()

            @pl.when(distance == 1)
            def _():
                line_copy(rows_chunk, number, halves, 1, 0, False).start()

            @pl.when(distance == 3)
            def _():
                line_copy(rows_chunk, number, halves, 0, 1, False).start()

        for rows_chunk, d, number, first, count in pieces_of(step):
            halves = halves_of(first, count)
            distance = lax.rem(rows_chunk - x + SIDE, SIDE)
            for way in range(2):

                @pl.when(distance == 1 + 2 * way)
                def _():
                    which = halves[way]
                    line_copy(rows_chunk, number, halves, way, way, True).wait_recv()
                    part[rows_chunk, core, which] = part[rows_chunk, core, which] + relay[way, which]
                    line_copy(rows_chunk, number, halves, way, way, False).start()

    swap_begin(0)
    swap_begin(1)
    local_moments()
    copies = group_moments_begin()
    swap_begin(2)
    copies = ring_moments_begin(copies)
    ring_moments_end(copies)
    for step in range(len(STEPS)):
        swap_end(step)
        if step + 3 < len(STEPS):
            swap_begin(step + 3)
        standardize(step)
        multiply(step)
        reduce(step)

    for step in range(len(STEPS)):
        for rows_chunk, d, number, first, count in pieces_of(step):
            halves = halves_of(first, count)

            @pl.when(x != rows_chunk)
            def _():
                for half in range(2):
                    line_copy(rows_chunk, number, halves, half, 0, False).wait_send()

            @pl.when(x == rows_chunk)
            def _():
                for way in range(2):
                    for half in range(2):
                        line_copy(rows_chunk, number, halves, half, way, False).wait_recv()

    for d in range(REACH + 1):
        for index, (p, q) in enumerate(PLACES[d]):
            tile = STARTS[d] + index
            out_ref[p, d * OWN + q - p] = part[x, core, tile] + (ring[0, tile] + ring[1, tile])


def tiles(dosages):
    half_tile = (PANEL // 2, PANEL)
    dma = pltpu.SemaphoreType.DMA
    return pl.pallas_call(
        tiles_kernel,
        out_shape=jax.ShapeDtypeStruct((OWN, WMAX + 1) + half_tile, jnp.float32),
        in_specs=[pl.BlockSpec(memory_space=pl.ANY)],
        out_specs=pl.BlockSpec(memory_space=pltpu.VMEM),
        scratch_shapes=[
            pltpu.VMEM((GROUPS * SIDE, ROWS, CHUNK), jnp.bfloat16),
            pltpu.VMEM((CHUNKS, GROUPS, ROWS, CHUNK), jnp.bfloat16),
            pltpu.VMEM((GROUPS * SIDE + REACH, 2 * OWN, PANEL), jnp.float32),
            pltpu.VMEM((GROUPS, CHUNKS, 2 * OWN, PANEL), jnp.float32),
            pltpu.VMEM((8, CHUNKS, 2 * OWN, PANEL), jnp.float32),
            pltpu.VMEM((CHUNKS, 2 * OWN, PANEL), jnp.float32),
            pltpu.VMEM((CHUNKS, LOCAL, CHUNK), jnp.bfloat16),
            pltpu.VMEM((SIDE, CHUNK, LOCAL), jnp.bfloat16),
            pltpu.VMEM((SIDE, 2, TILES) + half_tile, jnp.float32),
            pltpu.VMEM((SIDE, TILES) + half_tile, jnp.float32),
            pltpu.VMEM((2, TILES) + half_tile, jnp.float32),
            pltpu.VMEM((2, TILES) + half_tile, jnp.float32),
            dma((GROUPS * SIDE,)),
            dma((len(STEPS),)),
            dma((len(STEPS), GROUPS)),
            dma((len(STEPS), GROUPS)),
            dma((GROUPS,)),
            dma((GROUPS,)),
            dma((7,)),
            dma((7,)),
            dma((SIDE, REACH + 2)),
            dma((SIDE, REACH + 2)),
            dma((2, REACH + 2)),
            dma((SIDE, REACH + 2, 2)),
            dma((2, REACH + 2, 2)),
        ],
        compiler_params=pltpu.CompilerParams(
            collective_id=0, has_side_effects=True, vmem_limit_bytes=60 * 1024 * 1024
        ),
        name="tiles",
    )(dosages)


def per_device(dosages, band_width):
    band_tiles = tiles(dosages)
    offsets = jnp.arange(WMAX + 1, dtype=jnp.int32)
    panel_count = OWN * lax.axis_size("var")
    global_panel = lax.axis_index("var") * OWN + jnp.arange(OWN, dtype=jnp.int32)
    in_band = (offsets[None, :] <= band_width[:, None]) & (
        global_panel[:, None] + offsets[None, :] < panel_count
    )
    return jnp.where(in_band[:, :, None, None], band_tiles * (1.0 / SAMPLES), 0.0)


def solution(mesh):
    in_specs = (P(("var", "samp"), None), P("var"))
    out_specs = P("var", None, "samp", None)
    return jax.shard_map(
        per_device, mesh=mesh, in_specs=in_specs, out_specs=out_specs, check_vma=False
    )
```

```python
import jax
import jax.numpy as jnp
from jax import lax
from jax.experimental import pallas as pl
from jax.experimental.pallas import tpu as pltpu
from jax.sharding import PartitionSpec as P

MESH = pl.DeviceIdType.MESH
WMAX = 8
PANEL = 128
SIDE = 4
GROUPS = SIDE * SIDE
OWN = 4
CHUNK = OWN * PANEL
REACH = WMAX // OWN
CHUNKS = SIDE + REACH
ROWS = 64
LOCAL = GROUPS * ROWS
BLOCK = 2 * PANEL
STEPS = [(chunk, 0, CHUNK) for chunk in range(CHUNKS - 1)] + [(CHUNKS - 1, first, BLOCK) for first in (0, BLOCK)]
AHEAD = 8
ORDER = [10, 15, 1, 4, 6, 3, 9, 12, 11, 14, 7, 13, 2, 8, 5]
SAMPLES = 8192
PLACES = [
    [(p, q) for q in range(OWN) for p in range(OWN) if 0 <= d * OWN + q - p <= WMAX] for d in range(REACH + 1)
]
STARTS = [sum(len(places) for places in PLACES[:d]) for d in range(REACH + 2)]
TILES = STARTS[-1]


def position():
    var = lax.axis_index("var")
    return var // SIDE, lax.rem(var, SIDE), lax.axis_index("samp")


def tiles_kernel(
    dos_ref, out_ref, staged, received, moments, gathered, sums, totals, standard, turned, part, twin, relay, ring,
    stage_sem, own_sem, swap_send, swap_recv, group_send, group_recv, stat_send, stat_recv, twin_send, twin_recv, relay_recv, ring_send, ring_recv,
):
    group, x, core = position()
    z, y = group // SIDE, lax.rem(group, SIDE)

    def stage(index):
        first = pl.multiple_of(index * CHUNK, CHUNK)
        return pltpu.make_async_copy(dos_ref.at[:, pl.ds(first, CHUNK)], staged.at[index], stage_sem.at[index])

    def stage_begin(index, carry):
        stage(index).start()
        return carry

    def stage_end(index, carry):
        stage(index).wait()
        return carry

    lax.fori_loop(0, GROUPS * SIDE, stage_begin, 0)

    peers = []
    for dx in range(SIDE):
        for dc in range(2):
            if dx or dc:
                peer_x, peer_c = lax.rem(x + dx, SIDE), lax.rem(core + dc, 2)
                peers.append((group * SIDE + peer_x, peer_c))

    def group_at(offset):
        return lax.rem(z + offset // SIDE, SIDE) * SIDE + lax.rem(y + offset % SIDE, SIDE)

    barrier = pltpu.get_barrier_semaphore()
    for offset in range(1, GROUPS):
        pl.semaphore_signal(
            barrier, inc=1, device_id=(group_at(offset) * SIDE + x, core), device_id_type=MESH
        )
    for peer in peers:
        pl.semaphore_signal(barrier, inc=1, device_id=peer, device_id_type=MESH)
    lax.fori_loop(0, GROUPS * SIDE, stage_end, 0)
    pl.semaphore_wait(barrier, GROUPS - 1 + len(peers))

    def swap(index):
        step, turn = divmod(index, GROUPS - 1)
        chunk, first, count = STEPS[step]
        columns = pl.ds(first, count)
        offset = ORDER[turn]
        other = group_at(offset)
        return pltpu.make_async_remote_copy(
            src_ref=staged.at[lax.rem(other * SIDE + chunk, GROUPS * SIDE), :, columns],
            dst_ref=received.at[chunk, offset, :, columns],
            send_sem=swap_send.at[step, offset],
            recv_sem=swap_recv.at[step, offset],
            device_id=(other * SIDE + x, core),
            device_id_type=MESH,
        )

    swaps = [swap(index) for index in range(len(STEPS) * (GROUPS - 1))]
    started = [0]

    def pump(count):
        for index in range(started[0], min(started[0] + count, len(swaps))):
            if index >= AHEAD:
                swaps[index - AHEAD].wait_send()
            swaps[index].start()
            started[0] = index + 1

    def own_copy(step):
        chunk, first, count = STEPS[step]
        columns = pl.ds(first, count)
        return pltpu.make_async_copy(
            staged.at[lax.rem(group * SIDE + chunk, GROUPS * SIDE), :, columns],
            received.at[chunk, 0, :, columns],
            own_sem.at[step],
        )

    def swap_end(step):
        own_copy(step).wait()
        for copy in swaps[step * (GROUPS - 1):(step + 1) * (GROUPS - 1)]:
            copy.wait_recv()

    def local_moments():
        def chunk_moments(index, carry):
            values = staged[index].astype(jnp.float32).reshape(ROWS // 8, 8, CHUNK)
            for row, total in enumerate((jnp.sum(values, 0), jnp.sum(values * values, 0))):
                total = jnp.sum(total, 0, keepdims=True)
                for q in range(OWN):
                    moments[index, row * OWN + q:row * OWN + q + 1, :] = total[:, q * PANEL:(q + 1) * PANEL]
            return carry

        lax.fori_loop(0, GROUPS * SIDE, chunk_moments, 0)
        for extra in range(REACH):
            moments[GROUPS * SIDE + extra] = moments[extra]

    def group_moments_begin():
        gathered[0] = moments[pl.ds(group * SIDE, CHUNKS)]
        copies = []
        for offset in range(1, GROUPS):
            other = group_at(offset)
            copy = pltpu.make_async_remote_copy(
                src_ref=moments.at[pl.ds(other * SIDE, CHUNKS)],
                dst_ref=gathered.at[offset],
                send_sem=group_send.at[offset],
                recv_sem=group_recv.at[offset],
                device_id=(other * SIDE + x, core),
                device_id_type=MESH,
            )
            copy.start()
            copies.append(copy)
        return copies

    def ring_moments_begin(copies):
        for copy in copies:
            copy.wait()
        sums[0] = jnp.sum(gathered[...], 0)
        copies = []
        for index, peer in enumerate(peers):
            copy = pltpu.make_async_remote_copy(
                src_ref=sums.at[0],
                dst_ref=sums.at[index + 1],
                send_sem=stat_send.at[index],
                recv_sem=stat_recv.at[index],
                device_id=peer,
                device_id_type=MESH,
            )
            copy.start()
            copies.append(copy)
        return copies

    def ring_moments_end(copies):
        for copy in copies:
            copy.wait()
        totals[...] = jnp.sum(sums[...], 0)

    def standardize(step):
        chunk, start, count = STEPS[step]
        columns = pl.ds(start, count)
        panels = range(start // PANEL, (start + count) // PANEL)
        first, second = totals[chunk, 0:OWN], totals[chunk, OWN:2 * OWN]
        mean = first * (1.0 / SAMPLES)
        inv_scale = lax.rsqrt(second * (1.0 / SAMPLES) - mean * mean + 1e-05)
        mean = jnp.concatenate([mean[q:q + 1] for q in panels], axis=1)
        inv_scale = jnp.concatenate([inv_scale[q:q + 1] for q in panels], axis=1)

        def block_standard(block, carry):
            rows = pl.ds(pl.multiple_of(block * ROWS, ROWS), ROWS)
            values = received[chunk, block, :, columns].astype(jnp.float32)
            standard[chunk, rows, columns] = ((values - mean) * inv_scale).astype(jnp.bfloat16)
            return carry

        lax.fori_loop(0, GROUPS, block_standard, 0)
        if chunk < SIDE:
            turned[chunk] = standard[chunk].T

    def pieces_of(step):
        chunk, start, count = STEPS[step]
        pieces = []
        for d in range(REACH + 1):
            if 0 <= chunk - d < SIDE:
                inside = [
                    index for index, (p, q) in enumerate(PLACES[d])
                    if start // PANEL <= q < (start + count) // PANEL
                ]
                pieces.append((chunk - d, d, d + (start > 0), STARTS[d] + inside[0], len(inside)))
        return pieces

    def twin_copy(rows_chunk, number, first, count):
        which = pl.ds(first, count)
        return pltpu.make_async_remote_copy(
            src_ref=part.at[rows_chunk, 1 - core, which],
            dst_ref=twin.at[rows_chunk, which],
            send_sem=twin_send.at[rows_chunk, number],
            recv_sem=twin_recv.at[rows_chunk, number],
            device_id=(group * SIDE + x, 1 - core),
            device_id_type=MESH,
        )

    def multiply(step):
        chunk, start, columns = STEPS[step]
        for rows_chunk, d, number, first, count in pieces_of(step):
            for pp in range(OWN // 2):
                for qq in range(start // BLOCK, (start + columns) // BLOCK):
                    inside = [
                        (p, q) for p in range(2) for q in range(2) if (2 * pp + p, 2 * qq + q) in PLACES[d]
                    ]
                    if not inside:
                        continue
                    block = jnp.dot(
                        turned[rows_chunk, pp * BLOCK:(pp + 1) * BLOCK, :],
                        standard[chunk, :, qq * BLOCK:(qq + 1) * BLOCK],
                        preferred_element_type=jnp.float32,
                    )
                    for p, q in inside:
                        tile = STARTS[d] + PLACES[d].index((2 * pp + p, 2 * qq + q))
                        for half in range(2):
                            top = p * PANEL + half * (PANEL // 2)
                            part[rows_chunk, half, tile] = block[
                                top:top + PANEL // 2, q * PANEL:(q + 1) * PANEL
                            ]
            twin_copy(rows_chunk, number, first, count).start()

    def halves_of(first, count):
        upper = (count + 1) // 2
        return pl.ds(first, upper), pl.ds(first + upper, count - upper)

    def line_copy(rows_chunk, number, halves, half, way, relayed):
        which = halves[half]
        return pltpu.make_async_remote_copy(
            src_ref=part.at[rows_chunk, core, which],
            dst_ref=(relay if relayed else ring).at[way, which],
            send_sem=ring_send.at[rows_chunk, number, half],
            recv_sem=relay_recv.at[way, number] if relayed else ring_recv.at[way, number, half],
            device_id=(group * SIDE + lax.rem(x + 1 + 2 * way, SIDE), core),
            device_id_type=MESH,
        )

    def reduce(step):
        for rows_chunk, d, number, first, count in pieces_of(step):
            which = pl.ds(first, count)
            halves = halves_of(first, count)
            twin_copy(rows_chunk, number, first, count).wait()
            part[rows_chunk, core, which] = part[rows_chunk, core, which] + twin[rows_chunk, which]
            distance = lax.rem(rows_chunk - x + SIDE, SIDE)

            @pl.when(distance == 2)
            def _():
                line_copy(rows_chunk, number, halves, 0, 0, True).start()
                line_copy(rows_chunk, number, halves, 1, 1, True).start()

            @pl.when(distance == 1)
            def _():
                line_copy(rows_chunk, number, halves, 1, 0, False).start()

            @pl.when(distance == 3)
            def _():
                line_copy(rows_chunk, number, halves, 0, 1, False).start()

        pump(5)
        for rows_chunk, d, number, first, count in pieces_of(step):
            halves = halves_of(first, count)
            distance = lax.rem(rows_chunk - x + SIDE, SIDE)
            for way in range(2):

                @pl.when(distance == 1 + 2 * way)
                def _():
                    which = halves[way]
                    line_copy(rows_chunk, number, halves, way, way, True).wait_recv()
                    part[rows_chunk, core, which] = part[rows_chunk, core, which] + relay[way, which]
                    line_copy(rows_chunk, number, halves, way, way, False).start()

    pump(4)
    for step in range(len(STEPS)):
        own_copy(step).start()
    local_moments()
    copies = group_moments_begin()
    pump(8)
    copies = ring_moments_begin(copies)
    pump(8)
    ring_moments_end(copies)
    for step in range(len(STEPS)):
        pump((step + 1) * (GROUPS - 1) + AHEAD - started[0])
        swap_end(step)
        standardize(step)
        multiply(step)
        pump(3)
        reduce(step)
        pump(3)
    for copy in swaps[-AHEAD:]:
        copy.wait_send()

    for step in range(len(STEPS)):
        for rows_chunk, d, number, first, count in pieces_of(step):
            halves = halves_of(first, count)

            @pl.when(x != rows_chunk)
            def _():
                for half in range(2):
                    line_copy(rows_chunk, number, halves, half, 0, False).wait_send()

            @pl.when(x == rows_chunk)
            def _():
                for way in range(2):
                    for half in range(2):
                        line_copy(rows_chunk, number, halves, half, way, False).wait_recv()

    for d in range(REACH + 1):
        for index, (p, q) in enumerate(PLACES[d]):
            tile = STARTS[d] + index
            out_ref[p, d * OWN + q - p] = part[x, core, tile] + (ring[0, tile] + ring[1, tile])


def tiles(dosages):
    half_tile = (PANEL // 2, PANEL)
    dma = pltpu.SemaphoreType.DMA
    return pl.pallas_call(
        tiles_kernel,
        out_shape=jax.ShapeDtypeStruct((OWN, WMAX + 1) + half_tile, jnp.float32),
        in_specs=[pl.BlockSpec(memory_space=pl.ANY)],
        out_specs=pl.BlockSpec(memory_space=pltpu.VMEM),
        scratch_shapes=[
            pltpu.VMEM((GROUPS * SIDE, ROWS, CHUNK), jnp.bfloat16),
            pltpu.VMEM((CHUNKS, GROUPS, ROWS, CHUNK), jnp.bfloat16),
            pltpu.VMEM((GROUPS * SIDE + REACH, 2 * OWN, PANEL), jnp.float32),
            pltpu.VMEM((GROUPS, CHUNKS, 2 * OWN, PANEL), jnp.float32),
            pltpu.VMEM((8, CHUNKS, 2 * OWN, PANEL), jnp.float32),
            pltpu.VMEM((CHUNKS, 2 * OWN, PANEL), jnp.float32),
            pltpu.VMEM((CHUNKS, LOCAL, CHUNK), jnp.bfloat16),
            pltpu.VMEM((SIDE, CHUNK, LOCAL), jnp.bfloat16),
            pltpu.VMEM((SIDE, 2, TILES) + half_tile, jnp.float32),
            pltpu.VMEM((SIDE, TILES) + half_tile, jnp.float32),
            pltpu.VMEM((2, TILES) + half_tile, jnp.float32),
            pltpu.VMEM((2, TILES) + half_tile, jnp.float32),
            dma((GROUPS * SIDE,)),
            dma((len(STEPS),)),
            dma((len(STEPS), GROUPS)),
            dma((len(STEPS), GROUPS)),
            dma((GROUPS,)),
            dma((GROUPS,)),
            dma((7,)),
            dma((7,)),
            dma((SIDE, REACH + 2)),
            dma((SIDE, REACH + 2)),
            dma((2, REACH + 2)),
            dma((SIDE, REACH + 2, 2)),
            dma((2, REACH + 2, 2)),
        ],
        compiler_params=pltpu.CompilerParams(
            collective_id=0, has_side_effects=True, vmem_limit_bytes=60 * 1024 * 1024
        ),
        name="tiles",
    )(dosages)


def per_device(dosages, band_width):
    band_tiles = tiles(dosages)
    offsets = jnp.arange(WMAX + 1, dtype=jnp.int32)
    panel_count = OWN * lax.axis_size("var")
    global_panel = lax.axis_index("var") * OWN + jnp.arange(OWN, dtype=jnp.int32)
    in_band = (offsets[None, :] <= band_width[:, None]) & (
        global_panel[:, None] + offsets[None, :] < panel_count
    )
    return jnp.where(in_band[:, :, None, None], band_tiles * (1.0 / SAMPLES), 0.0)


def solution(mesh):
    in_specs = (P(("var", "samp"), None), P("var"))
    out_specs = P("var", None, "samp", None)
    return jax.shard_map(
        per_device, mesh=mesh, in_specs=in_specs, out_specs=out_specs, check_vma=False
    )
```

```python
import jax
import jax.numpy as jnp
from jax import lax
from jax.experimental import pallas as pl
from jax.experimental.pallas import tpu as pltpu
from jax.sharding import PartitionSpec as P

MESH = pl.DeviceIdType.MESH
WMAX = 8
PANEL = 128
SIDE = 4
GROUPS = SIDE * SIDE
OWN = 4
CHUNK = OWN * PANEL
REACH = WMAX // OWN
CHUNKS = SIDE + REACH
ROWS = 64
LOCAL = GROUPS * ROWS
BLOCK = 2 * PANEL
SWAPS = [(0, 2, 0, CHUNK), (2, 2, 0, CHUNK), (4, 1, 0, CHUNK), (5, 1, 0, BLOCK), (5, 1, BLOCK, BLOCK)]
READY = [0, 0, 1, 1, 2, 3, 4]
STEPS = [(chunk, 0, CHUNK) for chunk in range(CHUNKS - 1)] + [(CHUNKS - 1, first, BLOCK) for first in (0, BLOCK)]
AHEAD = 4
LAG = 2
ORDER = [10, 15, 1, 4, 6, 3, 9, 12, 11, 14, 7, 13, 2, 8, 5]
PARTNER = [1, 0, 3, 2, 5, 4, 7, 6, 9, 8, 11, 10, 13, 12, 14]
SAMPLES = 8192
PLACES = [
    [(p, q) for q in range(OWN) for p in range(OWN) if 0 <= d * OWN + q - p <= WMAX] for d in range(REACH + 1)
]
STARTS = [sum(len(places) for places in PLACES[:d]) for d in range(REACH + 2)]
TILES = STARTS[-1]


def position():
    var = lax.axis_index("var")
    return var // SIDE, lax.rem(var, SIDE), lax.axis_index("samp")


def tiles_kernel(
    dos_ref, out_ref, staged, received, moments, gathered, sums, totals, standard, turned, part, twin, relay, ring,
    stage_sem, own_sem, swap_send, swap_recv, group_send, group_recv, stat_send, stat_recv, twin_send, twin_recv, relay_recv, ring_send, ring_recv,
):
    group, x, core = position()
    z, y = group // SIDE, lax.rem(group, SIDE)

    def stage(index):
        first = pl.multiple_of(index * CHUNK, CHUNK)
        return pltpu.make_async_copy(dos_ref.at[:, pl.ds(first, CHUNK)], staged.at[index], stage_sem.at[index])

    def stage_begin(index, carry):
        stage(index).start()
        return carry

    def stage_end(index, carry):
        stage(index).wait()
        return carry

    lax.fori_loop(0, GROUPS * SIDE, stage_begin, 0)

    peers = []
    for dx in range(SIDE):
        for dc in range(2):
            if dx or dc:
                peer_x, peer_c = lax.rem(x + dx, SIDE), lax.rem(core + dc, 2)
                peers.append((group * SIDE + peer_x, peer_c))

    def group_at(offset):
        return lax.rem(z + offset // SIDE, SIDE) * SIDE + lax.rem(y + lax.rem(offset, SIDE), SIDE)

    barrier = pltpu.get_barrier_semaphore()
    for offset in range(1, GROUPS):
        pl.semaphore_signal(
            barrier, inc=1, device_id=(group_at(offset) * SIDE + x, core), device_id_type=MESH
        )
    for peer in peers:
        pl.semaphore_signal(barrier, inc=1, device_id=peer, device_id_type=MESH)
    lax.fori_loop(0, GROUPS * SIDE, stage_end, 0)
    pl.semaphore_wait(barrier, GROUPS - 1 + len(peers))

    def swap(index):
        step, turn = divmod(index, GROUPS - 1)
        chunk, chunks, first, count = SWAPS[step]
        columns = pl.ds(first, count)
        offset = ORDER[turn] + core * (ORDER[PARTNER[turn]] - ORDER[turn])
        other = group_at(offset)
        return pltpu.make_async_remote_copy(
            src_ref=staged.at[pl.ds(lax.rem(other * SIDE + chunk, GROUPS * SIDE), chunks), :, columns],
            dst_ref=received.at[pl.ds(chunk, chunks), offset, :, columns],
            send_sem=swap_send.at[step, offset],
            recv_sem=swap_recv.at[step, offset],
            device_id=(other * SIDE + x, core),
            device_id_type=MESH,
        )

    swaps = [swap(index) for index in range(len(SWAPS) * (GROUPS - 1))]
    started, arrived = [0], [0]

    def arrive(count):
        for index in range(arrived[0], count):
            swaps[index].wait_recv()
            arrived[0] = index + 1

    def pump(count):
        for index in range(started[0], min(started[0] + count, len(swaps))):
            if index >= AHEAD:
                swaps[index - AHEAD].wait_send()
            arrive(index - AHEAD - LAG)
            swaps[index].start()
            started[0] = index + 1

    def own_copy(step):
        chunk, chunks, first, count = SWAPS[step]
        columns = pl.ds(first, count)
        return pltpu.make_async_copy(
            staged.at[pl.ds(lax.rem(group * SIDE + chunk, GROUPS * SIDE), chunks), :, columns],
            received.at[pl.ds(chunk, chunks), 0, :, columns],
            own_sem.at[step],
        )

    def swap_end(step):
        own_copy(step).wait()
        arrive((step + 1) * (GROUPS - 1))

    def local_moments():
        def chunk_moments(index, carry):
            values = staged[index].astype(jnp.float32).reshape(ROWS // 8, 8, CHUNK)
            for row, total in enumerate((jnp.sum(values, 0), jnp.sum(values * values, 0))):
                total = jnp.sum(total, 0, keepdims=True)
                for q in range(OWN):
                    moments[index, row * OWN + q:row * OWN + q + 1, :] = total[:, q * PANEL:(q + 1) * PANEL]
            return carry

        lax.fori_loop(0, GROUPS * SIDE, chunk_moments, 0)
        for extra in range(REACH):
            moments[GROUPS * SIDE + extra] = moments[extra]

    def group_moments_begin():
        gathered[0] = moments[pl.ds(group * SIDE, CHUNKS)]
        copies = []
        for offset in range(1, GROUPS):
            other = group_at(offset)
            copy = pltpu.make_async_remote_copy(
                src_ref=moments.at[pl.ds(other * SIDE, CHUNKS)],
                dst_ref=gathered.at[offset],
                send_sem=group_send.at[offset],
                recv_sem=group_recv.at[offset],
                device_id=(other * SIDE + x, core),
                device_id_type=MESH,
            )
            copy.start()
            copies.append(copy)
        return copies

    def ring_moments_begin(copies):
        for copy in copies:
            copy.wait()
        sums[0] = jnp.sum(gathered[...], 0)
        copies = []
        for index, peer in enumerate(peers):
            copy = pltpu.make_async_remote_copy(
                src_ref=sums.at[0],
                dst_ref=sums.at[index + 1],
                send_sem=stat_send.at[index],
                recv_sem=stat_recv.at[index],
                device_id=peer,
                device_id_type=MESH,
            )
            copy.start()
            copies.append(copy)
        return copies

    def ring_moments_end(copies):
        for copy in copies:
            copy.wait()
        totals[...] = jnp.sum(sums[...], 0)

    def standardize(step):
        chunk, start, count = STEPS[step]
        columns = pl.ds(start, count)
        panels = range(start // PANEL, (start + count) // PANEL)
        first, second = totals[chunk, 0:OWN], totals[chunk, OWN:2 * OWN]
        mean = first * (1.0 / SAMPLES)
        inv_scale = lax.rsqrt(second * (1.0 / SAMPLES) - mean * mean + 1e-05)
        mean = jnp.concatenate([mean[q:q + 1] for q in panels], axis=1)
        inv_scale = jnp.concatenate([inv_scale[q:q + 1] for q in panels], axis=1)

        def block_standard(block, carry):
            rows = pl.ds(pl.multiple_of(block * ROWS, ROWS), ROWS)
            values = received[chunk, block, :, columns].astype(jnp.float32)
            standard[chunk, rows, columns] = ((values - mean) * inv_scale).astype(jnp.bfloat16)
            return carry

        lax.fori_loop(0, GROUPS, block_standard, 0)
        if chunk < SIDE:
            turned[chunk] = standard[chunk].T

    def pieces_of(step):
        chunk, start, count = STEPS[step]
        pieces = []
        for d in range(REACH + 1):
            if 0 <= chunk - d < SIDE:
                inside = [
                    index for index, (p, q) in enumerate(PLACES[d])
                    if start // PANEL <= q < (start + count) // PANEL
                ]
                pieces.append((chunk - d, d, d + (start > 0), STARTS[d] + inside[0], len(inside)))
        return pieces

    def twin_copy(rows_chunk, number, first, count):
        which = pl.ds(first, count)
        return pltpu.make_async_remote_copy(
            src_ref=part.at[rows_chunk, 1 - core, which],
            dst_ref=twin.at[rows_chunk, which],
            send_sem=twin_send.at[rows_chunk, number],
            recv_sem=twin_recv.at[rows_chunk, number],
            device_id=(group * SIDE + x, 1 - core),
            device_id_type=MESH,
        )

    def multiply(step):
        chunk, start, columns = STEPS[step]
        for rows_chunk, d, number, first, count in pieces_of(step):
            for pp in range(OWN // 2):
                for qq in range(start // BLOCK, (start + columns) // BLOCK):
                    inside = [
                        (p, q) for p in range(2) for q in range(2) if (2 * pp + p, 2 * qq + q) in PLACES[d]
                    ]
                    if not inside:
                        continue
                    block = jnp.dot(
                        turned[rows_chunk, pp * BLOCK:(pp + 1) * BLOCK, :],
                        standard[chunk, :, qq * BLOCK:(qq + 1) * BLOCK],
                        preferred_element_type=jnp.float32,
                    )
                    for p, q in inside:
                        tile = STARTS[d] + PLACES[d].index((2 * pp + p, 2 * qq + q))
                        for half in range(2):
                            top = p * PANEL + half * (PANEL // 2)
                            part[rows_chunk, half, tile] = block[
                                top:top + PANEL // 2, q * PANEL:(q + 1) * PANEL
                            ]
            twin_copy(rows_chunk, number, first, count).start()

    def halves_of(first, count):
        upper = (count + 1) // 2
        return pl.ds(first, upper), pl.ds(first + upper, count - upper)

    def line_copy(rows_chunk, number, halves, half, way, relayed):
        which = halves[half]
        return pltpu.make_async_remote_copy(
            src_ref=part.at[rows_chunk, core, which],
            dst_ref=(relay if relayed else ring).at[way, which],
            send_sem=ring_send.at[rows_chunk, number, half],
            recv_sem=relay_recv.at[way, number] if relayed else ring_recv.at[way, number, half],
            device_id=(group * SIDE + lax.rem(x + 1 + 2 * way, SIDE), core),
            device_id_type=MESH,
        )

    def reduce(step):
        for rows_chunk, d, number, first, count in pieces_of(step):
            which = pl.ds(first, count)
            halves = halves_of(first, count)
            twin_copy(rows_chunk, number, first, count).wait()
            part[rows_chunk, core, which] = part[rows_chunk, core, which] + twin[rows_chunk, which]
            distance = lax.rem(rows_chunk - x + SIDE, SIDE)

            @pl.when(distance == 2)
            def _():
                line_copy(rows_chunk, number, halves, 0, 0, True).start()
                line_copy(rows_chunk, number, halves, 1, 1, True).start()

            @pl.when(distance == 1)
            def _():
                line_copy(rows_chunk, number, halves, 1, 0, False).start()

            @pl.when(distance == 3)
            def _():
                line_copy(rows_chunk, number, halves, 0, 1, False).start()

        pump(3)
        for rows_chunk, d, number, first, count in pieces_of(step):
            halves = halves_of(first, count)
            distance = lax.rem(rows_chunk - x + SIDE, SIDE)
            for way in range(2):

                @pl.when(distance == 1 + 2 * way)
                def _():
                    which = halves[way]
                    line_copy(rows_chunk, number, halves, way, way, True).wait_recv()
                    part[rows_chunk, core, which] = part[rows_chunk, core, which] + relay[way, which]
                    line_copy(rows_chunk, number, halves, way, way, False).start()

    pump(3)
    for step in range(len(SWAPS)):
        own_copy(step).start()
    local_moments()
    copies = group_moments_begin()
    pump(4)
    copies = ring_moments_begin(copies)
    pump(4)
    ring_moments_end(copies)
    for step, swap_step in enumerate(READY):
        if step == READY.index(swap_step):
            pump((swap_step + 1) * (GROUPS - 1) + AHEAD - started[0])
            swap_end(swap_step)
        standardize(step)
        multiply(step)
        pump(2)
        reduce(step)
        pump(2)
    for copy in swaps[-AHEAD:]:
        copy.wait_send()

    for step in range(len(STEPS)):
        for rows_chunk, d, number, first, count in pieces_of(step):
            halves = halves_of(first, count)

            @pl.when(x != rows_chunk)
            def _():
                for half in range(2):
                    line_copy(rows_chunk, number, halves, half, 0, False).wait_send()

            @pl.when(x == rows_chunk)
            def _():
                for way in range(2):
                    for half in range(2):
                        line_copy(rows_chunk, number, halves, half, way, False).wait_recv()

    for d in range(REACH + 1):
        for index, (p, q) in enumerate(PLACES[d]):
            tile = STARTS[d] + index
            out_ref[p, d * OWN + q - p] = part[x, core, tile] + (ring[0, tile] + ring[1, tile])


def tiles(dosages):
    half_tile = (PANEL // 2, PANEL)
    dma = pltpu.SemaphoreType.DMA
    return pl.pallas_call(
        tiles_kernel,
        out_shape=jax.ShapeDtypeStruct((OWN, WMAX + 1) + half_tile, jnp.float32),
        in_specs=[pl.BlockSpec(memory_space=pl.ANY)],
        out_specs=pl.BlockSpec(memory_space=pltpu.VMEM),
        scratch_shapes=[
            pltpu.VMEM((GROUPS * SIDE, ROWS, CHUNK), jnp.bfloat16),
            pltpu.VMEM((CHUNKS, GROUPS, ROWS, CHUNK), jnp.bfloat16),
            pltpu.VMEM((GROUPS * SIDE + REACH, 2 * OWN, PANEL), jnp.float32),
            pltpu.VMEM((GROUPS, CHUNKS, 2 * OWN, PANEL), jnp.float32),
            pltpu.VMEM((8, CHUNKS, 2 * OWN, PANEL), jnp.float32),
            pltpu.VMEM((CHUNKS, 2 * OWN, PANEL), jnp.float32),
            pltpu.VMEM((CHUNKS, LOCAL, CHUNK), jnp.bfloat16),
            pltpu.VMEM((SIDE, CHUNK, LOCAL), jnp.bfloat16),
            pltpu.VMEM((SIDE, 2, TILES) + half_tile, jnp.float32),
            pltpu.VMEM((SIDE, TILES) + half_tile, jnp.float32),
            pltpu.VMEM((2, TILES) + half_tile, jnp.float32),
            pltpu.VMEM((2, TILES) + half_tile, jnp.float32),
            dma((GROUPS * SIDE,)),
            dma((len(SWAPS),)),
            dma((len(SWAPS), GROUPS)),
            dma((len(SWAPS), GROUPS)),
            dma((GROUPS,)),
            dma((GROUPS,)),
            dma((7,)),
            dma((7,)),
            dma((SIDE, REACH + 2)),
            dma((SIDE, REACH + 2)),
            dma((2, REACH + 2)),
            dma((SIDE, REACH + 2, 2)),
            dma((2, REACH + 2, 2)),
        ],
        compiler_params=pltpu.CompilerParams(
            collective_id=0, has_side_effects=True, vmem_limit_bytes=60 * 1024 * 1024
        ),
        name="tiles",
    )(dosages)


def per_device(dosages, band_width):
    band_tiles = tiles(dosages)
    offsets = jnp.arange(WMAX + 1, dtype=jnp.int32)
    panel_count = OWN * lax.axis_size("var")
    global_panel = lax.axis_index("var") * OWN + jnp.arange(OWN, dtype=jnp.int32)
    in_band = (offsets[None, :] <= band_width[:, None]) & (
        global_panel[:, None] + offsets[None, :] < panel_count
    )
    return jnp.where(in_band[:, :, None, None], band_tiles * (1.0 / SAMPLES), 0.0)


def solution(mesh):
    in_specs = (P(("var", "samp"), None), P("var"))
    out_specs = P("var", None, "samp", None)
    return jax.shard_map(
        per_device, mesh=mesh, in_specs=in_specs, out_specs=out_specs, check_vma=False
    )
```

```python
import jax
import jax.numpy as jnp
from jax import lax
from jax.experimental import pallas as pl
from jax.experimental.pallas import tpu as pltpu
from jax.sharding import PartitionSpec as P

MESH = pl.DeviceIdType.MESH
WMAX = 8
PANEL = 128
SIDE = 4
GROUPS = SIDE * SIDE
OWN = 4
CHUNK = OWN * PANEL
REACH = WMAX // OWN
CHUNKS = SIDE + REACH
ROWS = 64
LOCAL = GROUPS * ROWS
BLOCK = 2 * PANEL
STEPS = [(chunk, 0, CHUNK) for chunk in range(CHUNKS - 1)] + [(CHUNKS - 1, first, BLOCK) for first in (0, BLOCK)]
AHEAD = 15
ORDER = [10, 15, 1, 4, 6, 3, 9, 12, 11, 14, 7, 13, 2, 8, 5]
SAMPLES = 8192
PLACES = [
    [(p, q) for q in range(OWN) for p in range(OWN) if 0 <= d * OWN + q - p <= WMAX] for d in range(REACH + 1)
]
STARTS = [sum(len(places) for places in PLACES[:d]) for d in range(REACH + 2)]
TILES = STARTS[-1]


def position():
    var = lax.axis_index("var")
    return var // SIDE, lax.rem(var, SIDE), lax.axis_index("samp")


def tiles_kernel(
    dos_ref, out_ref, staged, received, moments, gathered, sums, totals, standard, turned, part, twin, relay, ring,
    stage_sem, own_sem, swap_send, swap_recv, group_send, group_recv, stat_send, stat_recv, twin_send, twin_recv, relay_recv, ring_send, ring_recv,
):
    group, x, core = position()
    z, y = group // SIDE, lax.rem(group, SIDE)

    def stage(index):
        first = pl.multiple_of(index * CHUNK, CHUNK)
        return pltpu.make_async_copy(dos_ref.at[:, pl.ds(first, CHUNK)], staged.at[index], stage_sem.at[index])

    def stage_begin(index, carry):
        stage(index).start()
        return carry

    def stage_end(index, carry):
        stage(index).wait()
        return carry

    lax.fori_loop(0, GROUPS * SIDE, stage_begin, 0)

    peers = []
    for dx in range(SIDE):
        for dc in range(2):
            if dx or dc:
                peer_x, peer_c = lax.rem(x + dx, SIDE), lax.rem(core + dc, 2)
                peers.append((group * SIDE + peer_x, peer_c))

    def group_at(offset):
        return lax.rem(z + offset // SIDE, SIDE) * SIDE + lax.rem(y + offset % SIDE, SIDE)

    barrier = pltpu.get_barrier_semaphore()
    for offset in range(1, GROUPS):
        pl.semaphore_signal(
            barrier, inc=1, device_id=(group_at(offset) * SIDE + x, core), device_id_type=MESH
        )
    for peer in peers:
        pl.semaphore_signal(barrier, inc=1, device_id=peer, device_id_type=MESH)
    lax.fori_loop(0, GROUPS * SIDE, stage_end, 0)
    pl.semaphore_wait(barrier, GROUPS - 1 + len(peers))

    def swap(index):
        step, turn = divmod(index, GROUPS - 1)
        chunk, first, count = STEPS[step]
        columns = pl.ds(first, count)
        offset = ORDER[turn]
        other = group_at(offset)
        return pltpu.make_async_remote_copy(
            src_ref=staged.at[lax.rem(other * SIDE + chunk, GROUPS * SIDE), :, columns],
            dst_ref=received.at[chunk, offset, :, columns],
            send_sem=swap_send.at[step, offset],
            recv_sem=swap_recv.at[step, offset],
            device_id=(other * SIDE + x, core),
            device_id_type=MESH,
        )

    swaps = [swap(index) for index in range(len(STEPS) * (GROUPS - 1))]
    started = [0]

    def pump(count):
        for index in range(started[0], min(started[0] + count, len(swaps))):
            if index >= AHEAD:
                swaps[index - AHEAD].wait_send()
            swaps[index].start()
            started[0] = index + 1

    def own_copy(step):
        chunk, first, count = STEPS[step]
        columns = pl.ds(first, count)
        return pltpu.make_async_copy(
            staged.at[lax.rem(group * SIDE + chunk, GROUPS * SIDE), :, columns],
            received.at[chunk, 0, :, columns],
            own_sem.at[step],
        )

    def swap_end(step):
        own_copy(step).wait()
        for copy in swaps[step * (GROUPS - 1):(step + 1) * (GROUPS - 1)]:
            copy.wait_recv()

    def local_moments():
        def chunk_moments(index, carry):
            values = staged[index].astype(jnp.float32).reshape(ROWS // 8, 8, CHUNK)
            for row, total in enumerate((jnp.sum(values, 0), jnp.sum(values * values, 0))):
                total = jnp.sum(total, 0, keepdims=True)
                for q in range(OWN):
                    moments[index, row * OWN + q:row * OWN + q + 1, :] = total[:, q * PANEL:(q + 1) * PANEL]
            return carry

        lax.fori_loop(0, GROUPS * SIDE, chunk_moments, 0)
        for extra in range(REACH):
            moments[GROUPS * SIDE + extra] = moments[extra]

    def group_moments_begin():
        gathered[0] = moments[pl.ds(group * SIDE, CHUNKS)]
        copies = []
        for offset in range(1, GROUPS):
            other = group_at(offset)
            copy = pltpu.make_async_remote_copy(
                src_ref=moments.at[pl.ds(other * SIDE, CHUNKS)],
                dst_ref=gathered.at[offset],
                send_sem=group_send.at[offset],
                recv_sem=group_recv.at[offset],
                device_id=(other * SIDE + x, core),
                device_id_type=MESH,
            )
            copy.start()
            copies.append(copy)
        return copies

    def ring_moments_begin(copies):
        for copy in copies:
            copy.wait()
        sums[0] = jnp.sum(gathered[...], 0)
        copies = []
        for index, peer in enumerate(peers):
            copy = pltpu.make_async_remote_copy(
                src_ref=sums.at[0],
                dst_ref=sums.at[index + 1],
                send_sem=stat_send.at[index],
                recv_sem=stat_recv.at[index],
                device_id=peer,
                device_id_type=MESH,
            )
            copy.start()
            copies.append(copy)
        return copies

    def ring_moments_end(copies):
        for copy in copies:
            copy.wait()
        totals[...] = jnp.sum(sums[...], 0)

    def standardize(step):
        chunk, start, count = STEPS[step]
        columns = pl.ds(start, count)
        panels = range(start // PANEL, (start + count) // PANEL)
        first, second = totals[chunk, 0:OWN], totals[chunk, OWN:2 * OWN]
        mean = first * (1.0 / SAMPLES)
        inv_scale = lax.rsqrt(second * (1.0 / SAMPLES) - mean * mean + 1e-05)
        mean = jnp.concatenate([mean[q:q + 1] for q in panels], axis=1)
        inv_scale = jnp.concatenate([inv_scale[q:q + 1] for q in panels], axis=1)

        def block_standard(block, carry):
            rows = pl.ds(pl.multiple_of(block * ROWS, ROWS), ROWS)
            values = received[chunk, block, :, columns].astype(jnp.float32)
            standard[chunk, rows, columns] = ((values - mean) * inv_scale).astype(jnp.bfloat16)
            return carry

        lax.fori_loop(0, GROUPS, block_standard, 0)
        if chunk < SIDE:
            turned[chunk] = standard[chunk].T

    def pieces_of(step):
        chunk, start, count = STEPS[step]
        pieces = []
        for d in range(REACH + 1):
            if 0 <= chunk - d < SIDE:
                inside = [
                    index for index, (p, q) in enumerate(PLACES[d])
                    if start // PANEL <= q < (start + count) // PANEL
                ]
                pieces.append((chunk - d, d, d + (start > 0), STARTS[d] + inside[0], len(inside)))
        return pieces

    def twin_copy(rows_chunk, number, first, count):
        which = pl.ds(first, count)
        return pltpu.make_async_remote_copy(
            src_ref=part.at[rows_chunk, 1 - core, which],
            dst_ref=twin.at[rows_chunk, which],
            send_sem=twin_send.at[rows_chunk, number],
            recv_sem=twin_recv.at[rows_chunk, number],
            device_id=(group * SIDE + x, 1 - core),
            device_id_type=MESH,
        )

    def multiply(step):
        chunk, start, columns = STEPS[step]
        for rows_chunk, d, number, first, count in pieces_of(step):
            for pp in range(OWN // 2):
                for qq in range(start // BLOCK, (start + columns) // BLOCK):
                    inside = [
                        (p, q) for p in range(2) for q in range(2) if (2 * pp + p, 2 * qq + q) in PLACES[d]
                    ]
                    if not inside:
                        continue
                    block = jnp.dot(
                        turned[rows_chunk, pp * BLOCK:(pp + 1) * BLOCK, :],
                        standard[chunk, :, qq * BLOCK:(qq + 1) * BLOCK],
                        preferred_element_type=jnp.float32,
                    )
                    for p, q in inside:
                        tile = STARTS[d] + PLACES[d].index((2 * pp + p, 2 * qq + q))
                        for half in range(2):
                            top = p * PANEL + half * (PANEL // 2)
                            part[rows_chunk, half, tile] = block[
                                top:top + PANEL // 2, q * PANEL:(q + 1) * PANEL
                            ]
            twin_copy(rows_chunk, number, first, count).start()

    def halves_of(first, count):
        upper = (count + 1) // 2
        return pl.ds(first, upper), pl.ds(first + upper, count - upper)

    def line_copy(rows_chunk, number, halves, half, way, relayed):
        which = halves[half]
        return pltpu.make_async_remote_copy(
            src_ref=part.at[rows_chunk, core, which],
            dst_ref=(relay if relayed else ring).at[way, which],
            send_sem=ring_send.at[rows_chunk, number, half],
            recv_sem=relay_recv.at[way, number] if relayed else ring_recv.at[way, number, half],
            device_id=(group * SIDE + lax.rem(x + 1 + 2 * way, SIDE), core),
            device_id_type=MESH,
        )

    def reduce(step):
        for rows_chunk, d, number, first, count in pieces_of(step):
            which = pl.ds(first, count)
            halves = halves_of(first, count)
            twin_copy(rows_chunk, number, first, count).wait()
            part[rows_chunk, core, which] = part[rows_chunk, core, which] + twin[rows_chunk, which]
            distance = lax.rem(rows_chunk - x + SIDE, SIDE)

            @pl.when(distance == 2)
            def _():
                line_copy(rows_chunk, number, halves, 0, 0, True).start()
                line_copy(rows_chunk, number, halves, 1, 1, True).start()

            @pl.when(distance == 1)
            def _():
                line_copy(rows_chunk, number, halves, 1, 0, False).start()

            @pl.when(distance == 3)
            def _():
                line_copy(rows_chunk, number, halves, 0, 1, False).start()

        pump(5)
        for rows_chunk, d, number, first, count in pieces_of(step):
            halves = halves_of(first, count)
            distance = lax.rem(rows_chunk - x + SIDE, SIDE)
            for way in range(2):

                @pl.when(distance == 1 + 2 * way)
                def _():
                    which = halves[way]
                    line_copy(rows_chunk, number, halves, way, way, True).wait_recv()
                    part[rows_chunk, core, which] = part[rows_chunk, core, which] + relay[way, which]
                    line_copy(rows_chunk, number, halves, way, way, False).start()

    pump(8)
    for step in range(len(STEPS)):
        own_copy(step).start()
    local_moments()
    copies = group_moments_begin()
    pump(8)
    copies = ring_moments_begin(copies)
    pump(8)
    ring_moments_end(copies)
    for step in range(len(STEPS)):
        pump((step + 1) * (GROUPS - 1) + AHEAD - started[0])
        swap_end(step)
        standardize(step)
        multiply(step)
        pump(3)
        reduce(step)
        pump(3)
    for copy in swaps[-AHEAD:]:
        copy.wait_send()

    for step in range(len(STEPS)):
        for rows_chunk, d, number, first, count in pieces_of(step):
            halves = halves_of(first, count)

            @pl.when(x != rows_chunk)
            def _():
                for half in range(2):
                    line_copy(rows_chunk, number, halves, half, 0, False).wait_send()

            @pl.when(x == rows_chunk)
            def _():
                for way in range(2):
                    for half in range(2):
                        line_copy(rows_chunk, number, halves, half, way, False).wait_recv()

    for d in range(REACH + 1):
        for index, (p, q) in enumerate(PLACES[d]):
            tile = STARTS[d] + index
            out_ref[p, d * OWN + q - p] = part[x, core, tile] + (ring[0, tile] + ring[1, tile])


def tiles(dosages):
    half_tile = (PANEL // 2, PANEL)
    dma = pltpu.SemaphoreType.DMA
    return pl.pallas_call(
        tiles_kernel,
        out_shape=jax.ShapeDtypeStruct((OWN, WMAX + 1) + half_tile, jnp.float32),
        in_specs=[pl.BlockSpec(memory_space=pl.ANY)],
        out_specs=pl.BlockSpec(memory_space=pltpu.VMEM),
        scratch_shapes=[
            pltpu.VMEM((GROUPS * SIDE, ROWS, CHUNK), jnp.bfloat16),
            pltpu.VMEM((CHUNKS, GROUPS, ROWS, CHUNK), jnp.bfloat16),
            pltpu.VMEM((GROUPS * SIDE + REACH, 2 * OWN, PANEL), jnp.float32),
            pltpu.VMEM((GROUPS, CHUNKS, 2 * OWN, PANEL), jnp.float32),
            pltpu.VMEM((8, CHUNKS, 2 * OWN, PANEL), jnp.float32),
            pltpu.VMEM((CHUNKS, 2 * OWN, PANEL), jnp.float32),
            pltpu.VMEM((CHUNKS, LOCAL, CHUNK), jnp.bfloat16),
            pltpu.VMEM((SIDE, CHUNK, LOCAL), jnp.bfloat16),
            pltpu.VMEM((SIDE, 2, TILES) + half_tile, jnp.float32),
            pltpu.VMEM((SIDE, TILES) + half_tile, jnp.float32),
            pltpu.VMEM((2, TILES) + half_tile, jnp.float32),
            pltpu.VMEM((2, TILES) + half_tile, jnp.float32),
            dma((GROUPS * SIDE,)),
            dma((len(STEPS),)),
            dma((len(STEPS), GROUPS)),
            dma((len(STEPS), GROUPS)),
            dma((GROUPS,)),
            dma((GROUPS,)),
            dma((7,)),
            dma((7,)),
            dma((SIDE, REACH + 2)),
            dma((SIDE, REACH + 2)),
            dma((2, REACH + 2)),
            dma((SIDE, REACH + 2, 2)),
            dma((2, REACH + 2, 2)),
        ],
        compiler_params=pltpu.CompilerParams(
            collective_id=0, has_side_effects=True, vmem_limit_bytes=60 * 1024 * 1024
        ),
        name="tiles",
    )(dosages)


def per_device(dosages, band_width):
    band_tiles = tiles(dosages)
    offsets = jnp.arange(WMAX + 1, dtype=jnp.int32)
    panel_count = OWN * lax.axis_size("var")
    global_panel = lax.axis_index("var") * OWN + jnp.arange(OWN, dtype=jnp.int32)
    in_band = (offsets[None, :] <= band_width[:, None]) & (
        global_panel[:, None] + offsets[None, :] < panel_count
    )
    return jnp.where(in_band[:, :, None, None], band_tiles * (1.0 / SAMPLES), 0.0)


def solution(mesh):
    in_specs = (P(("var", "samp"), None), P("var"))
    out_specs = P("var", None, "samp", None)
    return jax.shard_map(
        per_device, mesh=mesh, in_specs=in_specs, out_specs=out_specs, check_vma=False
    )
```

```python
import jax
import jax.numpy as jnp
from jax import lax
from jax.experimental import pallas as pl
from jax.experimental.pallas import tpu as pltpu
from jax.sharding import PartitionSpec as P

MESH = pl.DeviceIdType.MESH
WMAX = 8
PANEL = 128
SIDE = 4
GROUPS = SIDE * SIDE
OWN = 4
CHUNK = OWN * PANEL
REACH = WMAX // OWN
CHUNKS = SIDE + REACH
ROWS = 64
LOCAL = GROUPS * ROWS
BLOCK = 2 * PANEL
STEPS = [(chunk, 0, CHUNK) for chunk in range(CHUNKS - 1)] + [(CHUNKS - 1, first, BLOCK) for first in (0, BLOCK)]
AHEAD = 15
ORDER = [10, 15, 1, 4, 6, 3, 9, 12, 11, 14, 7, 13, 2, 8, 5]
SAMPLES = 8192
PLACES = [
    [(p, q) for q in range(OWN) for p in range(OWN) if 0 <= d * OWN + q - p <= WMAX] for d in range(REACH + 1)
]
STARTS = [sum(len(places) for places in PLACES[:d]) for d in range(REACH + 2)]
TILES = STARTS[-1]


def position():
    var = lax.axis_index("var")
    return var // SIDE, lax.rem(var, SIDE), lax.axis_index("samp")


def tiles_kernel(
    dos_ref, out_ref, staged, received, moments, gathered, sums, totals, standard, turned, part, twin, relay, ring,
    stage_sem, own_sem, swap_send, swap_recv, group_send, group_recv, stat_send, stat_recv, twin_send, twin_recv, relay_recv, ring_send, ring_recv,
):
    group, x, core = position()
    z, y = group // SIDE, lax.rem(group, SIDE)

    def stage(index):
        first = pl.multiple_of(index * CHUNK, CHUNK)
        return pltpu.make_async_copy(dos_ref.at[:, pl.ds(first, CHUNK)], staged.at[index], stage_sem.at[index])

    def stage_begin(index, carry):
        stage(index).start()
        return carry

    def stage_end(index, carry):
        stage(index).wait()
        return carry

    lax.fori_loop(0, GROUPS * SIDE, stage_begin, 0)

    peers = []
    for dx in range(SIDE):
        for dc in range(2):
            if dx or dc:
                peer_x, peer_c = lax.rem(x + dx, SIDE), lax.rem(core + dc, 2)
                peers.append((group * SIDE + peer_x, peer_c))

    def group_at(offset):
        return lax.rem(z + offset // SIDE, SIDE) * SIDE + lax.rem(y + offset % SIDE, SIDE)

    barrier = pltpu.get_barrier_semaphore()
    for offset in range(1, GROUPS):
        pl.semaphore_signal(
            barrier, inc=1, device_id=(group_at(offset) * SIDE + x, core), device_id_type=MESH
        )
    for peer in peers:
        pl.semaphore_signal(barrier, inc=1, device_id=peer, device_id_type=MESH)
    pl.semaphore_wait(barrier, GROUPS - 1 + len(peers))

    def columns_of(other, chunk, first, count):
        top = lax.rem(other * SIDE + chunk, GROUPS * SIDE) * CHUNK + first
        return dos_ref.at[:, pl.ds(pl.multiple_of(top, BLOCK), count)]

    def swap(index):
        step, turn = divmod(index, GROUPS - 1)
        chunk, first, count = STEPS[step]
        columns = pl.ds(first, count)
        offset = ORDER[turn]
        other = group_at(offset)
        return pltpu.make_async_remote_copy(
            src_ref=columns_of(other, chunk, first, count),
            dst_ref=received.at[chunk, offset, :, columns],
            send_sem=swap_send.at[step, offset],
            recv_sem=swap_recv.at[step, offset],
            device_id=(other * SIDE + x, core),
            device_id_type=MESH,
        )

    swaps = [swap(index) for index in range(len(STEPS) * (GROUPS - 1))]
    started = [0]

    def pump(count):
        for index in range(started[0], min(started[0] + count, len(swaps))):
            if index >= AHEAD:
                swaps[index - AHEAD].wait_send()
            swaps[index].start()
            started[0] = index + 1

    def own_copy(step):
        chunk, first, count = STEPS[step]
        columns = pl.ds(first, count)
        return pltpu.make_async_copy(
            columns_of(group, chunk, first, count),
            received.at[chunk, 0, :, columns],
            own_sem.at[step],
        )

    def swap_end(step):
        own_copy(step).wait()
        for copy in swaps[step * (GROUPS - 1):(step + 1) * (GROUPS - 1)]:
            copy.wait_recv()

    def local_moments():
        def chunk_moments(index, carry):
            values = staged[index].astype(jnp.float32).reshape(ROWS // 8, 8, CHUNK)
            for row, total in enumerate((jnp.sum(values, 0), jnp.sum(values * values, 0))):
                total = jnp.sum(total, 0, keepdims=True)
                for q in range(OWN):
                    moments[index, row * OWN + q:row * OWN + q + 1, :] = total[:, q * PANEL:(q + 1) * PANEL]
            return carry

        lax.fori_loop(0, GROUPS * SIDE, chunk_moments, 0)
        for extra in range(REACH):
            moments[GROUPS * SIDE + extra] = moments[extra]

    def group_moments_begin():
        gathered[0] = moments[pl.ds(group * SIDE, CHUNKS)]
        copies = []
        for offset in range(1, GROUPS):
            other = group_at(offset)
            copy = pltpu.make_async_remote_copy(
                src_ref=moments.at[pl.ds(other * SIDE, CHUNKS)],
                dst_ref=gathered.at[offset],
                send_sem=group_send.at[offset],
                recv_sem=group_recv.at[offset],
                device_id=(other * SIDE + x, core),
                device_id_type=MESH,
            )
            copy.start()
            copies.append(copy)
        return copies

    def ring_moments_begin(copies):
        for copy in copies:
            copy.wait()
        sums[0] = jnp.sum(gathered[...], 0)
        copies = []
        for index, peer in enumerate(peers):
            copy = pltpu.make_async_remote_copy(
                src_ref=sums.at[0],
                dst_ref=sums.at[index + 1],
                send_sem=stat_send.at[index],
                recv_sem=stat_recv.at[index],
                device_id=peer,
                device_id_type=MESH,
            )
            copy.start()
            copies.append(copy)
        return copies

    def ring_moments_end(copies):
        for copy in copies:
            copy.wait()
        totals[...] = jnp.sum(sums[...], 0)

    def standardize(step):
        chunk, start, count = STEPS[step]
        columns = pl.ds(start, count)
        panels = range(start // PANEL, (start + count) // PANEL)
        first, second = totals[chunk, 0:OWN], totals[chunk, OWN:2 * OWN]
        mean = first * (1.0 / SAMPLES)
        inv_scale = lax.rsqrt(second * (1.0 / SAMPLES) - mean * mean + 1e-05)
        mean = jnp.concatenate([mean[q:q + 1] for q in panels], axis=1)
        inv_scale = jnp.concatenate([inv_scale[q:q + 1] for q in panels], axis=1)

        def block_standard(block, carry):
            rows = pl.ds(pl.multiple_of(block * ROWS, ROWS), ROWS)
            values = received[chunk, block, :, columns].astype(jnp.float32)
            standard[chunk, rows, columns] = ((values - mean) * inv_scale).astype(jnp.bfloat16)
            return carry

        lax.fori_loop(0, GROUPS, block_standard, 0)
        if chunk < SIDE:
            turned[chunk] = standard[chunk].T

    def pieces_of(step):
        chunk, start, count = STEPS[step]
        pieces = []
        for d in range(REACH + 1):
            if 0 <= chunk - d < SIDE:
                inside = [
                    index for index, (p, q) in enumerate(PLACES[d])
                    if start // PANEL <= q < (start + count) // PANEL
                ]
                pieces.append((chunk - d, d, d + (start > 0), STARTS[d] + inside[0], len(inside)))
        return pieces

    def twin_copy(rows_chunk, number, first, count):
        which = pl.ds(first, count)
        return pltpu.make_async_remote_copy(
            src_ref=part.at[rows_chunk, 1 - core, which],
            dst_ref=twin.at[rows_chunk, which],
            send_sem=twin_send.at[rows_chunk, number],
            recv_sem=twin_recv.at[rows_chunk, number],
            device_id=(group * SIDE + x, 1 - core),
            device_id_type=MESH,
        )

    def multiply(step):
        chunk, start, columns = STEPS[step]
        for rows_chunk, d, number, first, count in pieces_of(step):
            for pp in range(OWN // 2):
                for qq in range(start // BLOCK, (start + columns) // BLOCK):
                    inside = [
                        (p, q) for p in range(2) for q in range(2) if (2 * pp + p, 2 * qq + q) in PLACES[d]
                    ]
                    if not inside:
                        continue
                    block = jnp.dot(
                        turned[rows_chunk, pp * BLOCK:(pp + 1) * BLOCK, :],
                        standard[chunk, :, qq * BLOCK:(qq + 1) * BLOCK],
                        preferred_element_type=jnp.float32,
                    )
                    for p, q in inside:
                        tile = STARTS[d] + PLACES[d].index((2 * pp + p, 2 * qq + q))
                        for half in range(2):
                            top = p * PANEL + half * (PANEL // 2)
                            part[rows_chunk, half, tile] = block[
                                top:top + PANEL // 2, q * PANEL:(q + 1) * PANEL
                            ]
            twin_copy(rows_chunk, number, first, count).start()

    def halves_of(first, count):
        upper = (count + 1) // 2
        return pl.ds(first, upper), pl.ds(first + upper, count - upper)

    def line_copy(rows_chunk, number, halves, half, way, relayed):
        which = halves[half]
        return pltpu.make_async_remote_copy(
            src_ref=part.at[rows_chunk, core, which],
            dst_ref=(relay if relayed else ring).at[way, which],
            send_sem=ring_send.at[rows_chunk, number, half],
            recv_sem=relay_recv.at[way, number] if relayed else ring_recv.at[way, number, half],
            device_id=(group * SIDE + lax.rem(x + 1 + 2 * way, SIDE), core),
            device_id_type=MESH,
        )

    def reduce(step):
        for rows_chunk, d, number, first, count in pieces_of(step):
            which = pl.ds(first, count)
            halves = halves_of(first, count)
            twin_copy(rows_chunk, number, first, count).wait()
            part[rows_chunk, core, which] = part[rows_chunk, core, which] + twin[rows_chunk, which]
            distance = lax.rem(rows_chunk - x + SIDE, SIDE)

            @pl.when(distance == 2)
            def _():
                line_copy(rows_chunk, number, halves, 0, 0, True).start()
                line_copy(rows_chunk, number, halves, 1, 1, True).start()

            @pl.when(distance == 1)
            def _():
                line_copy(rows_chunk, number, halves, 1, 0, False).start()

            @pl.when(distance == 3)
            def _():
                line_copy(rows_chunk, number, halves, 0, 1, False).start()

            pump(4)

        pump(3)
        for rows_chunk, d, number, first, count in pieces_of(step):
            halves = halves_of(first, count)
            distance = lax.rem(rows_chunk - x + SIDE, SIDE)
            for way in range(2):

                @pl.when(distance == 1 + 2 * way)
                def _():
                    which = halves[way]
                    line_copy(rows_chunk, number, halves, way, way, True).wait_recv()
                    part[rows_chunk, core, which] = part[rows_chunk, core, which] + relay[way, which]
                    line_copy(rows_chunk, number, halves, way, way, False).start()

    pump(8)
    for step in range(len(STEPS)):
        own_copy(step).start()
    lax.fori_loop(0, GROUPS * SIDE, stage_end, 0)
    local_moments()
    copies = group_moments_begin()
    pump(8)
    copies = ring_moments_begin(copies)
    pump(8)
    ring_moments_end(copies)
    for step in range(len(STEPS)):
        pump((step + 1) * (GROUPS - 1) + AHEAD - started[0])
        swap_end(step)
        standardize(step)
        multiply(step)
        pump(2)
        reduce(step)
    for copy in swaps[-AHEAD:]:
        copy.wait_send()

    for step in range(len(STEPS)):
        for rows_chunk, d, number, first, count in pieces_of(step):
            halves = halves_of(first, count)

            @pl.when(x != rows_chunk)
            def _():
                for half in range(2):
                    line_copy(rows_chunk, number, halves, half, 0, False).wait_send()

            @pl.when(x == rows_chunk)
            def _():
                for way in range(2):
                    for half in range(2):
                        line_copy(rows_chunk, number, halves, half, way, False).wait_recv()

    for d in range(REACH + 1):
        for index, (p, q) in enumerate(PLACES[d]):
            tile = STARTS[d] + index
            out_ref[p, d * OWN + q - p] = part[x, core, tile] + (ring[0, tile] + ring[1, tile])


def tiles(dosages):
    half_tile = (PANEL // 2, PANEL)
    dma = pltpu.SemaphoreType.DMA
    return pl.pallas_call(
        tiles_kernel,
        out_shape=jax.ShapeDtypeStruct((OWN, WMAX + 1) + half_tile, jnp.float32),
        in_specs=[pl.BlockSpec(memory_space=pl.ANY)],
        out_specs=pl.BlockSpec(memory_space=pltpu.VMEM),
        scratch_shapes=[
            pltpu.VMEM((GROUPS * SIDE, ROWS, CHUNK), jnp.bfloat16),
            pltpu.VMEM((CHUNKS, GROUPS, ROWS, CHUNK), jnp.bfloat16),
            pltpu.VMEM((GROUPS * SIDE + REACH, 2 * OWN, PANEL), jnp.float32),
            pltpu.VMEM((GROUPS, CHUNKS, 2 * OWN, PANEL), jnp.float32),
            pltpu.VMEM((8, CHUNKS, 2 * OWN, PANEL), jnp.float32),
            pltpu.VMEM((CHUNKS, 2 * OWN, PANEL), jnp.float32),
            pltpu.VMEM((CHUNKS, LOCAL, CHUNK), jnp.bfloat16),
            pltpu.VMEM((SIDE, CHUNK, LOCAL), jnp.bfloat16),
            pltpu.VMEM((SIDE, 2, TILES) + half_tile, jnp.float32),
            pltpu.VMEM((SIDE, TILES) + half_tile, jnp.float32),
            pltpu.VMEM((2, TILES) + half_tile, jnp.float32),
            pltpu.VMEM((2, TILES) + half_tile, jnp.float32),
            dma((GROUPS * SIDE,)),
            dma((len(STEPS),)),
            dma((len(STEPS), GROUPS)),
            dma((len(STEPS), GROUPS)),
            dma((GROUPS,)),
            dma((GROUPS,)),
            dma((7,)),
            dma((7,)),
            dma((SIDE, REACH + 2)),
            dma((SIDE, REACH + 2)),
            dma((2, REACH + 2)),
            dma((SIDE, REACH + 2, 2)),
            dma((2, REACH + 2, 2)),
        ],
        compiler_params=pltpu.CompilerParams(
            collective_id=0, has_side_effects=True, vmem_limit_bytes=60 * 1024 * 1024
        ),
        name="tiles",
    )(dosages)


def per_device(dosages, band_width):
    band_tiles = tiles(dosages)
    offsets = jnp.arange(WMAX + 1, dtype=jnp.int32)
    panel_count = OWN * lax.axis_size("var")
    global_panel = lax.axis_index("var") * OWN + jnp.arange(OWN, dtype=jnp.int32)
    in_band = (offsets[None, :] <= band_width[:, None]) & (
        global_panel[:, None] + offsets[None, :] < panel_count
    )
    return jnp.where(in_band[:, :, None, None], band_tiles * (1.0 / SAMPLES), 0.0)


def solution(mesh):
    in_specs = (P(("var", "samp"), None), P("var"))
    out_specs = P("var", None, "samp", None)
    return jax.shard_map(
        per_device, mesh=mesh, in_specs=in_specs, out_specs=out_specs, check_vma=False
    )
```

```python
import jax
import jax.numpy as jnp
from jax import lax
from jax.experimental import pallas as pl
from jax.experimental.pallas import tpu as pltpu
from jax.sharding import PartitionSpec as P

MESH = pl.DeviceIdType.MESH
WMAX = 8
PANEL = 128
SIDE = 4
GROUPS = SIDE * SIDE
OWN = 4
CHUNK = OWN * PANEL
REACH = WMAX // OWN
CHUNKS = SIDE + REACH
ROWS = 64
LOCAL = GROUPS * ROWS
BLOCK = 2 * PANEL
STEPS = [(chunk, 0, CHUNK) for chunk in range(CHUNKS - 1)] + [(CHUNKS - 1, first, BLOCK) for first in (0, BLOCK)]
AHEAD = 24
ORDER = [10, 15, 1, 4, 6, 3, 9, 12, 11, 14, 7, 13, 2, 8, 5]
SAMPLES = 8192
PLACES = [
    [(p, q) for q in range(OWN) for p in range(OWN) if 0 <= d * OWN + q - p <= WMAX] for d in range(REACH + 1)
]
STARTS = [sum(len(places) for places in PLACES[:d]) for d in range(REACH + 2)]
TILES = STARTS[-1]


def position():
    var = lax.axis_index("var")
    return var // SIDE, lax.rem(var, SIDE), lax.axis_index("samp")


def tiles_kernel(
    dos_ref, out_ref, staged, received, moments, gathered, sums, totals, standard, turned, part, twin, relay, ring,
    stage_sem, own_sem, swap_send, swap_recv, group_send, group_recv, stat_send, stat_recv, twin_send, twin_recv, relay_recv, ring_send, ring_recv,
):
    group, x, core = position()
    z, y = group // SIDE, lax.rem(group, SIDE)

    def stage(index):
        first = pl.multiple_of(index * CHUNK, CHUNK)
        return pltpu.make_async_copy(dos_ref.at[:, pl.ds(first, CHUNK)], staged.at[index], stage_sem.at[index])

    def stage_begin(index, carry):
        stage(index).start()
        return carry

    def stage_end(index, carry):
        stage(index).wait()
        return carry

    lax.fori_loop(0, GROUPS * SIDE, stage_begin, 0)

    peers = []
    for dx in range(SIDE):
        for dc in range(2):
            if dx or dc:
                peer_x, peer_c = lax.rem(x + dx, SIDE), lax.rem(core + dc, 2)
                peers.append((group * SIDE + peer_x, peer_c))

    def group_at(offset):
        return lax.rem(z + offset // SIDE, SIDE) * SIDE + lax.rem(y + offset % SIDE, SIDE)

    barrier = pltpu.get_barrier_semaphore()
    for offset in range(1, GROUPS):
        pl.semaphore_signal(
            barrier, inc=1, device_id=(group_at(offset) * SIDE + x, core), device_id_type=MESH
        )
    for peer in peers:
        pl.semaphore_signal(barrier, inc=1, device_id=peer, device_id_type=MESH)
    pl.semaphore_wait(barrier, GROUPS - 1 + len(peers))

    def columns_of(other, chunk, first, count):
        top = lax.rem(other * SIDE + chunk, GROUPS * SIDE) * CHUNK + first
        return dos_ref.at[:, pl.ds(pl.multiple_of(top, BLOCK), count)]

    def swap(index):
        step, turn = divmod(index, GROUPS - 1)
        chunk, first, count = STEPS[step]
        columns = pl.ds(first, count)
        offset = ORDER[turn]
        other = group_at(offset)
        return pltpu.make_async_remote_copy(
            src_ref=columns_of(other, chunk, first, count),
            dst_ref=received.at[chunk, offset, :, columns],
            send_sem=swap_send.at[step, offset],
            recv_sem=swap_recv.at[step, offset],
            device_id=(other * SIDE + x, core),
            device_id_type=MESH,
        )

    swaps = [swap(index) for index in range(len(STEPS) * (GROUPS - 1))]
    started = [0]

    def pump(count):
        for index in range(started[0], min(started[0] + count, len(swaps))):
            if index >= AHEAD:
                swaps[index - AHEAD].wait_send()
            swaps[index].start()
            started[0] = index + 1

    def own_copy(step):
        chunk, first, count = STEPS[step]
        columns = pl.ds(first, count)
        return pltpu.make_async_copy(
            columns_of(group, chunk, first, count),
            received.at[chunk, 0, :, columns],
            own_sem.at[step],
        )

    def swap_end(step):
        own_copy(step).wait()
        for copy in swaps[step * (GROUPS - 1):(step + 1) * (GROUPS - 1)]:
            copy.wait_recv()

    def local_moments():
        def chunk_moments(index, carry):
            values = staged[index].astype(jnp.float32).reshape(ROWS // 8, 8, CHUNK)
            for row, total in enumerate((jnp.sum(values, 0), jnp.sum(values * values, 0))):
                total = jnp.sum(total, 0, keepdims=True)
                for q in range(OWN):
                    moments[index, row * OWN + q:row * OWN + q + 1, :] = total[:, q * PANEL:(q + 1) * PANEL]
            return carry

        lax.fori_loop(0, GROUPS * SIDE, chunk_moments, 0)
        for extra in range(REACH):
            moments[GROUPS * SIDE + extra] = moments[extra]

    def group_moments_begin():
        gathered[0] = moments[pl.ds(group * SIDE, CHUNKS)]
        copies = []
        for offset in range(1, GROUPS):
            other = group_at(offset)
            copy = pltpu.make_async_remote_copy(
                src_ref=moments.at[pl.ds(other * SIDE, CHUNKS)],
                dst_ref=gathered.at[offset],
                send_sem=group_send.at[offset],
                recv_sem=group_recv.at[offset],
                device_id=(other * SIDE + x, core),
                device_id_type=MESH,
            )
            copy.start()
            copies.append(copy)
        return copies

    def ring_moments_begin(copies):
        for copy in copies:
            copy.wait()
        sums[0] = jnp.sum(gathered[...], 0)
        copies = []
        for index, peer in enumerate(peers):
            copy = pltpu.make_async_remote_copy(
                src_ref=sums.at[0],
                dst_ref=sums.at[index + 1],
                send_sem=stat_send.at[index],
                recv_sem=stat_recv.at[index],
                device_id=peer,
                device_id_type=MESH,
            )
            copy.start()
            copies.append(copy)
        return copies

    def ring_moments_end(copies):
        for copy in copies:
            copy.wait()
        totals[...] = jnp.sum(sums[...], 0)

    def standardize(step):
        chunk, start, count = STEPS[step]
        columns = pl.ds(start, count)
        panels = range(start // PANEL, (start + count) // PANEL)
        first, second = totals[chunk, 0:OWN], totals[chunk, OWN:2 * OWN]
        mean = first * (1.0 / SAMPLES)
        inv_scale = lax.rsqrt(second * (1.0 / SAMPLES) - mean * mean + 1e-05)
        mean = jnp.concatenate([mean[q:q + 1] for q in panels], axis=1)
        inv_scale = jnp.concatenate([inv_scale[q:q + 1] for q in panels], axis=1)

        def block_standard(block, carry):
            rows = pl.ds(pl.multiple_of(block * ROWS, ROWS), ROWS)
            values = received[chunk, block, :, columns].astype(jnp.float32)
            standard[chunk, rows, columns] = ((values - mean) * inv_scale).astype(jnp.bfloat16)
            return carry

        lax.fori_loop(0, GROUPS, block_standard, 0)
        if chunk < SIDE:
            turned[chunk] = standard[chunk].T

    def pieces_of(step):
        chunk, start, count = STEPS[step]
        pieces = []
        for d in range(REACH + 1):
            if 0 <= chunk - d < SIDE:
                inside = [
                    index for index, (p, q) in enumerate(PLACES[d])
                    if start // PANEL <= q < (start + count) // PANEL
                ]
                pieces.append((chunk - d, d, d + (start > 0), STARTS[d] + inside[0], len(inside)))
        return pieces

    def twin_copy(rows_chunk, number, first, count):
        which = pl.ds(first, count)
        return pltpu.make_async_remote_copy(
            src_ref=part.at[rows_chunk, 1 - core, which],
            dst_ref=twin.at[rows_chunk, which],
            send_sem=twin_send.at[rows_chunk, number],
            recv_sem=twin_recv.at[rows_chunk, number],
            device_id=(group * SIDE + x, 1 - core),
            device_id_type=MESH,
        )

    def multiply(step):
        chunk, start, columns = STEPS[step]
        for rows_chunk, d, number, first, count in pieces_of(step):
            for pp in range(OWN // 2):
                for qq in range(start // BLOCK, (start + columns) // BLOCK):
                    inside = [
                        (p, q) for p in range(2) for q in range(2) if (2 * pp + p, 2 * qq + q) in PLACES[d]
                    ]
                    if not inside:
                        continue
                    block = jnp.dot(
                        turned[rows_chunk, pp * BLOCK:(pp + 1) * BLOCK, :],
                        standard[chunk, :, qq * BLOCK:(qq + 1) * BLOCK],
                        preferred_element_type=jnp.float32,
                    )
                    for p, q in inside:
                        tile = STARTS[d] + PLACES[d].index((2 * pp + p, 2 * qq + q))
                        for half in range(2):
                            top = p * PANEL + half * (PANEL // 2)
                            part[rows_chunk, half, tile] = block[
                                top:top + PANEL // 2, q * PANEL:(q + 1) * PANEL
                            ]
            twin_copy(rows_chunk, number, first, count).start()

    def halves_of(first, count):
        upper = (count + 1) // 2
        return pl.ds(first, upper), pl.ds(first + upper, count - upper)

    def line_copy(rows_chunk, number, halves, half, way, relayed):
        which = halves[half]
        return pltpu.make_async_remote_copy(
            src_ref=part.at[rows_chunk, core, which],
            dst_ref=(relay if relayed else ring).at[way, which],
            send_sem=ring_send.at[rows_chunk, number, half],
            recv_sem=relay_recv.at[way, number] if relayed else ring_recv.at[way, number, half],
            device_id=(group * SIDE + lax.rem(x + 1 + 2 * way, SIDE), core),
            device_id_type=MESH,
        )

    def reduce(step):
        for rows_chunk, d, number, first, count in pieces_of(step):
            which = pl.ds(first, count)
            halves = halves_of(first, count)
            twin_copy(rows_chunk, number, first, count).wait()
            part[rows_chunk, core, which] = part[rows_chunk, core, which] + twin[rows_chunk, which]
            distance = lax.rem(rows_chunk - x + SIDE, SIDE)

            @pl.when(distance == 2)
            def _():
                line_copy(rows_chunk, number, halves, 0, 0, True).start()
                line_copy(rows_chunk, number, halves, 1, 1, True).start()

            @pl.when(distance == 1)
            def _():
                line_copy(rows_chunk, number, halves, 1, 0, False).start()

            @pl.when(distance == 3)
            def _():
                line_copy(rows_chunk, number, halves, 0, 1, False).start()

            pump(4)

        pump(3)
        for rows_chunk, d, number, first, count in pieces_of(step):
            halves = halves_of(first, count)
            distance = lax.rem(rows_chunk - x + SIDE, SIDE)
            for way in range(2):

                @pl.when(distance == 1 + 2 * way)
                def _():
                    which = halves[way]
                    line_copy(rows_chunk, number, halves, way, way, True).wait_recv()
                    part[rows_chunk, core, which] = part[rows_chunk, core, which] + relay[way, which]
                    line_copy(rows_chunk, number, halves, way, way, False).start()

    pump(8)
    for step in range(len(STEPS)):
        own_copy(step).start()
    lax.fori_loop(0, GROUPS * SIDE, stage_end, 0)
    local_moments()
    copies = group_moments_begin()
    pump(8)
    copies = ring_moments_begin(copies)
    pump(8)
    ring_moments_end(copies)
    for step in range(len(STEPS)):
        pump((step + 1) * (GROUPS - 1) + AHEAD - started[0])
        swap_end(step)
        standardize(step)
        multiply(step)
        pump(2)
        reduce(step)
    for copy in swaps[-AHEAD:]:
        copy.wait_send()

    for step in range(len(STEPS)):
        for rows_chunk, d, number, first, count in pieces_of(step):
            halves = halves_of(first, count)

            @pl.when(x != rows_chunk)
            def _():
                for half in range(2):
                    line_copy(rows_chunk, number, halves, half, 0, False).wait_send()

            @pl.when(x == rows_chunk)
            def _():
                for way in range(2):
                    for half in range(2):
                        line_copy(rows_chunk, number, halves, half, way, False).wait_recv()

    for d in range(REACH + 1):
        for index, (p, q) in enumerate(PLACES[d]):
            tile = STARTS[d] + index
            out_ref[p, d * OWN + q - p] = part[x, core, tile] + (ring[0, tile] + ring[1, tile])


def tiles(dosages):
    half_tile = (PANEL // 2, PANEL)
    dma = pltpu.SemaphoreType.DMA
    return pl.pallas_call(
        tiles_kernel,
        out_shape=jax.ShapeDtypeStruct((OWN, WMAX + 1) + half_tile, jnp.float32),
        in_specs=[pl.BlockSpec(memory_space=pltpu.HBM)],
        out_specs=pl.BlockSpec(memory_space=pltpu.VMEM),
        scratch_shapes=[
            pltpu.VMEM((GROUPS * SIDE, ROWS, CHUNK), jnp.bfloat16),
            pltpu.VMEM((CHUNKS, GROUPS, ROWS, CHUNK), jnp.bfloat16),
            pltpu.VMEM((GROUPS * SIDE + REACH, 2 * OWN, PANEL), jnp.float32),
            pltpu.VMEM((GROUPS, CHUNKS, 2 * OWN, PANEL), jnp.float32),
            pltpu.VMEM((8, CHUNKS, 2 * OWN, PANEL), jnp.float32),
            pltpu.VMEM((CHUNKS, 2 * OWN, PANEL), jnp.float32),
            pltpu.VMEM((CHUNKS, LOCAL, CHUNK), jnp.bfloat16),
            pltpu.VMEM((SIDE, CHUNK, LOCAL), jnp.bfloat16),
            pltpu.VMEM((SIDE, 2, TILES) + half_tile, jnp.float32),
            pltpu.VMEM((SIDE, TILES) + half_tile, jnp.float32),
            pltpu.VMEM((2, TILES) + half_tile, jnp.float32),
            pltpu.VMEM((2, TILES) + half_tile, jnp.float32),
            dma((GROUPS * SIDE,)),
            dma((len(STEPS),)),
            dma((len(STEPS), GROUPS)),
            dma((len(STEPS), GROUPS)),
            dma((GROUPS,)),
            dma((GROUPS,)),
            dma((7,)),
            dma((7,)),
            dma((SIDE, REACH + 2)),
            dma((SIDE, REACH + 2)),
            dma((2, REACH + 2)),
            dma((SIDE, REACH + 2, 2)),
            dma((2, REACH + 2, 2)),
        ],
        compiler_params=pltpu.CompilerParams(
            collective_id=0, has_side_effects=True, vmem_limit_bytes=52 * 1024 * 1024
        ),
        name="tiles",
    )(dosages)


def per_device(dosages, band_width):
    band_tiles = tiles(dosages)
    offsets = jnp.arange(WMAX + 1, dtype=jnp.int32)
    panel_count = OWN * lax.axis_size("var")
    global_panel = lax.axis_index("var") * OWN + jnp.arange(OWN, dtype=jnp.int32)
    in_band = (offsets[None, :] <= band_width[:, None]) & (
        global_panel[:, None] + offsets[None, :] < panel_count
    )
    return jnp.where(in_band[:, :, None, None], band_tiles * (1.0 / SAMPLES), 0.0)


def solution(mesh):
    in_specs = (P(("var", "samp"), None), P("var"))
    out_specs = P("var", None, "samp", None)
    return jax.shard_map(
        per_device, mesh=mesh, in_specs=in_specs, out_specs=out_specs, check_vma=False
    )
```

```python
import jax
import jax.numpy as jnp
from jax import lax
from jax.experimental import pallas as pl
from jax.experimental.pallas import tpu as pltpu
from jax.sharding import PartitionSpec as P

MESH = pl.DeviceIdType.MESH
WMAX = 8
PANEL = 128
SIDE = 4
GROUPS = SIDE * SIDE
OWN = 4
CHUNK = OWN * PANEL
REACH = WMAX // OWN
CHUNKS = SIDE + REACH
ROWS = 64
LOCAL = GROUPS * ROWS
BLOCK = 2 * PANEL
SWAPS = [(0, 2, 0, CHUNK), (2, 2, 0, CHUNK), (4, 1, 0, CHUNK), (5, 1, 0, BLOCK), (5, 1, BLOCK, BLOCK)]
READY = [0, 0, 1, 1, 2, 3, 4]
STEPS = [(chunk, 0, CHUNK) for chunk in range(CHUNKS - 1)] + [(CHUNKS - 1, first, BLOCK) for first in (0, BLOCK)]
AHEAD = 20
ORDER = [10, 15, 1, 4, 6, 3, 9, 12, 11, 14, 7, 13, 2, 8, 5]
SAMPLES = 8192
PLACES = [
    [(p, q) for q in range(OWN) for p in range(OWN) if 0 <= d * OWN + q - p <= WMAX] for d in range(REACH + 1)
]
STARTS = [sum(len(places) for places in PLACES[:d]) for d in range(REACH + 2)]
TILES = STARTS[-1]


def position():
    var = lax.axis_index("var")
    return var // SIDE, lax.rem(var, SIDE), lax.axis_index("samp")


def tiles_kernel(
    dos_ref, out_ref, staged, received, moments, gathered, sums, totals, standard, turned, part, twin, relay, ring,
    stage_sem, own_sem, swap_send, swap_recv, group_send, group_recv, stat_send, stat_recv, twin_send, twin_recv, relay_recv, ring_send, ring_recv,
):
    group, x, core = position()
    z, y = group // SIDE, lax.rem(group, SIDE)

    def stage(index):
        first = pl.multiple_of(index * CHUNK, CHUNK)
        return pltpu.make_async_copy(dos_ref.at[:, pl.ds(first, CHUNK)], staged.at[index], stage_sem.at[index])

    def stage_begin(index, carry):
        stage(index).start()
        return carry

    def stage_end(index, carry):
        stage(index).wait()
        return carry

    lax.fori_loop(0, GROUPS * SIDE, stage_begin, 0)

    peers = []
    for dx in range(SIDE):
        for dc in range(2):
            if dx or dc:
                peer_x, peer_c = lax.rem(x + dx, SIDE), lax.rem(core + dc, 2)
                peers.append((group * SIDE + peer_x, peer_c))

    def group_at(offset):
        return lax.rem(z + offset // SIDE, SIDE) * SIDE + lax.rem(y + offset % SIDE, SIDE)

    barrier = pltpu.get_barrier_semaphore()
    for offset in range(1, GROUPS):
        pl.semaphore_signal(
            barrier, inc=1, device_id=(group_at(offset) * SIDE + x, core), device_id_type=MESH
        )
    for peer in peers:
        pl.semaphore_signal(barrier, inc=1, device_id=peer, device_id_type=MESH)
    lax.fori_loop(0, GROUPS * SIDE, stage_end, 0)
    pl.semaphore_wait(barrier, GROUPS - 1 + len(peers))

    def source_and_target(step, other, slot):
        chunk, chunks, first, count = SWAPS[step]
        columns = pl.ds(first, count)
        source = staged.at[pl.ds(lax.rem(other * SIDE + chunk, GROUPS * SIDE), chunks), :, columns]
        return source, received.at[pl.ds(chunk, chunks), slot, :, columns]

    def swap(index):
        step, turn = divmod(index, GROUPS - 1)
        offset = ORDER[turn]
        other = group_at(offset)
        source, target = source_and_target(step, other, offset)
        return pltpu.make_async_remote_copy(
            src_ref=source,
            dst_ref=target,
            send_sem=swap_send.at[step, offset],
            recv_sem=swap_recv.at[step, offset],
            device_id=(other * SIDE + x, core),
            device_id_type=MESH,
        )

    swaps = [swap(index) for index in range(len(SWAPS) * (GROUPS - 1))]
    started = [0]

    def pump(count):
        for index in range(started[0], min(started[0] + count, len(swaps))):
            if index >= AHEAD:
                swaps[index - AHEAD].wait_send()
            swaps[index].start()
            started[0] = index + 1

    def own_copy(step):
        source, target = source_and_target(step, group, 0)
        return pltpu.make_async_copy(source, target, own_sem.at[step])

    def swap_end(step):
        own_copy(step).wait()
        for copy in swaps[step * (GROUPS - 1):(step + 1) * (GROUPS - 1)]:
            copy.wait_recv()

    def local_moments():
        def chunk_moments(index, carry):
            values = staged[index].astype(jnp.float32).reshape(ROWS // 8, 8, CHUNK)
            for row, total in enumerate((jnp.sum(values, 0), jnp.sum(values * values, 0))):
                total = jnp.sum(total, 0, keepdims=True)
                for q in range(OWN):
                    moments[index, row * OWN + q:row * OWN + q + 1, :] = total[:, q * PANEL:(q + 1) * PANEL]
            return carry

        lax.fori_loop(0, GROUPS * SIDE, chunk_moments, 0)
        for extra in range(REACH):
            moments[GROUPS * SIDE + extra] = moments[extra]

    def group_moments_begin():
        gathered[0] = moments[pl.ds(group * SIDE, CHUNKS)]
        copies = []
        for offset in range(1, GROUPS):
            other = group_at(offset)
            copy = pltpu.make_async_remote_copy(
                src_ref=moments.at[pl.ds(other * SIDE, CHUNKS)],
                dst_ref=gathered.at[offset],
                send_sem=group_send.at[offset],
                recv_sem=group_recv.at[offset],
                device_id=(other * SIDE + x, core),
                device_id_type=MESH,
            )
            copy.start()
            copies.append(copy)
        return copies

    def ring_moments_begin(copies):
        for copy in copies:
            copy.wait()
        sums[0] = jnp.sum(gathered[...], 0)
        copies = []
        for index, peer in enumerate(peers):
            copy = pltpu.make_async_remote_copy(
                src_ref=sums.at[0],
                dst_ref=sums.at[index + 1],
                send_sem=stat_send.at[index],
                recv_sem=stat_recv.at[index],
                device_id=peer,
                device_id_type=MESH,
            )
            copy.start()
            copies.append(copy)
        return copies

    def ring_moments_end(copies):
        for copy in copies:
            copy.wait()
        totals[...] = jnp.sum(sums[...], 0)

    def standardize(step):
        chunk, start, count = STEPS[step]
        columns = pl.ds(start, count)
        panels = range(start // PANEL, (start + count) // PANEL)
        first, second = totals[chunk, 0:OWN], totals[chunk, OWN:2 * OWN]
        mean = first * (1.0 / SAMPLES)
        inv_scale = lax.rsqrt(second * (1.0 / SAMPLES) - mean * mean + 1e-05)
        mean = jnp.concatenate([mean[q:q + 1] for q in panels], axis=1)
        inv_scale = jnp.concatenate([inv_scale[q:q + 1] for q in panels], axis=1)

        def block_standard(block, carry):
            rows = pl.ds(pl.multiple_of(block * ROWS, ROWS), ROWS)
            values = received[chunk, block, :, columns].astype(jnp.float32)
            standard[chunk, rows, columns] = ((values - mean) * inv_scale).astype(jnp.bfloat16)
            return carry

        lax.fori_loop(0, GROUPS, block_standard, 0)
        if chunk < SIDE:
            turned[chunk] = standard[chunk].T

    def pieces_of(step):
        chunk, start, count = STEPS[step]
        pieces = []
        for d in range(REACH + 1):
            if 0 <= chunk - d < SIDE:
                inside = [
                    index for index, (p, q) in enumerate(PLACES[d])
                    if start // PANEL <= q < (start + count) // PANEL
                ]
                pieces.append((chunk - d, d, d + (start > 0), STARTS[d] + inside[0], len(inside)))
        return pieces

    def twin_copy(rows_chunk, number, first, count):
        which = pl.ds(first, count)
        return pltpu.make_async_remote_copy(
            src_ref=part.at[rows_chunk, 1 - core, which],
            dst_ref=twin.at[rows_chunk, which],
            send_sem=twin_send.at[rows_chunk, number],
            recv_sem=twin_recv.at[rows_chunk, number],
            device_id=(group * SIDE + x, 1 - core),
            device_id_type=MESH,
        )

    def multiply(step):
        chunk, start, columns = STEPS[step]
        for rows_chunk, d, number, first, count in pieces_of(step):
            for pp in range(OWN // 2):
                for qq in range(start // BLOCK, (start + columns) // BLOCK):
                    inside = [
                        (p, q) for p in range(2) for q in range(2) if (2 * pp + p, 2 * qq + q) in PLACES[d]
                    ]
                    if not inside:
                        continue
                    block = jnp.dot(
                        turned[rows_chunk, pp * BLOCK:(pp + 1) * BLOCK, :],
                        standard[chunk, :, qq * BLOCK:(qq + 1) * BLOCK],
                        preferred_element_type=jnp.float32,
                    )
                    for p, q in inside:
                        tile = STARTS[d] + PLACES[d].index((2 * pp + p, 2 * qq + q))
                        for half in range(2):
                            top = p * PANEL + half * (PANEL // 2)
                            part[rows_chunk, half, tile] = block[
                                top:top + PANEL // 2, q * PANEL:(q + 1) * PANEL
                            ]
            twin_copy(rows_chunk, number, first, count).start()

    def halves_of(first, count):
        upper = (count + 1) // 2
        return pl.ds(first, upper), pl.ds(first + upper, count - upper)

    def line_copy(rows_chunk, number, halves, half, way, relayed):
        which = halves[half]
        return pltpu.make_async_remote_copy(
            src_ref=part.at[rows_chunk, core, which],
            dst_ref=(relay if relayed else ring).at[way, which],
            send_sem=ring_send.at[rows_chunk, number, half],
            recv_sem=relay_recv.at[way, number] if relayed else ring_recv.at[way, number, half],
            device_id=(group * SIDE + lax.rem(x + 1 + 2 * way, SIDE), core),
            device_id_type=MESH,
        )

    def reduce(step):
        for rows_chunk, d, number, first, count in pieces_of(step):
            which = pl.ds(first, count)
            halves = halves_of(first, count)
            twin_copy(rows_chunk, number, first, count).wait()
            part[rows_chunk, core, which] = part[rows_chunk, core, which] + twin[rows_chunk, which]
            distance = lax.rem(rows_chunk - x + SIDE, SIDE)

            @pl.when(distance == 2)
            def _():
                line_copy(rows_chunk, number, halves, 0, 0, True).start()
                line_copy(rows_chunk, number, halves, 1, 1, True).start()

            @pl.when(distance == 1)
            def _():
                line_copy(rows_chunk, number, halves, 1, 0, False).start()

            @pl.when(distance == 3)
            def _():
                line_copy(rows_chunk, number, halves, 0, 1, False).start()

            pump(4)

        pump(3)
        for rows_chunk, d, number, first, count in pieces_of(step):
            halves = halves_of(first, count)
            distance = lax.rem(rows_chunk - x + SIDE, SIDE)
            for way in range(2):

                @pl.when(distance == 1 + 2 * way)
                def _():
                    which = halves[way]
                    line_copy(rows_chunk, number, halves, way, way, True).wait_recv()
                    part[rows_chunk, core, which] = part[rows_chunk, core, which] + relay[way, which]
                    line_copy(rows_chunk, number, halves, way, way, False).start()

    pump(8)
    for step in range(len(SWAPS)):
        own_copy(step).start()
    local_moments()
    copies = group_moments_begin()
    pump(8)
    copies = ring_moments_begin(copies)
    pump(8)
    ring_moments_end(copies)
    for step, swap_step in enumerate(READY):
        if step == READY.index(swap_step):
            pump((swap_step + 1) * (GROUPS - 1) + AHEAD - started[0])
            swap_end(swap_step)
        standardize(step)
        multiply(step)
        pump(2)
        reduce(step)
    for copy in swaps[-AHEAD:]:
        copy.wait_send()

    for step in range(len(STEPS)):
        for rows_chunk, d, number, first, count in pieces_of(step):
            halves = halves_of(first, count)

            @pl.when(x != rows_chunk)
            def _():
                for half in range(2):
                    line_copy(rows_chunk, number, halves, half, 0, False).wait_send()

            @pl.when(x == rows_chunk)
            def _():
                for way in range(2):
                    for half in range(2):
                        line_copy(rows_chunk, number, halves, half, way, False).wait_recv()

    for d in range(REACH + 1):
        for index, (p, q) in enumerate(PLACES[d]):
            tile = STARTS[d] + index
            out_ref[p, d * OWN + q - p] = part[x, core, tile] + (ring[0, tile] + ring[1, tile])


def tiles(dosages):
    half_tile = (PANEL // 2, PANEL)
    dma = pltpu.SemaphoreType.DMA
    return pl.pallas_call(
        tiles_kernel,
        out_shape=jax.ShapeDtypeStruct((OWN, WMAX + 1) + half_tile, jnp.float32),
        in_specs=[pl.BlockSpec(memory_space=pltpu.HBM)],
        out_specs=pl.BlockSpec(memory_space=pltpu.VMEM),
        scratch_shapes=[
            pltpu.VMEM((GROUPS * SIDE, ROWS, CHUNK), jnp.bfloat16),
            pltpu.VMEM((CHUNKS, GROUPS, ROWS, CHUNK), jnp.bfloat16),
            pltpu.VMEM((GROUPS * SIDE + REACH, 2 * OWN, PANEL), jnp.float32),
            pltpu.VMEM((GROUPS, CHUNKS, 2 * OWN, PANEL), jnp.float32),
            pltpu.VMEM((8, CHUNKS, 2 * OWN, PANEL), jnp.float32),
            pltpu.VMEM((CHUNKS, 2 * OWN, PANEL), jnp.float32),
            pltpu.VMEM((CHUNKS, LOCAL, CHUNK), jnp.bfloat16),
            pltpu.VMEM((SIDE, CHUNK, LOCAL), jnp.bfloat16),
            pltpu.VMEM((SIDE, 2, TILES) + half_tile, jnp.float32),
            pltpu.VMEM((SIDE, TILES) + half_tile, jnp.float32),
            pltpu.VMEM((2, TILES) + half_tile, jnp.float32),
            pltpu.VMEM((2, TILES) + half_tile, jnp.float32),
            dma((GROUPS * SIDE,)),
            dma((len(SWAPS),)),
            dma((len(SWAPS), GROUPS)),
            dma((len(SWAPS), GROUPS)),
            dma((GROUPS,)),
            dma((GROUPS,)),
            dma((7,)),
            dma((7,)),
            dma((SIDE, REACH + 2)),
            dma((SIDE, REACH + 2)),
            dma((2, REACH + 2)),
            dma((SIDE, REACH + 2, 2)),
            dma((2, REACH + 2, 2)),
        ],
        compiler_params=pltpu.CompilerParams(
            collective_id=0, has_side_effects=True, vmem_limit_bytes=52 * 1024 * 1024
        ),
        name="tiles",
    )(dosages)


def per_device(dosages, band_width):
    band_tiles = tiles(dosages)
    offsets = jnp.arange(WMAX + 1, dtype=jnp.int32)
    panel_count = OWN * lax.axis_size("var")
    global_panel = lax.axis_index("var") * OWN + jnp.arange(OWN, dtype=jnp.int32)
    in_band = (offsets[None, :] <= band_width[:, None]) & (
        global_panel[:, None] + offsets[None, :] < panel_count
    )
    return jnp.where(in_band[:, :, None, None], band_tiles * (1.0 / SAMPLES), 0.0)


def solution(mesh):
    in_specs = (P(("var", "samp"), None), P("var"))
    out_specs = P("var", None, "samp", None)
    return jax.shard_map(
        per_device, mesh=mesh, in_specs=in_specs, out_specs=out_specs, check_vma=False
    )
```

```python
import jax
import jax.numpy as jnp
from jax import lax
from jax.experimental import pallas as pl
from jax.experimental.pallas import tpu as pltpu
from jax.sharding import PartitionSpec as P

MESH = pl.DeviceIdType.MESH
WMAX = 8
PANEL = 128
SIDE = 4
GROUPS = SIDE * SIDE
OWN = 4
CHUNK = OWN * PANEL
REACH = WMAX // OWN
CHUNKS = SIDE + REACH
ROWS = 64
LOCAL = GROUPS * ROWS
BLOCK = 2 * PANEL
STEPS = [(chunk, 0, CHUNK) for chunk in range(CHUNKS - 1)] + [(CHUNKS - 1, first, BLOCK) for first in (0, BLOCK)]
AHEAD = 12
PROMPT = len(STEPS) - 3
ORDER = [10, 15, 1, 4, 6, 3, 9, 12, 11, 14, 7, 13, 2, 8, 5]
SAMPLES = 8192
PLACES = [
    [(p, q) for q in range(OWN) for p in range(OWN) if 0 <= d * OWN + q - p <= WMAX] for d in range(REACH + 1)
]
STARTS = [sum(len(places) for places in PLACES[:d]) for d in range(REACH + 2)]
TILES = STARTS[-1]


def position():
    var = lax.axis_index("var")
    return var // SIDE, lax.rem(var, SIDE), lax.axis_index("samp")


def tiles_kernel(
    dos_ref, out_ref, staged, received, moments, gathered, sums, totals, standard, turned, part, twin, relay, ring,
    stage_sem, own_sem, swap_send, swap_recv, group_send, group_recv, stat_send, stat_recv, twin_send, twin_recv, relay_recv, ring_send, ring_recv,
):
    group, x, core = position()
    z, y = group // SIDE, lax.rem(group, SIDE)

    def stage(index):
        first = pl.multiple_of(index * CHUNK, CHUNK)
        return pltpu.make_async_copy(dos_ref.at[:, pl.ds(first, CHUNK)], staged.at[index], stage_sem.at[index])

    def stage_begin(index, carry):
        stage(index).start()
        return carry

    def stage_end(index, carry):
        stage(index).wait()
        return carry

    lax.fori_loop(0, GROUPS * SIDE, stage_begin, 0)

    peers = []
    for dx in range(SIDE):
        for dc in range(2):
            if dx or dc:
                peer_x, peer_c = lax.rem(x + dx, SIDE), lax.rem(core + dc, 2)
                peers.append((group * SIDE + peer_x, peer_c))

    def group_at(offset):
        return lax.rem(z + offset // SIDE, SIDE) * SIDE + lax.rem(y + offset % SIDE, SIDE)

    barrier = pltpu.get_barrier_semaphore()
    for offset in range(1, GROUPS):
        pl.semaphore_signal(
            barrier, inc=1, device_id=(group_at(offset) * SIDE + x, core), device_id_type=MESH
        )
    for peer in peers:
        pl.semaphore_signal(barrier, inc=1, device_id=peer, device_id_type=MESH)
    pl.semaphore_wait(barrier, GROUPS - 1 + len(peers))

    def columns_of(other, chunk, first, count):
        top = lax.rem(other * SIDE + chunk, GROUPS * SIDE) * CHUNK + first
        return dos_ref.at[:, pl.ds(pl.multiple_of(top, BLOCK), count)]

    def swap(index):
        step, turn = divmod(index, GROUPS - 1)
        chunk, first, count = STEPS[step]
        columns = pl.ds(first, count)
        offset = ORDER[turn]
        other = group_at(offset)
        return pltpu.make_async_remote_copy(
            src_ref=columns_of(other, chunk, first, count),
            dst_ref=received.at[chunk, offset, :, columns],
            send_sem=swap_send.at[step, offset],
            recv_sem=swap_recv.at[step, offset],
            device_id=(other * SIDE + x, core),
            device_id_type=MESH,
        )

    swaps = [swap(index) for index in range(len(STEPS) * (GROUPS - 1))]
    started = [0]

    def pump(count):
        for index in range(started[0], min(started[0] + count, len(swaps))):
            if index >= AHEAD:
                swaps[index - AHEAD].wait_send()
            swaps[index].start()
            started[0] = index + 1

    def own_copy(step):
        chunk, first, count = STEPS[step]
        columns = pl.ds(first, count)
        return pltpu.make_async_copy(
            columns_of(group, chunk, first, count),
            received.at[chunk, 0, :, columns],
            own_sem.at[step],
        )

    def swap_end(step):
        own_copy(step).wait()
        for copy in swaps[step * (GROUPS - 1):(step + 1) * (GROUPS - 1)]:
            copy.wait_recv()

    def local_moments():
        def chunk_moments(index, carry):
            values = staged[index].astype(jnp.float32).reshape(ROWS // 8, 8, CHUNK)
            for row, total in enumerate((jnp.sum(values, 0), jnp.sum(values * values, 0))):
                total = jnp.sum(total, 0, keepdims=True)
                for q in range(OWN):
                    moments[index, row * OWN + q:row * OWN + q + 1, :] = total[:, q * PANEL:(q + 1) * PANEL]
            return carry

        lax.fori_loop(0, GROUPS * SIDE, chunk_moments, 0)
        for extra in range(REACH):
            moments[GROUPS * SIDE + extra] = moments[extra]

    def group_moments_begin():
        gathered[0] = moments[pl.ds(group * SIDE, CHUNKS)]
        copies = []
        for offset in range(1, GROUPS):
            other = group_at(offset)
            copy = pltpu.make_async_remote_copy(
                src_ref=moments.at[pl.ds(other * SIDE, CHUNKS)],
                dst_ref=gathered.at[offset],
                send_sem=group_send.at[offset],
                recv_sem=group_recv.at[offset],
                device_id=(other * SIDE + x, core),
                device_id_type=MESH,
            )
            copy.start()
            copies.append(copy)
        return copies

    def ring_moments_begin(copies):
        for copy in copies:
            copy.wait()
        sums[0] = jnp.sum(gathered[...], 0)
        copies = []
        for index, peer in enumerate(peers):
            copy = pltpu.make_async_remote_copy(
                src_ref=sums.at[0],
                dst_ref=sums.at[index + 1],
                send_sem=stat_send.at[index],
                recv_sem=stat_recv.at[index],
                device_id=peer,
                device_id_type=MESH,
            )
            copy.start()
            copies.append(copy)
        return copies

    def ring_moments_end(copies):
        for copy in copies:
            copy.wait()
        totals[...] = jnp.sum(sums[...], 0)

    def standardize(step):
        chunk, start, count = STEPS[step]
        columns = pl.ds(start, count)
        panels = range(start // PANEL, (start + count) // PANEL)
        first, second = totals[chunk, 0:OWN], totals[chunk, OWN:2 * OWN]
        mean = first * (1.0 / SAMPLES)
        inv_scale = lax.rsqrt(second * (1.0 / SAMPLES) - mean * mean + 1e-05)
        mean = jnp.concatenate([mean[q:q + 1] for q in panels], axis=1)
        inv_scale = jnp.concatenate([inv_scale[q:q + 1] for q in panels], axis=1)

        def block_standard(block, carry):
            rows = pl.ds(pl.multiple_of(block * ROWS, ROWS), ROWS)
            values = received[chunk, block, :, columns].astype(jnp.float32)
            standard[chunk, rows, columns] = ((values - mean) * inv_scale).astype(jnp.bfloat16)
            return carry

        lax.fori_loop(0, GROUPS, block_standard, 0)
        if chunk < SIDE:
            turned[chunk] = standard[chunk].T

    def pieces_of(step):
        chunk, start, count = STEPS[step]
        pieces = []
        for d in range(REACH + 1):
            if 0 <= chunk - d < SIDE:
                inside = [
                    index for index, (p, q) in enumerate(PLACES[d])
                    if start // PANEL <= q < (start + count) // PANEL
                ]
                pieces.append((chunk - d, d, d + (start > 0), STARTS[d] + inside[0], len(inside)))
        return pieces

    def twin_copy(rows_chunk, number, first, count):
        which = pl.ds(first, count)
        return pltpu.make_async_remote_copy(
            src_ref=part.at[rows_chunk, 1 - core, which],
            dst_ref=twin.at[rows_chunk, which],
            send_sem=twin_send.at[rows_chunk, number],
            recv_sem=twin_recv.at[rows_chunk, number],
            device_id=(group * SIDE + x, 1 - core),
            device_id_type=MESH,
        )

    def multiply(step):
        chunk, start, columns = STEPS[step]
        for rows_chunk, d, number, first, count in pieces_of(step):
            for pp in range(OWN // 2):
                for qq in range(start // BLOCK, (start + columns) // BLOCK):
                    inside = [
                        (p, q) for p in range(2) for q in range(2) if (2 * pp + p, 2 * qq + q) in PLACES[d]
                    ]
                    if not inside:
                        continue
                    block = jnp.dot(
                        turned[rows_chunk, pp * BLOCK:(pp + 1) * BLOCK, :],
                        standard[chunk, :, qq * BLOCK:(qq + 1) * BLOCK],
                        preferred_element_type=jnp.float32,
                    )
                    for p, q in inside:
                        tile = STARTS[d] + PLACES[d].index((2 * pp + p, 2 * qq + q))
                        for half in range(2):
                            top = p * PANEL + half * (PANEL // 2)
                            part[rows_chunk, half, tile] = block[
                                top:top + PANEL // 2, q * PANEL:(q + 1) * PANEL
                            ]
            twin_copy(rows_chunk, number, first, count).start()

    def halves_of(first, count):
        upper = (count + 1) // 2
        return pl.ds(first, upper), pl.ds(first + upper, count - upper)

    def line_copy(rows_chunk, number, halves, half, way, relayed):
        which = halves[half]
        return pltpu.make_async_remote_copy(
            src_ref=part.at[rows_chunk, core, which],
            dst_ref=(relay if relayed else ring).at[way, which],
            send_sem=ring_send.at[rows_chunk, number, half],
            recv_sem=relay_recv.at[way, number] if relayed else ring_recv.at[way, number, half],
            device_id=(group * SIDE + lax.rem(x + 1 + 2 * way, SIDE), core),
            device_id_type=MESH,
        )

    def reduce(step):
        for rows_chunk, d, number, first, count in pieces_of(step):
            which = pl.ds(first, count)
            halves = halves_of(first, count)
            twin_copy(rows_chunk, number, first, count).wait()
            part[rows_chunk, core, which] = part[rows_chunk, core, which] + twin[rows_chunk, which]
            distance = lax.rem(rows_chunk - x + SIDE, SIDE)

            @pl.when(distance == 2)
            def _():
                line_copy(rows_chunk, number, halves, 0, 0, True).start()
                line_copy(rows_chunk, number, halves, 1, 1, True).start()

            @pl.when(distance == 1)
            def _():
                line_copy(rows_chunk, number, halves, 1, 0, False).start()

            @pl.when(distance == 3)
            def _():
                line_copy(rows_chunk, number, halves, 0, 1, False).start()

    def relay_on(step):
        for rows_chunk, d, number, first, count in pieces_of(step):
            halves = halves_of(first, count)
            distance = lax.rem(rows_chunk - x + SIDE, SIDE)
            for way in range(2):

                @pl.when(distance == 1 + 2 * way)
                def _():
                    which = halves[way]
                    line_copy(rows_chunk, number, halves, way, way, True).wait_recv()
                    part[rows_chunk, core, which] = part[rows_chunk, core, which] + relay[way, which]
                    line_copy(rows_chunk, number, halves, way, way, False).start()

    pump(8)
    for step in range(len(STEPS)):
        own_copy(step).start()
    lax.fori_loop(0, GROUPS * SIDE, stage_end, 0)
    local_moments()
    copies = group_moments_begin()
    pump(8)
    copies = ring_moments_begin(copies)
    pump(8)
    ring_moments_end(copies)
    for step in range(len(STEPS)):
        pump((step + 1) * (GROUPS - 1) + AHEAD - started[0])
        swap_end(step)
        standardize(step)
        multiply(step)
        if 1 <= step <= PROMPT:
            relay_on(step - 1)
        pump(AHEAD)
        reduce(step)
        if step >= PROMPT:
            relay_on(step)
    for copy in swaps[-AHEAD:]:
        copy.wait_send()

    for step in range(len(STEPS)):
        for rows_chunk, d, number, first, count in pieces_of(step):
            halves = halves_of(first, count)

            @pl.when(x != rows_chunk)
            def _():
                for half in range(2):
                    line_copy(rows_chunk, number, halves, half, 0, False).wait_send()

            @pl.when(x == rows_chunk)
            def _():
                for way in range(2):
                    for half in range(2):
                        line_copy(rows_chunk, number, halves, half, way, False).wait_recv()

    for d in range(REACH + 1):
        for index, (p, q) in enumerate(PLACES[d]):
            tile = STARTS[d] + index
            out_ref[p, d * OWN + q - p] = part[x, core, tile] + (ring[0, tile] + ring[1, tile])


def tiles(dosages):
    half_tile = (PANEL // 2, PANEL)
    dma = pltpu.SemaphoreType.DMA
    return pl.pallas_call(
        tiles_kernel,
        out_shape=jax.ShapeDtypeStruct((OWN, WMAX + 1) + half_tile, jnp.float32),
        in_specs=[pl.BlockSpec(memory_space=pltpu.HBM)],
        out_specs=pl.BlockSpec(memory_space=pltpu.VMEM),
        scratch_shapes=[
            pltpu.VMEM((GROUPS * SIDE, ROWS, CHUNK), jnp.bfloat16),
            pltpu.VMEM((CHUNKS, GROUPS, ROWS, CHUNK), jnp.bfloat16),
            pltpu.VMEM((GROUPS * SIDE + REACH, 2 * OWN, PANEL), jnp.float32),
            pltpu.VMEM((GROUPS, CHUNKS, 2 * OWN, PANEL), jnp.float32),
            pltpu.VMEM((8, CHUNKS, 2 * OWN, PANEL), jnp.float32),
            pltpu.VMEM((CHUNKS, 2 * OWN, PANEL), jnp.float32),
            pltpu.VMEM((CHUNKS, LOCAL, CHUNK), jnp.bfloat16),
            pltpu.VMEM((SIDE, CHUNK, LOCAL), jnp.bfloat16),
            pltpu.VMEM((SIDE, 2, TILES) + half_tile, jnp.float32),
            pltpu.VMEM((SIDE, TILES) + half_tile, jnp.float32),
            pltpu.VMEM((2, TILES) + half_tile, jnp.float32),
            pltpu.VMEM((2, TILES) + half_tile, jnp.float32),
            dma((GROUPS * SIDE,)),
            dma((len(STEPS),)),
            dma((len(STEPS), GROUPS)),
            dma((len(STEPS), GROUPS)),
            dma((GROUPS,)),
            dma((GROUPS,)),
            dma((7,)),
            dma((7,)),
            dma((SIDE, REACH + 2)),
            dma((SIDE, REACH + 2)),
            dma((2, REACH + 2)),
            dma((SIDE, REACH + 2, 2)),
            dma((2, REACH + 2, 2)),
        ],
        compiler_params=pltpu.CompilerParams(
            collective_id=0, has_side_effects=True, vmem_limit_bytes=52 * 1024 * 1024
        ),
        name="tiles",
    )(dosages)


def per_device(dosages, band_width):
    band_tiles = tiles(dosages)
    offsets = jnp.arange(WMAX + 1, dtype=jnp.int32)
    panel_count = OWN * lax.axis_size("var")
    global_panel = lax.axis_index("var") * OWN + jnp.arange(OWN, dtype=jnp.int32)
    in_band = (offsets[None, :] <= band_width[:, None]) & (
        global_panel[:, None] + offsets[None, :] < panel_count
    )
    return jnp.where(in_band[:, :, None, None], band_tiles * (1.0 / SAMPLES), 0.0)


def solution(mesh):
    in_specs = (P(("var", "samp"), None), P("var"))
    out_specs = P("var", None, "samp", None)
    return jax.shard_map(
        per_device, mesh=mesh, in_specs=in_specs, out_specs=out_specs, check_vma=False
    )
```

```python
import jax
import jax.numpy as jnp
from jax import lax
from jax.experimental import pallas as pl
from jax.experimental.pallas import tpu as pltpu
from jax.sharding import PartitionSpec as P

MESH = pl.DeviceIdType.MESH
WMAX = 8
PANEL = 128
SIDE = 4
GROUPS = SIDE * SIDE
OWN = 4
CHUNK = OWN * PANEL
REACH = WMAX // OWN
CHUNKS = SIDE + REACH
ROWS = 64
LOCAL = GROUPS * ROWS
BLOCK = 2 * PANEL
STEPS = [(chunk, 0, CHUNK) for chunk in range(SIDE)]
STEPS += [(chunk, first, BLOCK) for chunk in range(SIDE, CHUNKS) for first in (0, BLOCK)]
AHEAD = 24
ORDER = [10, 2, 8, 6, 9, 14, 11, 5, 15, 7, 13, 1, 4, 3, 12]
SAMPLES = 8192
PLACES = [
    [(p, q) for q in range(OWN) for p in range(OWN) if 0 <= d * OWN + q - p <= WMAX] for d in range(REACH + 1)
]
STARTS = [sum(len(places) for places in PLACES[:d]) for d in range(REACH + 2)]
TILES = STARTS[-1]


def position():
    var = lax.axis_index("var")
    return var // SIDE, lax.rem(var, SIDE), lax.axis_index("samp")


def tiles_kernel(
    dos_ref, out_ref, staged, received, moments, gathered, sums, totals, standard, turned, part, twin, relay, ring,
    stage_sem, own_sem, swap_send, swap_recv, group_send, group_recv, stat_send, stat_recv, twin_send, twin_recv, relay_recv, ring_send, ring_recv,
):
    group, x, core = position()
    z, y = group // SIDE, lax.rem(group, SIDE)

    def stage(index):
        first = pl.multiple_of(index * CHUNK, CHUNK)
        return pltpu.make_async_copy(dos_ref.at[:, pl.ds(first, CHUNK)], staged.at[index], stage_sem.at[index])

    def stage_begin(index, carry):
        stage(index).start()
        return carry

    def stage_end(index, carry):
        stage(index).wait()
        return carry

    lax.fori_loop(0, GROUPS * SIDE, stage_begin, 0)

    peers = []
    for dx in range(SIDE):
        for dc in range(2):
            if dx or dc:
                peer_x, peer_c = lax.rem(x + dx, SIDE), lax.rem(core + dc, 2)
                peers.append((group * SIDE + peer_x, peer_c))

    def group_at(offset):
        return lax.rem(z + offset // SIDE, SIDE) * SIDE + lax.rem(y + offset % SIDE, SIDE)

    barrier = pltpu.get_barrier_semaphore()
    for offset in range(1, GROUPS):
        pl.semaphore_signal(
            barrier, inc=1, device_id=(group_at(offset) * SIDE + x, core), device_id_type=MESH
        )
    for peer in peers:
        pl.semaphore_signal(barrier, inc=1, device_id=peer, device_id_type=MESH)
    pl.semaphore_wait(barrier, GROUPS - 1 + len(peers))

    def columns_of(other, chunk, first, count):
        top = lax.rem(other * SIDE + chunk, GROUPS * SIDE) * CHUNK + first
        return dos_ref.at[:, pl.ds(pl.multiple_of(top, BLOCK), count)]

    def swap(index):
        step, turn = divmod(index, GROUPS - 1)
        chunk, first, count = STEPS[step]
        columns = pl.ds(first, count)
        offset = ORDER[turn]
        other = group_at(offset)
        return pltpu.make_async_remote_copy(
            src_ref=columns_of(other, chunk, first, count),
            dst_ref=received.at[chunk, offset, :, columns],
            send_sem=swap_send.at[step, offset],
            recv_sem=swap_recv.at[step, offset],
            device_id=(other * SIDE + x, core),
            device_id_type=MESH,
        )

    swaps = [swap(index) for index in range(len(STEPS) * (GROUPS - 1))]
    started = [0]

    def pump(count):
        for index in range(started[0], min(started[0] + count, len(swaps))):
            if index >= AHEAD:
                swaps[index - AHEAD].wait_send()
            swaps[index].start()
            started[0] = index + 1

    def own_copy(step):
        chunk, first, count = STEPS[step]
        columns = pl.ds(first, count)
        return pltpu.make_async_copy(
            columns_of(group, chunk, first, count),
            received.at[chunk, 0, :, columns],
            own_sem.at[step],
        )

    def swap_end(step):
        own_copy(step).wait()
        for copy in swaps[step * (GROUPS - 1):(step + 1) * (GROUPS - 1)]:
            copy.wait_recv()

    def local_moments():
        def chunk_moments(index, carry):
            values = staged[index].astype(jnp.float32).reshape(ROWS // 8, 8, CHUNK)
            for row, total in enumerate((jnp.sum(values, 0), jnp.sum(values * values, 0))):
                total = jnp.sum(total, 0, keepdims=True)
                for q in range(OWN):
                    moments[index, row * OWN + q:row * OWN + q + 1, :] = total[:, q * PANEL:(q + 1) * PANEL]
            return carry

        lax.fori_loop(0, GROUPS * SIDE, chunk_moments, 0)
        for extra in range(REACH):
            moments[GROUPS * SIDE + extra] = moments[extra]

    def group_moments_begin():
        gathered[0] = moments[pl.ds(group * SIDE, CHUNKS)]
        copies = []
        for offset in range(1, GROUPS):
            other = group_at(offset)
            copy = pltpu.make_async_remote_copy(
                src_ref=moments.at[pl.ds(other * SIDE, CHUNKS)],
                dst_ref=gathered.at[offset],
                send_sem=group_send.at[offset],
                recv_sem=group_recv.at[offset],
                device_id=(other * SIDE + x, core),
                device_id_type=MESH,
            )
            copy.start()
            copies.append(copy)
        return copies

    def ring_moments_begin(copies):
        for copy in copies:
            copy.wait()
        sums[0] = jnp.sum(gathered[...], 0)
        copies = []
        for index, peer in enumerate(peers):
            copy = pltpu.make_async_remote_copy(
                src_ref=sums.at[0],
                dst_ref=sums.at[index + 1],
                send_sem=stat_send.at[index],
                recv_sem=stat_recv.at[index],
                device_id=peer,
                device_id_type=MESH,
            )
            copy.start()
            copies.append(copy)
        return copies

    def ring_moments_end(copies):
        for copy in copies:
            copy.wait()
        totals[...] = jnp.sum(sums[...], 0)

    def standardize(step):
        chunk, start, count = STEPS[step]
        columns = pl.ds(start, count)
        panels = range(start // PANEL, (start + count) // PANEL)
        first, second = totals[chunk, 0:OWN], totals[chunk, OWN:2 * OWN]
        mean = first * (1.0 / SAMPLES)
        inv_scale = lax.rsqrt(second * (1.0 / SAMPLES) - mean * mean + 1e-05)
        mean = jnp.concatenate([mean[q:q + 1] for q in panels], axis=1)
        inv_scale = jnp.concatenate([inv_scale[q:q + 1] for q in panels], axis=1)

        def block_standard(block, carry):
            rows = pl.ds(pl.multiple_of(block * ROWS, ROWS), ROWS)
            values = received[chunk, block, :, columns].astype(jnp.float32)
            standard[chunk, rows, columns] = ((values - mean) * inv_scale).astype(jnp.bfloat16)
            return carry

        lax.fori_loop(0, GROUPS, block_standard, 0)
        if chunk < SIDE:
            turned[chunk] = standard[chunk].T

    def pieces_of(step):
        chunk, start, count = STEPS[step]
        pieces = []
        for d in range(REACH + 1):
            if 0 <= chunk - d < SIDE:
                inside = [
                    index for index, (p, q) in enumerate(PLACES[d])
                    if start // PANEL <= q < (start + count) // PANEL
                ]
                pieces.append((chunk - d, d, 2 * d + (start > 0), STARTS[d] + inside[0], len(inside)))
        return pieces

    def twin_copy(rows_chunk, number, first, count):
        which = pl.ds(first, count)
        return pltpu.make_async_remote_copy(
            src_ref=part.at[rows_chunk, 1 - core, which],
            dst_ref=twin.at[rows_chunk, which],
            send_sem=twin_send.at[rows_chunk, number],
            recv_sem=twin_recv.at[rows_chunk, number],
            device_id=(group * SIDE + x, 1 - core),
            device_id_type=MESH,
        )

    def multiply(step):
        chunk, start, columns = STEPS[step]
        for rows_chunk, d, number, first, count in pieces_of(step):
            for pp in range(OWN // 2):
                for qq in range(start // BLOCK, (start + columns) // BLOCK):
                    inside = [
                        (p, q) for p in range(2) for q in range(2) if (2 * pp + p, 2 * qq + q) in PLACES[d]
                    ]
                    if not inside:
                        continue
                    block = jnp.dot(
                        turned[rows_chunk, pp * BLOCK:(pp + 1) * BLOCK, :],
                        standard[chunk, :, qq * BLOCK:(qq + 1) * BLOCK],
                        preferred_element_type=jnp.float32,
                    )
                    for p, q in inside:
                        tile = STARTS[d] + PLACES[d].index((2 * pp + p, 2 * qq + q))
                        for half in range(2):
                            top = p * PANEL + half * (PANEL // 2)
                            part[rows_chunk, half, tile] = block[
                                top:top + PANEL // 2, q * PANEL:(q + 1) * PANEL
                            ]
            twin_copy(rows_chunk, number, first, count).start()

    def halves_of(first, count):
        upper = (count + 1) // 2
        return pl.ds(first, upper), pl.ds(first + upper, count - upper)

    def line_copy(rows_chunk, number, halves, half, way, relayed):
        which = halves[half]
        return pltpu.make_async_remote_copy(
            src_ref=part.at[rows_chunk, core, which],
            dst_ref=(relay if relayed else ring).at[way, which],
            send_sem=ring_send.at[rows_chunk, number, half],
            recv_sem=relay_recv.at[way, number] if relayed else ring_recv.at[way, number, half],
            device_id=(group * SIDE + lax.rem(x + 1 + 2 * way, SIDE), core),
            device_id_type=MESH,
        )

    def reduce(step):
        for rows_chunk, d, number, first, count in pieces_of(step):
            which = pl.ds(first, count)
            halves = halves_of(first, count)
            twin_copy(rows_chunk, number, first, count).wait()
            part[rows_chunk, core, which] = part[rows_chunk, core, which] + twin[rows_chunk, which]
            distance = lax.rem(rows_chunk - x + SIDE, SIDE)

            @pl.when(distance == 2)
            def _():
                line_copy(rows_chunk, number, halves, 0, 0, True).start()
                line_copy(rows_chunk, number, halves, 1, 1, True).start()

            @pl.when(distance == 1)
            def _():
                line_copy(rows_chunk, number, halves, 1, 0, False).start()

            @pl.when(distance == 3)
            def _():
                line_copy(rows_chunk, number, halves, 0, 1, False).start()

            pump(4)

        pump(3)
        for rows_chunk, d, number, first, count in pieces_of(step):
            halves = halves_of(first, count)
            distance = lax.rem(rows_chunk - x + SIDE, SIDE)
            for way in range(2):

                @pl.when(distance == 1 + 2 * way)
                def _():
                    which = halves[way]
                    line_copy(rows_chunk, number, halves, way, way, True).wait_recv()
                    part[rows_chunk, core, which] = part[rows_chunk, core, which] + relay[way, which]
                    line_copy(rows_chunk, number, halves, way, way, False).start()

    pump(8)
    for step in range(len(STEPS)):
        own_copy(step).start()
    lax.fori_loop(0, GROUPS * SIDE, stage_end, 0)
    local_moments()
    copies = group_moments_begin()
    pump(8)
    copies = ring_moments_begin(copies)
    pump(8)
    ring_moments_end(copies)
    for step in range(len(STEPS)):
        pump((step + 1) * (GROUPS - 1) + AHEAD - started[0])
        swap_end(step)
        standardize(step)
        multiply(step)
        pump(2)
        reduce(step)
    for copy in swaps[-AHEAD:]:
        copy.wait_send()

    for step in range(len(STEPS)):
        for rows_chunk, d, number, first, count in pieces_of(step):
            halves = halves_of(first, count)

            @pl.when(x != rows_chunk)
            def _():
                for half in range(2):
                    line_copy(rows_chunk, number, halves, half, 0, False).wait_send()

            @pl.when(x == rows_chunk)
            def _():
                for way in range(2):
                    for half in range(2):
                        line_copy(rows_chunk, number, halves, half, way, False).wait_recv()

    for d in range(REACH + 1):
        for index, (p, q) in enumerate(PLACES[d]):
            tile = STARTS[d] + index
            out_ref[p, d * OWN + q - p] = part[x, core, tile] + (ring[0, tile] + ring[1, tile])


def tiles(dosages):
    half_tile = (PANEL // 2, PANEL)
    dma = pltpu.SemaphoreType.DMA
    return pl.pallas_call(
        tiles_kernel,
        out_shape=jax.ShapeDtypeStruct((OWN, WMAX + 1) + half_tile, jnp.float32),
        in_specs=[pl.BlockSpec(memory_space=pltpu.HBM)],
        out_specs=pl.BlockSpec(memory_space=pltpu.VMEM),
        scratch_shapes=[
            pltpu.VMEM((GROUPS * SIDE, ROWS, CHUNK), jnp.bfloat16),
            pltpu.VMEM((CHUNKS, GROUPS, ROWS, CHUNK), jnp.bfloat16),
            pltpu.VMEM((GROUPS * SIDE + REACH, 2 * OWN, PANEL), jnp.float32),
            pltpu.VMEM((GROUPS, CHUNKS, 2 * OWN, PANEL), jnp.float32),
            pltpu.VMEM((8, CHUNKS, 2 * OWN, PANEL), jnp.float32),
            pltpu.VMEM((CHUNKS, 2 * OWN, PANEL), jnp.float32),
            pltpu.VMEM((CHUNKS, LOCAL, CHUNK), jnp.bfloat16),
            pltpu.VMEM((SIDE, CHUNK, LOCAL), jnp.bfloat16),
            pltpu.VMEM((SIDE, 2, TILES) + half_tile, jnp.float32),
            pltpu.VMEM((SIDE, TILES) + half_tile, jnp.float32),
            pltpu.VMEM((2, TILES) + half_tile, jnp.float32),
            pltpu.VMEM((2, TILES) + half_tile, jnp.float32),
            dma((GROUPS * SIDE,)),
            dma((len(STEPS),)),
            dma((len(STEPS), GROUPS)),
            dma((len(STEPS), GROUPS)),
            dma((GROUPS,)),
            dma((GROUPS,)),
            dma((7,)),
            dma((7,)),
            dma((SIDE, 2 * REACH + 2)),
            dma((SIDE, 2 * REACH + 2)),
            dma((2, 2 * REACH + 2)),
            dma((SIDE, 2 * REACH + 2, 2)),
            dma((2, 2 * REACH + 2, 2)),
        ],
        compiler_params=pltpu.CompilerParams(
            collective_id=0, has_side_effects=True, vmem_limit_bytes=52 * 1024 * 1024
        ),
        name="tiles",
    )(dosages)


def per_device(dosages, band_width):
    band_tiles = tiles(dosages)
    offsets = jnp.arange(WMAX + 1, dtype=jnp.int32)
    panel_count = OWN * lax.axis_size("var")
    global_panel = lax.axis_index("var") * OWN + jnp.arange(OWN, dtype=jnp.int32)
    in_band = (offsets[None, :] <= band_width[:, None]) & (
        global_panel[:, None] + offsets[None, :] < panel_count
    )
    return jnp.where(in_band[:, :, None, None], band_tiles * (1.0 / SAMPLES), 0.0)


def solution(mesh):
    in_specs = (P(("var", "samp"), None), P("var"))
    out_specs = P("var", None, "samp", None)
    return jax.shard_map(
        per_device, mesh=mesh, in_specs=in_specs, out_specs=out_specs, check_vma=False
    )
```

```python
import jax
import jax.numpy as jnp
from jax import lax
from jax.experimental import pallas as pl
from jax.experimental.pallas import tpu as pltpu
from jax.sharding import PartitionSpec as P

MESH = pl.DeviceIdType.MESH
WMAX = 8
PANEL = 128
SIDE = 4
GROUPS = SIDE * SIDE
OWN = 4
CHUNK = OWN * PANEL
REACH = WMAX // OWN
CHUNKS = SIDE + REACH
ROWS = 64
LOCAL = GROUPS * ROWS
BLOCK = 2 * PANEL
STEPS = [(chunk, 0, CHUNK) for chunk in range(CHUNKS - 1)] + [(CHUNKS - 1, first, BLOCK) for first in (0, BLOCK)]
AHEAD = 24
ORDER = [10, 15, 1, 4, 6, 3, 9, 12, 11, 14, 7, 13, 2, 8, 5]
PARTNER = [1, 0, 3, 2, 5, 4, 7, 6, 9, 8, 11, 10, 13, 12, 14]
SAMPLES = 8192
PLACES = [
    [(p, q) for q in range(OWN) for p in range(OWN) if 0 <= d * OWN + q - p <= WMAX] for d in range(REACH + 1)
]
STARTS = [sum(len(places) for places in PLACES[:d]) for d in range(REACH + 2)]
TILES = STARTS[-1]


def position():
    var = lax.axis_index("var")
    return var // SIDE, lax.rem(var, SIDE), lax.axis_index("samp")


def tiles_kernel(
    dos_ref, out_ref, staged, received, moments, gathered, sums, totals, standard, turned, part, twin, relay, ring,
    stage_sem, own_sem, swap_send, swap_recv, group_send, group_recv, stat_send, stat_recv, twin_send, twin_recv, relay_recv, ring_send, ring_recv,
):
    group, x, core = position()
    z, y = group // SIDE, lax.rem(group, SIDE)

    def stage(index):
        first = pl.multiple_of(index * CHUNK, CHUNK)
        return pltpu.make_async_copy(dos_ref.at[:, pl.ds(first, CHUNK)], staged.at[index], stage_sem.at[index])

    def stage_begin(index, carry):
        stage(index).start()
        return carry

    def stage_end(index, carry):
        stage(index).wait()
        return carry

    lax.fori_loop(0, GROUPS * SIDE, stage_begin, 0)

    peers = []
    for dx in range(SIDE):
        for dc in range(2):
            if dx or dc:
                peer_x, peer_c = lax.rem(x + dx, SIDE), lax.rem(core + dc, 2)
                peers.append((group * SIDE + peer_x, peer_c))

    def group_at(offset):
        return lax.rem(z + offset // SIDE, SIDE) * SIDE + lax.rem(y + lax.rem(offset, SIDE), SIDE)

    barrier = pltpu.get_barrier_semaphore()
    for offset in range(1, GROUPS):
        pl.semaphore_signal(
            barrier, inc=1, device_id=(group_at(offset) * SIDE + x, core), device_id_type=MESH
        )
    for peer in peers:
        pl.semaphore_signal(barrier, inc=1, device_id=peer, device_id_type=MESH)
    pl.semaphore_wait(barrier, GROUPS - 1 + len(peers))

    def columns_of(other, chunk, first, count):
        top = lax.rem(other * SIDE + chunk, GROUPS * SIDE) * CHUNK + first
        return dos_ref.at[:, pl.ds(pl.multiple_of(top, BLOCK), count)]

    def swap(index):
        step, turn = divmod(index, GROUPS - 1)
        chunk, first, count = STEPS[step]
        columns = pl.ds(first, count)
        offset = ORDER[turn] + core * (ORDER[PARTNER[turn]] - ORDER[turn])
        other = group_at(offset)
        return pltpu.make_async_remote_copy(
            src_ref=columns_of(other, chunk, first, count),
            dst_ref=received.at[chunk, offset, :, columns],
            send_sem=swap_send.at[step, offset],
            recv_sem=swap_recv.at[step, offset],
            device_id=(other * SIDE + x, core),
            device_id_type=MESH,
        )

    swaps = [swap(index) for index in range(len(STEPS) * (GROUPS - 1))]
    started = [0]

    def pump(count):
        for index in range(started[0], min(started[0] + count, len(swaps))):
            if index >= AHEAD:
                swaps[index - AHEAD].wait_send()
            swaps[index].start()
            started[0] = index + 1

    def own_copy(step):
        chunk, first, count = STEPS[step]
        columns = pl.ds(first, count)
        return pltpu.make_async_copy(
            columns_of(group, chunk, first, count),
            received.at[chunk, 0, :, columns],
            own_sem.at[step],
        )

    def swap_end(step):
        own_copy(step).wait()
        for copy in swaps[step * (GROUPS - 1):(step + 1) * (GROUPS - 1)]:
            copy.wait_recv()

    def local_moments():
        def chunk_moments(index, carry):
            values = staged[index].astype(jnp.float32).reshape(ROWS // 8, 8, CHUNK)
            for row, total in enumerate((jnp.sum(values, 0), jnp.sum(values * values, 0))):
                total = jnp.sum(total, 0, keepdims=True)
                for q in range(OWN):
                    moments[index, row * OWN + q:row * OWN + q + 1, :] = total[:, q * PANEL:(q + 1) * PANEL]
            return carry

        lax.fori_loop(0, GROUPS * SIDE, chunk_moments, 0)
        for extra in range(REACH):
            moments[GROUPS * SIDE + extra] = moments[extra]

    def group_moments_begin():
        gathered[0] = moments[pl.ds(group * SIDE, CHUNKS)]
        copies = []
        for offset in range(1, GROUPS):
            other = group_at(offset)
            copy = pltpu.make_async_remote_copy(
                src_ref=moments.at[pl.ds(other * SIDE, CHUNKS)],
                dst_ref=gathered.at[offset],
                send_sem=group_send.at[offset],
                recv_sem=group_recv.at[offset],
                device_id=(other * SIDE + x, core),
                device_id_type=MESH,
            )
            copy.start()
            copies.append(copy)
        return copies

    def ring_moments_begin(copies):
        for copy in copies:
            copy.wait()
        sums[0] = jnp.sum(gathered[...], 0)
        copies = []
        for index, peer in enumerate(peers):
            copy = pltpu.make_async_remote_copy(
                src_ref=sums.at[0],
                dst_ref=sums.at[index + 1],
                send_sem=stat_send.at[index],
                recv_sem=stat_recv.at[index],
                device_id=peer,
                device_id_type=MESH,
            )
            copy.start()
            copies.append(copy)
        return copies

    def ring_moments_end(copies):
        for copy in copies:
            copy.wait()
        totals[...] = jnp.sum(sums[...], 0)

    def standardize(step):
        chunk, start, count = STEPS[step]
        columns = pl.ds(start, count)
        panels = range(start // PANEL, (start + count) // PANEL)
        first, second = totals[chunk, 0:OWN], totals[chunk, OWN:2 * OWN]
        mean = first * (1.0 / SAMPLES)
        inv_scale = lax.rsqrt(second * (1.0 / SAMPLES) - mean * mean + 1e-05)
        mean = jnp.concatenate([mean[q:q + 1] for q in panels], axis=1)
        inv_scale = jnp.concatenate([inv_scale[q:q + 1] for q in panels], axis=1)

        def block_standard(block, carry):
            rows = pl.ds(pl.multiple_of(block * ROWS, ROWS), ROWS)
            values = received[chunk, block, :, columns].astype(jnp.float32)
            standard[chunk, rows, columns] = ((values - mean) * inv_scale).astype(jnp.bfloat16)
            return carry

        lax.fori_loop(0, GROUPS, block_standard, 0)
        if chunk < SIDE:
            turned[chunk] = standard[chunk].T

    def pieces_of(step):
        chunk, start, count = STEPS[step]
        pieces = []
        for d in range(REACH + 1):
            if 0 <= chunk - d < SIDE:
                inside = [
                    index for index, (p, q) in enumerate(PLACES[d])
                    if start // PANEL <= q < (start + count) // PANEL
                ]
                pieces.append((chunk - d, d, d + (start > 0), STARTS[d] + inside[0], len(inside)))
        return pieces

    def twin_copy(rows_chunk, number, first, count):
        which = pl.ds(first, count)
        return pltpu.make_async_remote_copy(
            src_ref=part.at[rows_chunk, 1 - core, which],
            dst_ref=twin.at[rows_chunk, which],
            send_sem=twin_send.at[rows_chunk, number],
            recv_sem=twin_recv.at[rows_chunk, number],
            device_id=(group * SIDE + x, 1 - core),
            device_id_type=MESH,
        )

    def multiply(step):
        chunk, start, columns = STEPS[step]
        for rows_chunk, d, number, first, count in pieces_of(step):
            for pp in range(OWN // 2):
                for qq in range(start // BLOCK, (start + columns) // BLOCK):
                    inside = [
                        (p, q) for p in range(2) for q in range(2) if (2 * pp + p, 2 * qq + q) in PLACES[d]
                    ]
                    if not inside:
                        continue
                    block = jnp.dot(
                        turned[rows_chunk, pp * BLOCK:(pp + 1) * BLOCK, :],
                        standard[chunk, :, qq * BLOCK:(qq + 1) * BLOCK],
                        preferred_element_type=jnp.float32,
                    )
                    for p, q in inside:
                        tile = STARTS[d] + PLACES[d].index((2 * pp + p, 2 * qq + q))
                        for half in range(2):
                            top = p * PANEL + half * (PANEL // 2)
                            part[rows_chunk, half, tile] = block[
                                top:top + PANEL // 2, q * PANEL:(q + 1) * PANEL
                            ]
            twin_copy(rows_chunk, number, first, count).start()

    def halves_of(first, count):
        upper = (count + 1) // 2
        return pl.ds(first, upper), pl.ds(first + upper, count - upper)

    def line_copy(rows_chunk, number, halves, half, way, relayed):
        which = halves[half]
        return pltpu.make_async_remote_copy(
            src_ref=part.at[rows_chunk, core, which],
            dst_ref=(relay if relayed else ring).at[way, which],
            send_sem=ring_send.at[rows_chunk, number, half],
            recv_sem=relay_recv.at[way, number] if relayed else ring_recv.at[way, number, half],
            device_id=(group * SIDE + lax.rem(x + 1 + 2 * way, SIDE), core),
            device_id_type=MESH,
        )

    def reduce(step):
        for rows_chunk, d, number, first, count in pieces_of(step):
            which = pl.ds(first, count)
            halves = halves_of(first, count)
            twin_copy(rows_chunk, number, first, count).wait()
            part[rows_chunk, core, which] = part[rows_chunk, core, which] + twin[rows_chunk, which]
            distance = lax.rem(rows_chunk - x + SIDE, SIDE)

            @pl.when(distance == 2)
            def _():
                line_copy(rows_chunk, number, halves, 0, 0, True).start()
                line_copy(rows_chunk, number, halves, 1, 1, True).start()

            @pl.when(distance == 1)
            def _():
                line_copy(rows_chunk, number, halves, 1, 0, False).start()

            @pl.when(distance == 3)
            def _():
                line_copy(rows_chunk, number, halves, 0, 1, False).start()

            pump(4)

        pump(3)
        for rows_chunk, d, number, first, count in pieces_of(step):
            halves = halves_of(first, count)
            distance = lax.rem(rows_chunk - x + SIDE, SIDE)
            for way in range(2):

                @pl.when(distance == 1 + 2 * way)
                def _():
                    which = halves[way]
                    line_copy(rows_chunk, number, halves, way, way, True).wait_recv()
                    part[rows_chunk, core, which] = part[rows_chunk, core, which] + relay[way, which]
                    line_copy(rows_chunk, number, halves, way, way, False).start()

    pump(8)
    for step in range(len(STEPS)):
        own_copy(step).start()
    lax.fori_loop(0, GROUPS * SIDE, stage_end, 0)
    local_moments()
    copies = group_moments_begin()
    pump(8)
    copies = ring_moments_begin(copies)
    pump(8)
    ring_moments_end(copies)
    for step in range(len(STEPS)):
        pump((step + 1) * (GROUPS - 1) + AHEAD - started[0])
        swap_end(step)
        standardize(step)
        multiply(step)
        pump(2)
        reduce(step)
    for copy in swaps[-AHEAD:]:
        copy.wait_send()

    for step in range(len(STEPS)):
        for rows_chunk, d, number, first, count in pieces_of(step):
            halves = halves_of(first, count)

            @pl.when(x != rows_chunk)
            def _():
                for half in range(2):
                    line_copy(rows_chunk, number, halves, half, 0, False).wait_send()

            @pl.when(x == rows_chunk)
            def _():
                for way in range(2):
                    for half in range(2):
                        line_copy(rows_chunk, number, halves, half, way, False).wait_recv()

    for d in range(REACH + 1):
        for index, (p, q) in enumerate(PLACES[d]):
            tile = STARTS[d] + index
            out_ref[p, d * OWN + q - p] = part[x, core, tile] + (ring[0, tile] + ring[1, tile])


def tiles(dosages):
    half_tile = (PANEL // 2, PANEL)
    dma = pltpu.SemaphoreType.DMA
    return pl.pallas_call(
        tiles_kernel,
        out_shape=jax.ShapeDtypeStruct((OWN, WMAX + 1) + half_tile, jnp.float32),
        in_specs=[pl.BlockSpec(memory_space=pltpu.HBM)],
        out_specs=pl.BlockSpec(memory_space=pltpu.VMEM),
        scratch_shapes=[
            pltpu.VMEM((GROUPS * SIDE, ROWS, CHUNK), jnp.bfloat16),
            pltpu.VMEM((CHUNKS, GROUPS, ROWS, CHUNK), jnp.bfloat16),
            pltpu.VMEM((GROUPS * SIDE + REACH, 2 * OWN, PANEL), jnp.float32),
            pltpu.VMEM((GROUPS, CHUNKS, 2 * OWN, PANEL), jnp.float32),
            pltpu.VMEM((8, CHUNKS, 2 * OWN, PANEL), jnp.float32),
            pltpu.VMEM((CHUNKS, 2 * OWN, PANEL), jnp.float32),
            pltpu.VMEM((CHUNKS, LOCAL, CHUNK), jnp.bfloat16),
            pltpu.VMEM((SIDE, CHUNK, LOCAL), jnp.bfloat16),
            pltpu.VMEM((SIDE, 2, TILES) + half_tile, jnp.float32),
            pltpu.VMEM((SIDE, TILES) + half_tile, jnp.float32),
            pltpu.VMEM((2, TILES) + half_tile, jnp.float32),
            pltpu.VMEM((2, TILES) + half_tile, jnp.float32),
            dma((GROUPS * SIDE,)),
            dma((len(STEPS),)),
            dma((len(STEPS), GROUPS)),
            dma((len(STEPS), GROUPS)),
            dma((GROUPS,)),
            dma((GROUPS,)),
            dma((7,)),
            dma((7,)),
            dma((SIDE, REACH + 2)),
            dma((SIDE, REACH + 2)),
            dma((2, REACH + 2)),
            dma((SIDE, REACH + 2, 2)),
            dma((2, REACH + 2, 2)),
        ],
        compiler_params=pltpu.CompilerParams(
            collective_id=0, has_side_effects=True, vmem_limit_bytes=52 * 1024 * 1024
        ),
        name="tiles",
    )(dosages)


def per_device(dosages, band_width):
    band_tiles = tiles(dosages)
    offsets = jnp.arange(WMAX + 1, dtype=jnp.int32)
    panel_count = OWN * lax.axis_size("var")
    global_panel = lax.axis_index("var") * OWN + jnp.arange(OWN, dtype=jnp.int32)
    in_band = (offsets[None, :] <= band_width[:, None]) & (
        global_panel[:, None] + offsets[None, :] < panel_count
    )
    return jnp.where(in_band[:, :, None, None], band_tiles * (1.0 / SAMPLES), 0.0)


def solution(mesh):
    in_specs = (P(("var", "samp"), None), P("var"))
    out_specs = P("var", None, "samp", None)
    return jax.shard_map(
        per_device, mesh=mesh, in_specs=in_specs, out_specs=out_specs, check_vma=False
    )
```

```python
import jax
import jax.numpy as jnp
from jax import lax
from jax.experimental import pallas as pl
from jax.experimental.pallas import tpu as pltpu
from jax.sharding import PartitionSpec as P

MESH = pl.DeviceIdType.MESH
WMAX = 8
PANEL = 128
SIDE = 4
GROUPS = SIDE * SIDE
OWN = 4
CHUNK = OWN * PANEL
REACH = WMAX // OWN
CHUNKS = SIDE + REACH
ROWS = 64
LOCAL = GROUPS * ROWS
BLOCK = 2 * PANEL
STEPS = [(chunk, 0, CHUNK) for chunk in range(CHUNKS - 1)] + [(CHUNKS - 1, first, BLOCK) for first in (0, BLOCK)]
AHEAD = 24
SAMPLES = 8192
PLACES = [
    [(p, q) for q in range(OWN) for p in range(OWN) if 0 <= d * OWN + q - p <= WMAX] for d in range(REACH + 1)
]
STARTS = [sum(len(places) for places in PLACES[:d]) for d in range(REACH + 2)]
TILES = STARTS[-1]


def position():
    var = lax.axis_index("var")
    return var // SIDE, lax.rem(var, SIDE), lax.axis_index("samp")


def tiles_kernel(
    dos_ref, out_ref, staged, received, moments, gathered, sums, totals, standard, turned, part, twin, relay, ring,
    stage_sem, own_sem, swap_send, swap_recv, group_send, group_recv, stat_send, stat_recv, twin_send, twin_recv, relay_recv, ring_send, ring_recv,
):
    group, x, core = position()
    z, y = group // SIDE, lax.rem(group, SIDE)

    def stage(index):
        first = pl.multiple_of(index * CHUNK, CHUNK)
        return pltpu.make_async_copy(dos_ref.at[:, pl.ds(first, CHUNK)], staged.at[index], stage_sem.at[index])

    def stage_begin(index, carry):
        stage(index).start()
        return carry

    def stage_end(index, carry):
        stage(index).wait()
        return carry

    lax.fori_loop(0, GROUPS * SIDE, stage_begin, 0)

    peers = []
    for dx in range(SIDE):
        for dc in range(2):
            if dx or dc:
                peer_x, peer_c = lax.rem(x + dx, SIDE), lax.rem(core + dc, 2)
                peers.append((group * SIDE + peer_x, peer_c))

    def group_at(offset):
        return lax.rem(z + offset // SIDE, SIDE) * SIDE + lax.rem(y + lax.rem(offset, SIDE), SIDE)

    barrier = pltpu.get_barrier_semaphore()
    for offset in range(1, GROUPS):
        pl.semaphore_signal(
            barrier, inc=1, device_id=(group_at(offset) * SIDE + x, core), device_id_type=MESH
        )
    for peer in peers:
        pl.semaphore_signal(barrier, inc=1, device_id=peer, device_id_type=MESH)
    pl.semaphore_wait(barrier, GROUPS - 1 + len(peers))

    def columns_of(other, chunk, first, count):
        top = lax.rem(other * SIDE + chunk, GROUPS * SIDE) * CHUNK + first
        return dos_ref.at[:, pl.ds(pl.multiple_of(top, BLOCK), count)]

    shift = z * 5 + y * 3 + core * 8

    def swap(index):
        step, turn = divmod(index, GROUPS - 1)
        chunk, first, count = STEPS[step]
        columns = pl.ds(first, count)
        offset = 1 + lax.rem(turn * 7 + shift, GROUPS - 1)
        other = group_at(offset)
        return pltpu.make_async_remote_copy(
            src_ref=columns_of(other, chunk, first, count),
            dst_ref=received.at[chunk, offset, :, columns],
            send_sem=swap_send.at[step, offset],
            recv_sem=swap_recv.at[step, offset],
            device_id=(other * SIDE + x, core),
            device_id_type=MESH,
        )

    swaps = [swap(index) for index in range(len(STEPS) * (GROUPS - 1))]
    started = [0]

    def pump(count):
        for index in range(started[0], min(started[0] + count, len(swaps))):
            if index >= AHEAD:
                swaps[index - AHEAD].wait_send()
            swaps[index].start()
            started[0] = index + 1

    def own_copy(step):
        chunk, first, count = STEPS[step]
        columns = pl.ds(first, count)
        return pltpu.make_async_copy(
            columns_of(group, chunk, first, count),
            received.at[chunk, 0, :, columns],
            own_sem.at[step],
        )

    def swap_end(step):
        own_copy(step).wait()
        for copy in swaps[step * (GROUPS - 1):(step + 1) * (GROUPS - 1)]:
            copy.wait_recv()

    def local_moments():
        def chunk_moments(index, carry):
            values = staged[index].astype(jnp.float32).reshape(ROWS // 8, 8, CHUNK)
            for row, total in enumerate((jnp.sum(values, 0), jnp.sum(values * values, 0))):
                total = jnp.sum(total, 0, keepdims=True)
                for q in range(OWN):
                    moments[index, row * OWN + q:row * OWN + q + 1, :] = total[:, q * PANEL:(q + 1) * PANEL]
            return carry

        lax.fori_loop(0, GROUPS * SIDE, chunk_moments, 0)
        for extra in range(REACH):
            moments[GROUPS * SIDE + extra] = moments[extra]

    def group_moments_begin():
        gathered[0] = moments[pl.ds(group * SIDE, CHUNKS)]
        copies = []
        for offset in range(1, GROUPS):
            other = group_at(offset)
            copy = pltpu.make_async_remote_copy(
                src_ref=moments.at[pl.ds(other * SIDE, CHUNKS)],
                dst_ref=gathered.at[offset],
                send_sem=group_send.at[offset],
                recv_sem=group_recv.at[offset],
                device_id=(other * SIDE + x, core),
                device_id_type=MESH,
            )
            copy.start()
            copies.append(copy)
        return copies

    def ring_moments_begin(copies):
        for copy in copies:
            copy.wait()
        sums[0] = jnp.sum(gathered[...], 0)
        copies = []
        for index, peer in enumerate(peers):
            copy = pltpu.make_async_remote_copy(
                src_ref=sums.at[0],
                dst_ref=sums.at[index + 1],
                send_sem=stat_send.at[index],
                recv_sem=stat_recv.at[index],
                device_id=peer,
                device_id_type=MESH,
            )
            copy.start()
            copies.append(copy)
        return copies

    def ring_moments_end(copies):
        for copy in copies:
            copy.wait()
        totals[...] = jnp.sum(sums[...], 0)

    def standardize(step):
        chunk, start, count = STEPS[step]
        columns = pl.ds(start, count)
        panels = range(start // PANEL, (start + count) // PANEL)
        first, second = totals[chunk, 0:OWN], totals[chunk, OWN:2 * OWN]
        mean = first * (1.0 / SAMPLES)
        inv_scale = lax.rsqrt(second * (1.0 / SAMPLES) - mean * mean + 1e-05)
        mean = jnp.concatenate([mean[q:q + 1] for q in panels], axis=1)
        inv_scale = jnp.concatenate([inv_scale[q:q + 1] for q in panels], axis=1)

        def block_standard(block, carry):
            rows = pl.ds(pl.multiple_of(block * ROWS, ROWS), ROWS)
            values = received[chunk, block, :, columns].astype(jnp.float32)
            standard[chunk, rows, columns] = ((values - mean) * inv_scale).astype(jnp.bfloat16)
            return carry

        lax.fori_loop(0, GROUPS, block_standard, 0)
        if chunk < SIDE:
            turned[chunk] = standard[chunk].T

    def pieces_of(step):
        chunk, start, count = STEPS[step]
        pieces = []
        for d in range(REACH + 1):
            if 0 <= chunk - d < SIDE:
                inside = [
                    index for index, (p, q) in enumerate(PLACES[d])
                    if start // PANEL <= q < (start + count) // PANEL
                ]
                pieces.append((chunk - d, d, d + (start > 0), STARTS[d] + inside[0], len(inside)))
        return pieces

    def twin_copy(rows_chunk, number, first, count):
        which = pl.ds(first, count)
        return pltpu.make_async_remote_copy(
            src_ref=part.at[rows_chunk, 1 - core, which],
            dst_ref=twin.at[rows_chunk, which],
            send_sem=twin_send.at[rows_chunk, number],
            recv_sem=twin_recv.at[rows_chunk, number],
            device_id=(group * SIDE + x, 1 - core),
            device_id_type=MESH,
        )

    def multiply(step):
        chunk, start, columns = STEPS[step]
        for rows_chunk, d, number, first, count in pieces_of(step):
            for pp in range(OWN // 2):
                for qq in range(start // BLOCK, (start + columns) // BLOCK):
                    inside = [
                        (p, q) for p in range(2) for q in range(2) if (2 * pp + p, 2 * qq + q) in PLACES[d]
                    ]
                    if not inside:
                        continue
                    block = jnp.dot(
                        turned[rows_chunk, pp * BLOCK:(pp + 1) * BLOCK, :],
                        standard[chunk, :, qq * BLOCK:(qq + 1) * BLOCK],
                        preferred_element_type=jnp.float32,
                    )
                    for p, q in inside:
                        tile = STARTS[d] + PLACES[d].index((2 * pp + p, 2 * qq + q))
                        for half in range(2):
                            top = p * PANEL + half * (PANEL // 2)
                            part[rows_chunk, half, tile] = block[
                                top:top + PANEL // 2, q * PANEL:(q + 1) * PANEL
                            ]
            twin_copy(rows_chunk, number, first, count).start()

    def halves_of(first, count):
        upper = (count + 1) // 2
        return pl.ds(first, upper), pl.ds(first + upper, count - upper)

    def line_copy(rows_chunk, number, halves, half, way, relayed):
        which = halves[half]
        return pltpu.make_async_remote_copy(
            src_ref=part.at[rows_chunk, core, which],
            dst_ref=(relay if relayed else ring).at[way, which],
            send_sem=ring_send.at[rows_chunk, number, half],
            recv_sem=relay_recv.at[way, number] if relayed else ring_recv.at[way, number, half],
            device_id=(group * SIDE + lax.rem(x + 1 + 2 * way, SIDE), core),
            device_id_type=MESH,
        )

    def reduce(step):
        for rows_chunk, d, number, first, count in pieces_of(step):
            which = pl.ds(first, count)
            halves = halves_of(first, count)
            twin_copy(rows_chunk, number, first, count).wait()
            part[rows_chunk, core, which] = part[rows_chunk, core, which] + twin[rows_chunk, which]
            distance = lax.rem(rows_chunk - x + SIDE, SIDE)

            @pl.when(distance == 2)
            def _():
                line_copy(rows_chunk, number, halves, 0, 0, True).start()
                line_copy(rows_chunk, number, halves, 1, 1, True).start()

            @pl.when(distance == 1)
            def _():
                line_copy(rows_chunk, number, halves, 1, 0, False).start()

            @pl.when(distance == 3)
            def _():
                line_copy(rows_chunk, number, halves, 0, 1, False).start()

            pump(4)

        pump(3)
        for rows_chunk, d, number, first, count in pieces_of(step):
            halves = halves_of(first, count)
            distance = lax.rem(rows_chunk - x + SIDE, SIDE)
            for way in range(2):

                @pl.when(distance == 1 + 2 * way)
                def _():
                    which = halves[way]
                    line_copy(rows_chunk, number, halves, way, way, True).wait_recv()
                    part[rows_chunk, core, which] = part[rows_chunk, core, which] + relay[way, which]
                    line_copy(rows_chunk, number, halves, way, way, False).start()

    pump(8)
    for step in range(len(STEPS)):
        own_copy(step).start()
    lax.fori_loop(0, GROUPS * SIDE, stage_end, 0)
    local_moments()
    copies = group_moments_begin()
    pump(8)
    copies = ring_moments_begin(copies)
    pump(8)
    ring_moments_end(copies)
    for step in range(len(STEPS)):
        pump((step + 1) * (GROUPS - 1) + AHEAD - started[0])
        swap_end(step)
        standardize(step)
        multiply(step)
        pump(2)
        reduce(step)
    for copy in swaps[-AHEAD:]:
        copy.wait_send()

    for step in range(len(STEPS)):
        for rows_chunk, d, number, first, count in pieces_of(step):
            halves = halves_of(first, count)

            @pl.when(x != rows_chunk)
            def _():
                for half in range(2):
                    line_copy(rows_chunk, number, halves, half, 0, False).wait_send()

            @pl.when(x == rows_chunk)
            def _():
                for way in range(2):
                    for half in range(2):
                        line_copy(rows_chunk, number, halves, half, way, False).wait_recv()

    for d in range(REACH + 1):
        for index, (p, q) in enumerate(PLACES[d]):
            tile = STARTS[d] + index
            out_ref[p, d * OWN + q - p] = part[x, core, tile] + (ring[0, tile] + ring[1, tile])


def tiles(dosages):
    half_tile = (PANEL // 2, PANEL)
    dma = pltpu.SemaphoreType.DMA
    return pl.pallas_call(
        tiles_kernel,
        out_shape=jax.ShapeDtypeStruct((OWN, WMAX + 1) + half_tile, jnp.float32),
        in_specs=[pl.BlockSpec(memory_space=pltpu.HBM)],
        out_specs=pl.BlockSpec(memory_space=pltpu.VMEM),
        scratch_shapes=[
            pltpu.VMEM((GROUPS * SIDE, ROWS, CHUNK), jnp.bfloat16),
            pltpu.VMEM((CHUNKS, GROUPS, ROWS, CHUNK), jnp.bfloat16),
            pltpu.VMEM((GROUPS * SIDE + REACH, 2 * OWN, PANEL), jnp.float32),
            pltpu.VMEM((GROUPS, CHUNKS, 2 * OWN, PANEL), jnp.float32),
            pltpu.VMEM((8, CHUNKS, 2 * OWN, PANEL), jnp.float32),
            pltpu.VMEM((CHUNKS, 2 * OWN, PANEL), jnp.float32),
            pltpu.VMEM((CHUNKS, LOCAL, CHUNK), jnp.bfloat16),
            pltpu.VMEM((SIDE, CHUNK, LOCAL), jnp.bfloat16),
            pltpu.VMEM((SIDE, 2, TILES) + half_tile, jnp.float32),
            pltpu.VMEM((SIDE, TILES) + half_tile, jnp.float32),
            pltpu.VMEM((2, TILES) + half_tile, jnp.float32),
            pltpu.VMEM((2, TILES) + half_tile, jnp.float32),
            dma((GROUPS * SIDE,)),
            dma((len(STEPS),)),
            dma((len(STEPS), GROUPS)),
            dma((len(STEPS), GROUPS)),
            dma((GROUPS,)),
            dma((GROUPS,)),
            dma((7,)),
            dma((7,)),
            dma((SIDE, REACH + 2)),
            dma((SIDE, REACH + 2)),
            dma((2, REACH + 2)),
            dma((SIDE, REACH + 2, 2)),
            dma((2, REACH + 2, 2)),
        ],
        compiler_params=pltpu.CompilerParams(
            collective_id=0, has_side_effects=True, vmem_limit_bytes=52 * 1024 * 1024
        ),
        name="tiles",
    )(dosages)


def per_device(dosages, band_width):
    band_tiles = tiles(dosages)
    offsets = jnp.arange(WMAX + 1, dtype=jnp.int32)
    panel_count = OWN * lax.axis_size("var")
    global_panel = lax.axis_index("var") * OWN + jnp.arange(OWN, dtype=jnp.int32)
    in_band = (offsets[None, :] <= band_width[:, None]) & (
        global_panel[:, None] + offsets[None, :] < panel_count
    )
    return jnp.where(in_band[:, :, None, None], band_tiles * (1.0 / SAMPLES), 0.0)


def solution(mesh):
    in_specs = (P(("var", "samp"), None), P("var"))
    out_specs = P("var", None, "samp", None)
    return jax.shard_map(
        per_device, mesh=mesh, in_specs=in_specs, out_specs=out_specs, check_vma=False
    )
```

```python
import jax
import jax.numpy as jnp
from jax import lax
from jax.experimental import pallas as pl
from jax.experimental.pallas import tpu as pltpu
from jax.sharding import PartitionSpec as P

MESH = pl.DeviceIdType.MESH
WMAX = 8
PANEL = 128
SIDE = 4
GROUPS = SIDE * SIDE
OWN = 4
CHUNK = OWN * PANEL
REACH = WMAX // OWN
CHUNKS = SIDE + REACH
ROWS = 64
LOCAL = GROUPS * ROWS
BLOCK = 2 * PANEL
STEPS = [(chunk, 0, CHUNK) for chunk in range(CHUNKS)]
AHEAD = 24
ORDER = [10, 15, 1, 4, 6, 3, 9, 12, 11, 14, 7, 13, 2, 8, 5]
PARTNER = [1, 0, 3, 2, 5, 4, 7, 6, 9, 8, 11, 10, 13, 12, 14]
SAMPLES = 8192
PLACES = [
    [(p, q) for q in range(OWN) for p in range(OWN) if 0 <= d * OWN + q - p <= WMAX] for d in range(REACH + 1)
]
STARTS = [sum(len(places) for places in PLACES[:d]) for d in range(REACH + 2)]
TILES = STARTS[-1]


def position():
    var = lax.axis_index("var")
    return var // SIDE, lax.rem(var, SIDE), lax.axis_index("samp")


def tiles_kernel(
    dos_ref, out_ref, staged, received, moments, gathered, sums, totals, standard, turned, part, twin, relay, ring,
    stage_sem, own_sem, swap_send, swap_recv, group_send, group_recv, stat_send, stat_recv, twin_send, twin_recv, relay_recv, ring_send, ring_recv,
):
    group, x, core = position()
    z, y = group // SIDE, lax.rem(group, SIDE)

    def stage(index):
        first = pl.multiple_of(index * CHUNK, CHUNK)
        return pltpu.make_async_copy(dos_ref.at[:, pl.ds(first, CHUNK)], staged.at[index], stage_sem.at[index])

    def stage_begin(index, carry):
        stage(index).start()
        return carry

    def stage_end(index, carry):
        stage(index).wait()
        return carry

    lax.fori_loop(0, GROUPS * SIDE, stage_begin, 0)

    peers = []
    for dx in range(SIDE):
        for dc in range(2):
            if dx or dc:
                peer_x, peer_c = lax.rem(x + dx, SIDE), lax.rem(core + dc, 2)
                peers.append((group * SIDE + peer_x, peer_c))

    def group_at(offset):
        return lax.rem(z + offset // SIDE, SIDE) * SIDE + lax.rem(y + lax.rem(offset, SIDE), SIDE)

    barrier = pltpu.get_barrier_semaphore()
    for offset in range(1, GROUPS):
        pl.semaphore_signal(
            barrier, inc=1, device_id=(group_at(offset) * SIDE + x, core), device_id_type=MESH
        )
    for peer in peers:
        pl.semaphore_signal(barrier, inc=1, device_id=peer, device_id_type=MESH)
    pl.semaphore_wait(barrier, GROUPS - 1 + len(peers))

    def columns_of(other, chunk, first, count):
        top = lax.rem(other * SIDE + chunk, GROUPS * SIDE) * CHUNK + first
        return dos_ref.at[:, pl.ds(pl.multiple_of(top, BLOCK), count)]

    def swap(index):
        step, turn = divmod(index, GROUPS - 1)
        chunk, first, count = STEPS[step]
        columns = pl.ds(first, count)
        offset = ORDER[turn] + core * (ORDER[PARTNER[turn]] - ORDER[turn])
        other = group_at(offset)
        return pltpu.make_async_remote_copy(
            src_ref=columns_of(other, chunk, first, count),
            dst_ref=received.at[chunk, offset, :, columns],
            send_sem=swap_send.at[step, offset],
            recv_sem=swap_recv.at[step, offset],
            device_id=(other * SIDE + x, core),
            device_id_type=MESH,
        )

    swaps = [swap(index) for index in range(len(STEPS) * (GROUPS - 1))]
    started = [0]

    def pump(count):
        for index in range(started[0], min(started[0] + count, len(swaps))):
            if index >= AHEAD:
                swaps[index - AHEAD].wait_send()
            swaps[index].start()
            started[0] = index + 1

    def own_copy(step):
        chunk, first, count = STEPS[step]
        columns = pl.ds(first, count)
        return pltpu.make_async_copy(
            columns_of(group, chunk, first, count),
            received.at[chunk, 0, :, columns],
            own_sem.at[step],
        )

    def swap_end(step):
        own_copy(step).wait()
        for copy in swaps[step * (GROUPS - 1):(step + 1) * (GROUPS - 1)]:
            copy.wait_recv()

    def local_moments():
        def chunk_moments(index, carry):
            values = staged[index].astype(jnp.float32).reshape(ROWS // 8, 8, CHUNK)
            for row, total in enumerate((jnp.sum(values, 0), jnp.sum(values * values, 0))):
                total = jnp.sum(total, 0, keepdims=True)
                for q in range(OWN):
                    moments[index, row * OWN + q:row * OWN + q + 1, :] = total[:, q * PANEL:(q + 1) * PANEL]
            return carry

        lax.fori_loop(0, GROUPS * SIDE, chunk_moments, 0)
        for extra in range(REACH):
            moments[GROUPS * SIDE + extra] = moments[extra]

    def group_moments_begin():
        gathered[0] = moments[pl.ds(group * SIDE, CHUNKS)]
        copies = []
        for offset in range(1, GROUPS):
            other = group_at(offset)
            copy = pltpu.make_async_remote_copy(
                src_ref=moments.at[pl.ds(other * SIDE, CHUNKS)],
                dst_ref=gathered.at[offset],
                send_sem=group_send.at[offset],
                recv_sem=group_recv.at[offset],
                device_id=(other * SIDE + x, core),
                device_id_type=MESH,
            )
            copy.start()
            copies.append(copy)
        return copies

    def ring_moments_begin(copies):
        for copy in copies:
            copy.wait()
        sums[0] = jnp.sum(gathered[...], 0)
        copies = []
        for index, peer in enumerate(peers):
            copy = pltpu.make_async_remote_copy(
                src_ref=sums.at[0],
                dst_ref=sums.at[index + 1],
                send_sem=stat_send.at[index],
                recv_sem=stat_recv.at[index],
                device_id=peer,
                device_id_type=MESH,
            )
            copy.start()
            copies.append(copy)
        return copies

    def ring_moments_end(copies):
        for copy in copies:
            copy.wait()
        totals[...] = jnp.sum(sums[...], 0)

    def standardize(step):
        chunk, start, count = STEPS[step]
        columns = pl.ds(start, count)
        panels = range(start // PANEL, (start + count) // PANEL)
        first, second = totals[chunk, 0:OWN], totals[chunk, OWN:2 * OWN]
        mean = first * (1.0 / SAMPLES)
        inv_scale = lax.rsqrt(second * (1.0 / SAMPLES) - mean * mean + 1e-05)
        mean = jnp.concatenate([mean[q:q + 1] for q in panels], axis=1)
        inv_scale = jnp.concatenate([inv_scale[q:q + 1] for q in panels], axis=1)

        def block_standard(block, carry):
            rows = pl.ds(pl.multiple_of(block * ROWS, ROWS), ROWS)
            values = received[chunk, block, :, columns].astype(jnp.float32)
            standard[chunk, rows, columns] = ((values - mean) * inv_scale).astype(jnp.bfloat16)
            return carry

        lax.fori_loop(0, GROUPS, block_standard, 0)
        if chunk < SIDE:
            turned[chunk] = standard[chunk].T

    def pieces_of(step):
        chunk, start, count = STEPS[step]
        pieces = []
        for d in range(REACH + 1):
            if 0 <= chunk - d < SIDE:
                inside = [
                    index for index, (p, q) in enumerate(PLACES[d])
                    if start // PANEL <= q < (start + count) // PANEL
                ]
                pieces.append((chunk - d, d, d + (start > 0), STARTS[d] + inside[0], len(inside)))
        return pieces

    def twin_copy(rows_chunk, number, first, count):
        which = pl.ds(first, count)
        return pltpu.make_async_remote_copy(
            src_ref=part.at[rows_chunk, 1 - core, which],
            dst_ref=twin.at[rows_chunk, which],
            send_sem=twin_send.at[rows_chunk, number],
            recv_sem=twin_recv.at[rows_chunk, number],
            device_id=(group * SIDE + x, 1 - core),
            device_id_type=MESH,
        )

    def multiply(step):
        chunk, start, columns = STEPS[step]
        for rows_chunk, d, number, first, count in pieces_of(step):
            for pp in range(OWN // 2):
                for qq in range(start // BLOCK, (start + columns) // BLOCK):
                    inside = [
                        (p, q) for p in range(2) for q in range(2) if (2 * pp + p, 2 * qq + q) in PLACES[d]
                    ]
                    if not inside:
                        continue
                    block = jnp.dot(
                        turned[rows_chunk, pp * BLOCK:(pp + 1) * BLOCK, :],
                        standard[chunk, :, qq * BLOCK:(qq + 1) * BLOCK],
                        preferred_element_type=jnp.float32,
                    )
                    for p, q in inside:
                        tile = STARTS[d] + PLACES[d].index((2 * pp + p, 2 * qq + q))
                        for half in range(2):
                            top = p * PANEL + half * (PANEL // 2)
                            part[rows_chunk, half, tile] = block[
                                top:top + PANEL // 2, q * PANEL:(q + 1) * PANEL
                            ]
            twin_copy(rows_chunk, number, first, count).start()

    def halves_of(first, count):
        upper = (count + 1) // 2
        return pl.ds(first, upper), pl.ds(first + upper, count - upper)

    def line_copy(rows_chunk, number, halves, half, way, relayed):
        which = halves[half]
        return pltpu.make_async_remote_copy(
            src_ref=part.at[rows_chunk, core, which],
            dst_ref=(relay if relayed else ring).at[way, which],
            send_sem=ring_send.at[rows_chunk, number, half],
            recv_sem=relay_recv.at[way, number] if relayed else ring_recv.at[way, number, half],
            device_id=(group * SIDE + lax.rem(x + 1 + 2 * way, SIDE), core),
            device_id_type=MESH,
        )

    def reduce(step):
        for rows_chunk, d, number, first, count in pieces_of(step):
            which = pl.ds(first, count)
            halves = halves_of(first, count)
            twin_copy(rows_chunk, number, first, count).wait()
            part[rows_chunk, core, which] = part[rows_chunk, core, which] + twin[rows_chunk, which]
            distance = lax.rem(rows_chunk - x + SIDE, SIDE)

            @pl.when(distance == 2)
            def _():
                line_copy(rows_chunk, number, halves, 0, 0, True).start()
                line_copy(rows_chunk, number, halves, 1, 1, True).start()

            @pl.when(distance == 1)
            def _():
                line_copy(rows_chunk, number, halves, 1, 0, False).start()

            @pl.when(distance == 3)
            def _():
                line_copy(rows_chunk, number, halves, 0, 1, False).start()

            pump(4)

        pump(3)
        for rows_chunk, d, number, first, count in pieces_of(step):
            halves = halves_of(first, count)
            distance = lax.rem(rows_chunk - x + SIDE, SIDE)
            for way in range(2):

                @pl.when(distance == 1 + 2 * way)
                def _():
                    which = halves[way]
                    line_copy(rows_chunk, number, halves, way, way, True).wait_recv()
                    part[rows_chunk, core, which] = part[rows_chunk, core, which] + relay[way, which]
                    line_copy(rows_chunk, number, halves, way, way, False).start()

    pump(8)
    for step in range(len(STEPS)):
        own_copy(step).start()
    lax.fori_loop(0, GROUPS * SIDE, stage_end, 0)
    local_moments()
    copies = group_moments_begin()
    pump(8)
    copies = ring_moments_begin(copies)
    pump(8)
    ring_moments_end(copies)
    for step in range(len(STEPS)):
        pump((step + 1) * (GROUPS - 1) + AHEAD - started[0])
        swap_end(step)
        standardize(step)
        multiply(step)
        pump(2)
        reduce(step)
    for copy in swaps[-AHEAD:]:
        copy.wait_send()

    for step in range(len(STEPS)):
        for rows_chunk, d, number, first, count in pieces_of(step):
            halves = halves_of(first, count)

            @pl.when(x != rows_chunk)
            def _():
                for half in range(2):
                    line_copy(rows_chunk, number, halves, half, 0, False).wait_send()

            @pl.when(x == rows_chunk)
            def _():
                for way in range(2):
                    for half in range(2):
                        line_copy(rows_chunk, number, halves, half, way, False).wait_recv()

    for d in range(REACH + 1):
        for index, (p, q) in enumerate(PLACES[d]):
            tile = STARTS[d] + index
            out_ref[p, d * OWN + q - p] = part[x, core, tile] + (ring[0, tile] + ring[1, tile])


def tiles(dosages):
    half_tile = (PANEL // 2, PANEL)
    dma = pltpu.SemaphoreType.DMA
    return pl.pallas_call(
        tiles_kernel,
        out_shape=jax.ShapeDtypeStruct((OWN, WMAX + 1) + half_tile, jnp.float32),
        in_specs=[pl.BlockSpec(memory_space=pltpu.HBM)],
        out_specs=pl.BlockSpec(memory_space=pltpu.VMEM),
        scratch_shapes=[
            pltpu.VMEM((GROUPS * SIDE, ROWS, CHUNK), jnp.bfloat16),
            pltpu.VMEM((CHUNKS, GROUPS, ROWS, CHUNK), jnp.bfloat16),
            pltpu.VMEM((GROUPS * SIDE + REACH, 2 * OWN, PANEL), jnp.float32),
            pltpu.VMEM((GROUPS, CHUNKS, 2 * OWN, PANEL), jnp.float32),
            pltpu.VMEM((8, CHUNKS, 2 * OWN, PANEL), jnp.float32),
            pltpu.VMEM((CHUNKS, 2 * OWN, PANEL), jnp.float32),
            pltpu.VMEM((CHUNKS, LOCAL, CHUNK), jnp.bfloat16),
            pltpu.VMEM((SIDE, CHUNK, LOCAL), jnp.bfloat16),
            pltpu.VMEM((SIDE, 2, TILES) + half_tile, jnp.float32),
            pltpu.VMEM((SIDE, TILES) + half_tile, jnp.float32),
            pltpu.VMEM((2, TILES) + half_tile, jnp.float32),
            pltpu.VMEM((2, TILES) + half_tile, jnp.float32),
            dma((GROUPS * SIDE,)),
            dma((len(STEPS),)),
            dma((len(STEPS), GROUPS)),
            dma((len(STEPS), GROUPS)),
            dma((GROUPS,)),
            dma((GROUPS,)),
            dma((7,)),
            dma((7,)),
            dma((SIDE, REACH + 2)),
            dma((SIDE, REACH + 2)),
            dma((2, REACH + 2)),
            dma((SIDE, REACH + 2, 2)),
            dma((2, REACH + 2, 2)),
        ],
        compiler_params=pltpu.CompilerParams(
            collective_id=0, has_side_effects=True, vmem_limit_bytes=52 * 1024 * 1024
        ),
        name="tiles",
    )(dosages)


def per_device(dosages, band_width):
    band_tiles = tiles(dosages)
    offsets = jnp.arange(WMAX + 1, dtype=jnp.int32)
    panel_count = OWN * lax.axis_size("var")
    global_panel = lax.axis_index("var") * OWN + jnp.arange(OWN, dtype=jnp.int32)
    in_band = (offsets[None, :] <= band_width[:, None]) & (
        global_panel[:, None] + offsets[None, :] < panel_count
    )
    return jnp.where(in_band[:, :, None, None], band_tiles * (1.0 / SAMPLES), 0.0)


def solution(mesh):
    in_specs = (P(("var", "samp"), None), P("var"))
    out_specs = P("var", None, "samp", None)
    return jax.shard_map(
        per_device, mesh=mesh, in_specs=in_specs, out_specs=out_specs, check_vma=False
    )
```

```python
import jax
import jax.numpy as jnp
from jax import lax
from jax.experimental import pallas as pl
from jax.experimental.pallas import tpu as pltpu
from jax.sharding import PartitionSpec as P

MESH = pl.DeviceIdType.MESH
WMAX = 8
PANEL = 128
SIDE = 4
GROUPS = SIDE * SIDE
OWN = 4
CHUNK = OWN * PANEL
REACH = WMAX // OWN
CHUNKS = SIDE + REACH
ROWS = 64
LOCAL = GROUPS * ROWS
BLOCK = 2 * PANEL
STEPS = [(chunk, 0, CHUNK) for chunk in range(CHUNKS)]
AHEAD = 24
ORDER = [10, 15, 1, 4, 6, 3, 9, 12, 11, 14, 7, 13, 2, 8, 5]
PARTNER = [1, 0, 3, 2, 5, 4, 7, 6, 9, 8, 11, 10, 13, 12, 14]
SAMPLES = 8192
PLACES = [
    [(p, q) for q in range(OWN) for p in range(OWN) if 0 <= d * OWN + q - p <= WMAX] for d in range(REACH + 1)
]
STARTS = [sum(len(places) for places in PLACES[:d]) for d in range(REACH + 2)]
TILES = STARTS[-1]


def position():
    var = lax.axis_index("var")
    return var // SIDE, lax.rem(var, SIDE), lax.axis_index("samp")


def tiles_kernel(
    dos_ref, out_ref, staged, received, moments, gathered, sums, totals, standard, turned, part, twin, relay, ring,
    stage_sem, own_sem, swap_send, swap_recv, group_send, group_recv, stat_send, stat_recv, twin_send, twin_recv, relay_recv, ring_send, ring_recv,
):
    group, x, core = position()
    z, y = group // SIDE, lax.rem(group, SIDE)

    def stage(index):
        first = pl.multiple_of(index * CHUNK, CHUNK)
        return pltpu.make_async_copy(dos_ref.at[:, pl.ds(first, CHUNK)], staged.at[index], stage_sem.at[index])

    def stage_begin(index, carry):
        stage(index).start()
        return carry

    def stage_end(index, carry):
        stage(index).wait()
        return carry

    lax.fori_loop(0, GROUPS * SIDE, stage_begin, 0)

    peers = []
    for dx in range(SIDE):
        for dc in range(2):
            if dx or dc:
                peer_x, peer_c = lax.rem(x + dx, SIDE), lax.rem(core + dc, 2)
                peers.append((group * SIDE + peer_x, peer_c))

    def group_at(offset):
        return lax.rem(z + offset // SIDE, SIDE) * SIDE + lax.rem(y + lax.rem(offset, SIDE), SIDE)

    barrier = pltpu.get_barrier_semaphore()
    for offset in range(1, GROUPS):
        pl.semaphore_signal(
            barrier, inc=1, device_id=(group_at(offset) * SIDE + x, core), device_id_type=MESH
        )
    for peer in peers:
        pl.semaphore_signal(barrier, inc=1, device_id=peer, device_id_type=MESH)
    pl.semaphore_wait(barrier, GROUPS - 1 + len(peers))

    def columns_of(other, chunk, first, count):
        top = lax.rem(other * SIDE + chunk, GROUPS * SIDE) * CHUNK + first
        return dos_ref.at[:, pl.ds(pl.multiple_of(top, BLOCK), count)]

    def swap(index):
        step, turn = divmod(index, GROUPS - 1)
        chunk, first, count = STEPS[step]
        columns = pl.ds(first, count)
        offset = ORDER[turn] + core * (ORDER[PARTNER[turn]] - ORDER[turn])
        other = group_at(offset)
        return pltpu.make_async_remote_copy(
            src_ref=columns_of(other, chunk, first, count),
            dst_ref=received.at[chunk, offset, :, columns],
            send_sem=swap_send.at[step, offset],
            recv_sem=swap_recv.at[step, offset],
            device_id=(other * SIDE + x, core),
            device_id_type=MESH,
        )

    swaps = [swap(index) for index in range(len(STEPS) * (GROUPS - 1))]
    started = [0]

    def pump(count):
        for index in range(started[0], min(started[0] + count, len(swaps))):
            if index >= AHEAD:
                swaps[index - AHEAD].wait_send()
            swaps[index].start()
            started[0] = index + 1

    def own_copy(step):
        chunk, first, count = STEPS[step]
        columns = pl.ds(first, count)
        return pltpu.make_async_copy(
            columns_of(group, chunk, first, count),
            received.at[chunk, 0, :, columns],
            own_sem.at[step],
        )

    def swap_end(step):
        own_copy(step).wait()
        for copy in swaps[step * (GROUPS - 1):(step + 1) * (GROUPS - 1)]:
            copy.wait_recv()

    def local_moments():
        def chunk_moments(index, carry):
            values = staged[index].astype(jnp.float32).reshape(ROWS // 8, 8, CHUNK)
            for row, total in enumerate((jnp.sum(values, 0), jnp.sum(values * values, 0))):
                total = jnp.sum(total, 0, keepdims=True)
                for q in range(OWN):
                    moments[index, row * OWN + q:row * OWN + q + 1, :] = total[:, q * PANEL:(q + 1) * PANEL]
            return carry

        lax.fori_loop(0, GROUPS * SIDE, chunk_moments, 0)
        for extra in range(REACH):
            moments[GROUPS * SIDE + extra] = moments[extra]

    def group_moments_begin():
        gathered[0] = moments[pl.ds(group * SIDE, CHUNKS)]
        copies = []
        for offset in range(1, GROUPS):
            other = group_at(offset)
            copy = pltpu.make_async_remote_copy(
                src_ref=moments.at[pl.ds(other * SIDE, CHUNKS)],
                dst_ref=gathered.at[offset],
                send_sem=group_send.at[offset],
                recv_sem=group_recv.at[offset],
                device_id=(other * SIDE + x, core),
                device_id_type=MESH,
            )
            copy.start()
            copies.append(copy)
        return copies

    def ring_moments_begin(copies):
        for copy in copies:
            copy.wait()
        sums[0] = jnp.sum(gathered[...], 0)
        copies = []
        for index, peer in enumerate(peers):
            copy = pltpu.make_async_remote_copy(
                src_ref=sums.at[0],
                dst_ref=sums.at[index + 1],
                send_sem=stat_send.at[index],
                recv_sem=stat_recv.at[index],
                device_id=peer,
                device_id_type=MESH,
            )
            copy.start()
            copies.append(copy)
        return copies

    def ring_moments_end(copies):
        for copy in copies:
            copy.wait()
        totals[...] = jnp.sum(sums[...], 0)

    def standardize(step):
        chunk, start, count = STEPS[step]
        columns = pl.ds(start, count)
        panels = range(start // PANEL, (start + count) // PANEL)
        first, second = totals[chunk, 0:OWN], totals[chunk, OWN:2 * OWN]
        mean = first * (1.0 / SAMPLES)
        inv_scale = lax.rsqrt(second * (1.0 / SAMPLES) - mean * mean + 1e-05)
        mean = jnp.concatenate([mean[q:q + 1] for q in panels], axis=1)
        inv_scale = jnp.concatenate([inv_scale[q:q + 1] for q in panels], axis=1)

        def block_standard(block, carry):
            rows = pl.ds(pl.multiple_of(block * ROWS, ROWS), ROWS)
            values = received[chunk, block, :, columns].astype(jnp.float32)
            standard[chunk, rows, columns] = ((values - mean) * inv_scale).astype(jnp.bfloat16)
            return carry

        lax.fori_loop(0, GROUPS, block_standard, 0)
        if chunk < SIDE:
            turned[chunk] = standard[chunk].T

    def pieces_of(step):
        chunk, start, count = STEPS[step]
        pieces = []
        for d in range(REACH + 1):
            if 0 <= chunk - d < SIDE:
                inside = [
                    index for index, (p, q) in enumerate(PLACES[d])
                    if start // PANEL <= q < (start + count) // PANEL
                ]
                pieces.append((chunk - d, d, d + (start > 0), STARTS[d] + inside[0], len(inside)))
        return pieces

    def twin_copy(rows_chunk, number, first, count):
        which = pl.ds(first, count)
        return pltpu.make_async_remote_copy(
            src_ref=part.at[rows_chunk, 1 - core, which],
            dst_ref=twin.at[rows_chunk, which],
            send_sem=twin_send.at[rows_chunk, number],
            recv_sem=twin_recv.at[rows_chunk, number],
            device_id=(group * SIDE + x, 1 - core),
            device_id_type=MESH,
        )

    def multiply(step):
        chunk, start, columns = STEPS[step]
        for rows_chunk, d, number, first, count in pieces_of(step):
            for pp in range(OWN // 2):
                for qq in range(start // BLOCK, (start + columns) // BLOCK):
                    inside = [
                        (p, q) for p in range(2) for q in range(2) if (2 * pp + p, 2 * qq + q) in PLACES[d]
                    ]
                    if not inside:
                        continue
                    block = jnp.dot(
                        turned[rows_chunk, pp * BLOCK:(pp + 1) * BLOCK, :],
                        standard[chunk, :, qq * BLOCK:(qq + 1) * BLOCK],
                        preferred_element_type=jnp.float32,
                    )
                    for p, q in inside:
                        tile = STARTS[d] + PLACES[d].index((2 * pp + p, 2 * qq + q))
                        for half in range(2):
                            top = p * PANEL + half * (PANEL // 2)
                            part[rows_chunk, half, tile] = block[
                                top:top + PANEL // 2, q * PANEL:(q + 1) * PANEL
                            ]
            twin_copy(rows_chunk, number, first, count).start()

    def halves_of(first, count):
        upper = (count + 1) // 2
        return pl.ds(first, upper), pl.ds(first + upper, count - upper)

    def line_copy(rows_chunk, number, halves, half, way, relayed):
        which = halves[half]
        return pltpu.make_async_remote_copy(
            src_ref=part.at[rows_chunk, core, which],
            dst_ref=(relay if relayed else ring).at[way, which],
            send_sem=ring_send.at[rows_chunk, number, half],
            recv_sem=relay_recv.at[way, number] if relayed else ring_recv.at[way, number, half],
            device_id=(group * SIDE + lax.rem(x + 1 + 2 * way, SIDE), core),
            device_id_type=MESH,
        )

    def reduce(step):
        for rows_chunk, d, number, first, count in pieces_of(step):
            which = pl.ds(first, count)
            halves = halves_of(first, count)
            twin_copy(rows_chunk, number, first, count).wait()
            part[rows_chunk, core, which] = part[rows_chunk, core, which] + twin[rows_chunk, which]
            distance = lax.rem(rows_chunk - x + SIDE, SIDE)

            @pl.when(distance == 2)
            def _():
                line_copy(rows_chunk, number, halves, 0, 0, True).start()
                line_copy(rows_chunk, number, halves, 1, 1, True).start()

            @pl.when(distance == 1)
            def _():
                line_copy(rows_chunk, number, halves, 1, 0, False).start()

            @pl.when(distance == 3)
            def _():
                line_copy(rows_chunk, number, halves, 0, 1, False).start()

            pump(2)

        pump(2)
        for rows_chunk, d, number, first, count in pieces_of(step):
            halves = halves_of(first, count)
            distance = lax.rem(rows_chunk - x + SIDE, SIDE)
            for way in range(2):

                @pl.when(distance == 1 + 2 * way)
                def _():
                    which = halves[way]
                    line_copy(rows_chunk, number, halves, way, way, True).wait_recv()
                    part[rows_chunk, core, which] = part[rows_chunk, core, which] + relay[way, which]
                    line_copy(rows_chunk, number, halves, way, way, False).start()

    pump(8)
    for step in range(len(STEPS)):
        own_copy(step).start()
    lax.fori_loop(0, GROUPS * SIDE, stage_end, 0)
    local_moments()
    copies = group_moments_begin()
    pump(8)
    copies = ring_moments_begin(copies)
    pump(8)
    ring_moments_end(copies)
    for step in range(len(STEPS)):
        pump((step + 1) * (GROUPS - 1) + 8 - started[0])
        swap_end(step)
        standardize(step)
        multiply(step)
        pump(7)
        reduce(step)
    for copy in swaps[-AHEAD:]:
        copy.wait_send()

    for step in range(len(STEPS)):
        for rows_chunk, d, number, first, count in pieces_of(step):
            halves = halves_of(first, count)

            @pl.when(x != rows_chunk)
            def _():
                for half in range(2):
                    line_copy(rows_chunk, number, halves, half, 0, False).wait_send()

            @pl.when(x == rows_chunk)
            def _():
                for way in range(2):
                    for half in range(2):
                        line_copy(rows_chunk, number, halves, half, way, False).wait_recv()

    for d in range(REACH + 1):
        for index, (p, q) in enumerate(PLACES[d]):
            tile = STARTS[d] + index
            out_ref[p, d * OWN + q - p] = part[x, core, tile] + (ring[0, tile] + ring[1, tile])


def tiles(dosages):
    half_tile = (PANEL // 2, PANEL)
    dma = pltpu.SemaphoreType.DMA
    return pl.pallas_call(
        tiles_kernel,
        out_shape=jax.ShapeDtypeStruct((OWN, WMAX + 1) + half_tile, jnp.float32),
        in_specs=[pl.BlockSpec(memory_space=pltpu.HBM)],
        out_specs=pl.BlockSpec(memory_space=pltpu.VMEM),
        scratch_shapes=[
            pltpu.VMEM((GROUPS * SIDE, ROWS, CHUNK), jnp.bfloat16),
            pltpu.VMEM((CHUNKS, GROUPS, ROWS, CHUNK), jnp.bfloat16),
            pltpu.VMEM((GROUPS * SIDE + REACH, 2 * OWN, PANEL), jnp.float32),
            pltpu.VMEM((GROUPS, CHUNKS, 2 * OWN, PANEL), jnp.float32),
            pltpu.VMEM((8, CHUNKS, 2 * OWN, PANEL), jnp.float32),
            pltpu.VMEM((CHUNKS, 2 * OWN, PANEL), jnp.float32),
            pltpu.VMEM((CHUNKS, LOCAL, CHUNK), jnp.bfloat16),
            pltpu.VMEM((SIDE, CHUNK, LOCAL), jnp.bfloat16),
            pltpu.VMEM((SIDE, 2, TILES) + half_tile, jnp.float32),
            pltpu.VMEM((SIDE, TILES) + half_tile, jnp.float32),
            pltpu.VMEM((2, TILES) + half_tile, jnp.float32),
            pltpu.VMEM((2, TILES) + half_tile, jnp.float32),
            dma((GROUPS * SIDE,)),
            dma((len(STEPS),)),
            dma((len(STEPS), GROUPS)),
            dma((len(STEPS), GROUPS)),
            dma((GROUPS,)),
            dma((GROUPS,)),
            dma((7,)),
            dma((7,)),
            dma((SIDE, REACH + 2)),
            dma((SIDE, REACH + 2)),
            dma((2, REACH + 2)),
            dma((SIDE, REACH + 2, 2)),
            dma((2, REACH + 2, 2)),
        ],
        compiler_params=pltpu.CompilerParams(
            collective_id=0, has_side_effects=True, vmem_limit_bytes=52 * 1024 * 1024
        ),
        name="tiles",
    )(dosages)


def per_device(dosages, band_width):
    band_tiles = tiles(dosages)
    offsets = jnp.arange(WMAX + 1, dtype=jnp.int32)
    panel_count = OWN * lax.axis_size("var")
    global_panel = lax.axis_index("var") * OWN + jnp.arange(OWN, dtype=jnp.int32)
    in_band = (offsets[None, :] <= band_width[:, None]) & (
        global_panel[:, None] + offsets[None, :] < panel_count
    )
    return jnp.where(in_band[:, :, None, None], band_tiles * (1.0 / SAMPLES), 0.0)


def solution(mesh):
    in_specs = (P(("var", "samp"), None), P("var"))
    out_specs = P("var", None, "samp", None)
    return jax.shard_map(
        per_device, mesh=mesh, in_specs=in_specs, out_specs=out_specs, check_vma=False
    )
```

```python
import jax
import jax.numpy as jnp
from jax import lax
from jax.experimental import pallas as pl
from jax.experimental.pallas import tpu as pltpu
from jax.sharding import PartitionSpec as P

MESH = pl.DeviceIdType.MESH
WMAX = 8
PANEL = 128
SIDE = 4
GROUPS = SIDE * SIDE
OWN = 4
CHUNK = OWN * PANEL
REACH = WMAX // OWN
CHUNKS = SIDE + REACH
ROWS = 64
LOCAL = GROUPS * ROWS
BLOCK = 2 * PANEL
STEPS = [(chunk, 0, CHUNK) for chunk in range(CHUNKS)]
AHEAD = 24
ORDER = [10, 15, 1, 4, 6, 3, 9, 12, 11, 14, 7, 13, 2, 8, 5]
PARTNER = [1, 0, 3, 2, 5, 4, 7, 6, 9, 8, 11, 10, 13, 12, 14]
SAMPLES = 8192
PLACES = [
    [(p, q) for q in range(OWN) for p in range(OWN) if 0 <= d * OWN + q - p <= WMAX] for d in range(REACH + 1)
]
STARTS = [sum(len(places) for places in PLACES[:d]) for d in range(REACH + 2)]
TILES = STARTS[-1]


def position():
    var = lax.axis_index("var")
    return var // SIDE, lax.rem(var, SIDE), lax.axis_index("samp")


def tiles_kernel(
    dos_ref, out_ref, staged, received, moments, gathered, sums, totals, standard, turned, part, twin, relay, ring,
    stage_sem, own_sem, swap_send, swap_recv, group_send, group_recv, stat_send, stat_recv, twin_send, twin_recv, relay_recv, ring_send, ring_recv,
):
    group, x, core = position()
    z, y = group // SIDE, lax.rem(group, SIDE)

    def stage(index):
        first = pl.multiple_of(index * CHUNK, CHUNK)
        return pltpu.make_async_copy(dos_ref.at[:, pl.ds(first, CHUNK)], staged.at[index], stage_sem.at[index])

    def stage_begin(index, carry):
        stage(index).start()
        return carry

    def stage_end(index, carry):
        stage(index).wait()
        return carry

    lax.fori_loop(0, GROUPS * SIDE, stage_begin, 0)

    peers = []
    for dx in range(SIDE):
        for dc in range(2):
            if dx or dc:
                peer_x, peer_c = lax.rem(x + dx, SIDE), lax.rem(core + dc, 2)
                peers.append((group * SIDE + peer_x, peer_c))

    def group_at(offset):
        return lax.rem(z + offset // SIDE, SIDE) * SIDE + lax.rem(y + lax.rem(offset, SIDE), SIDE)

    barrier = pltpu.get_barrier_semaphore()
    for offset in range(1, GROUPS):
        pl.semaphore_signal(
            barrier, inc=1, device_id=(group_at(offset) * SIDE + x, core), device_id_type=MESH
        )
    for peer in peers:
        pl.semaphore_signal(barrier, inc=1, device_id=peer, device_id_type=MESH)
    pl.semaphore_wait(barrier, GROUPS - 1 + len(peers))

    def columns_of(other, chunk, first, count):
        top = lax.rem(other * SIDE + chunk, GROUPS * SIDE) * CHUNK + first
        return dos_ref.at[:, pl.ds(pl.multiple_of(top, BLOCK), count)]

    def swap(index):
        step, turn = divmod(index, GROUPS - 1)
        chunk, first, count = STEPS[step]
        columns = pl.ds(first, count)
        offset = ORDER[turn] + core * (ORDER[PARTNER[turn]] - ORDER[turn])
        other = group_at(offset)
        return pltpu.make_async_remote_copy(
            src_ref=columns_of(other, chunk, first, count),
            dst_ref=received.at[chunk, offset, :, columns],
            send_sem=swap_send.at[step, offset],
            recv_sem=swap_recv.at[step, offset],
            device_id=(other * SIDE + x, core),
            device_id_type=MESH,
        )

    swaps = [swap(index) for index in range(len(STEPS) * (GROUPS - 1))]
    started = [0]

    def pump(count):
        for index in range(started[0], min(started[0] + count, len(swaps))):
            if index >= AHEAD:
                swaps[index - AHEAD].wait_send()
            swaps[index].start()
            started[0] = index + 1

    def own_copy(step):
        chunk, first, count = STEPS[step]
        columns = pl.ds(first, count)
        return pltpu.make_async_copy(
            columns_of(group, chunk, first, count),
            received.at[chunk, 0, :, columns],
            own_sem.at[step],
        )

    def swap_end(step):
        own_copy(step).wait()
        for copy in swaps[step * (GROUPS - 1):(step + 1) * (GROUPS - 1)]:
            copy.wait_recv()

    def local_moments():
        def chunk_moments(index, carry):
            values = staged[index].astype(jnp.float32).reshape(ROWS // 8, 8, CHUNK)
            for row, total in enumerate((jnp.sum(values, 0), jnp.sum(values * values, 0))):
                total = jnp.sum(total, 0, keepdims=True)
                for q in range(OWN):
                    moments[index, row * OWN + q:row * OWN + q + 1, :] = total[:, q * PANEL:(q + 1) * PANEL]
            return carry

        lax.fori_loop(0, GROUPS * SIDE, chunk_moments, 0)
        for extra in range(REACH):
            moments[GROUPS * SIDE + extra] = moments[extra]

    def group_moments_begin():
        gathered[0] = moments[pl.ds(group * SIDE, CHUNKS)]
        copies = []
        for offset in range(1, GROUPS):
            other = group_at(offset)
            copy = pltpu.make_async_remote_copy(
                src_ref=moments.at[pl.ds(other * SIDE, CHUNKS)],
                dst_ref=gathered.at[offset],
                send_sem=group_send.at[offset],
                recv_sem=group_recv.at[offset],
                device_id=(other * SIDE + x, core),
                device_id_type=MESH,
            )
            copy.start()
            copies.append(copy)
        return copies

    def ring_moments_begin(copies):
        for copy in copies:
            copy.wait()
        sums[0] = jnp.sum(gathered[...], 0)
        copies = []
        for index, peer in enumerate(peers):
            copy = pltpu.make_async_remote_copy(
                src_ref=sums.at[0],
                dst_ref=sums.at[index + 1],
                send_sem=stat_send.at[index],
                recv_sem=stat_recv.at[index],
                device_id=peer,
                device_id_type=MESH,
            )
            copy.start()
            copies.append(copy)
        return copies

    def ring_moments_end(copies):
        for copy in copies:
            copy.wait()
        totals[...] = jnp.sum(sums[...], 0)

    def standardize(step):
        chunk, start, count = STEPS[step]
        columns = pl.ds(start, count)
        panels = range(start // PANEL, (start + count) // PANEL)
        first, second = totals[chunk, 0:OWN], totals[chunk, OWN:2 * OWN]
        mean = first * (1.0 / SAMPLES)
        inv_scale = lax.rsqrt(second * (1.0 / SAMPLES) - mean * mean + 1e-05)
        mean = jnp.concatenate([mean[q:q + 1] for q in panels], axis=1)
        inv_scale = jnp.concatenate([inv_scale[q:q + 1] for q in panels], axis=1)

        def block_standard(block, carry):
            rows = pl.ds(pl.multiple_of(block * ROWS, ROWS), ROWS)
            values = received[chunk, block, :, columns].astype(jnp.float32)
            standard[chunk, rows, columns] = ((values - mean) * inv_scale).astype(jnp.bfloat16)
            return carry

        lax.fori_loop(0, GROUPS, block_standard, 0)
        if chunk < SIDE:
            turned[chunk] = standard[chunk].T

    def pieces_of(step):
        chunk, start, count = STEPS[step]
        pieces = []
        for d in range(REACH + 1):
            if 0 <= chunk - d < SIDE:
                inside = [
                    index for index, (p, q) in enumerate(PLACES[d])
                    if start // PANEL <= q < (start + count) // PANEL
                ]
                pieces.append((chunk - d, d, d + (start > 0), STARTS[d] + inside[0], len(inside)))
        return pieces

    def twin_copy(rows_chunk, number, first, count):
        which = pl.ds(first, count)
        return pltpu.make_async_remote_copy(
            src_ref=part.at[rows_chunk, 1 - core, which],
            dst_ref=twin.at[rows_chunk, which],
            send_sem=twin_send.at[rows_chunk, number],
            recv_sem=twin_recv.at[rows_chunk, number],
            device_id=(group * SIDE + x, 1 - core),
            device_id_type=MESH,
        )

    def multiply(step):
        chunk, start, columns = STEPS[step]
        for rows_chunk, d, number, first, count in pieces_of(step):
            for pp in range(OWN // 2):
                for qq in range(start // BLOCK, (start + columns) // BLOCK):
                    inside = [
                        (p, q) for p in range(2) for q in range(2) if (2 * pp + p, 2 * qq + q) in PLACES[d]
                    ]
                    if not inside:
                        continue
                    block = jnp.dot(
                        turned[rows_chunk, pp * BLOCK:(pp + 1) * BLOCK, :],
                        standard[chunk, :, qq * BLOCK:(qq + 1) * BLOCK],
                        preferred_element_type=jnp.float32,
                    )
                    for p, q in inside:
                        tile = STARTS[d] + PLACES[d].index((2 * pp + p, 2 * qq + q))
                        for half in range(2):
                            top = p * PANEL + half * (PANEL // 2)
                            part[rows_chunk, half, tile] = block[
                                top:top + PANEL // 2, q * PANEL:(q + 1) * PANEL
                            ]
            twin_copy(rows_chunk, number, first, count).start()

    def halves_of(first, count):
        upper = (count + 1) // 2
        return pl.ds(first, upper), pl.ds(first + upper, count - upper)

    def line_copy(rows_chunk, number, halves, half, way, relayed):
        which = halves[half]
        return pltpu.make_async_remote_copy(
            src_ref=part.at[rows_chunk, core, which],
            dst_ref=(relay if relayed else ring).at[way, which],
            send_sem=ring_send.at[rows_chunk, number, half],
            recv_sem=relay_recv.at[way, number] if relayed else ring_recv.at[way, number, half],
            device_id=(group * SIDE + lax.rem(x + 1 + 2 * way, SIDE), core),
            device_id_type=MESH,
        )

    def reduce(steps):
        pieces = [piece for step in steps for piece in pieces_of(step)]
        for rows_chunk, d, number, first, count in pieces:
            which = pl.ds(first, count)
            halves = halves_of(first, count)
            twin_copy(rows_chunk, number, first, count).wait()
            part[rows_chunk, core, which] = part[rows_chunk, core, which] + twin[rows_chunk, which]
            distance = lax.rem(rows_chunk - x + SIDE, SIDE)

            @pl.when(distance == 2)
            def _():
                line_copy(rows_chunk, number, halves, 0, 0, True).start()
                line_copy(rows_chunk, number, halves, 1, 1, True).start()

            @pl.when(distance == 1)
            def _():
                line_copy(rows_chunk, number, halves, 1, 0, False).start()

            @pl.when(distance == 3)
            def _():
                line_copy(rows_chunk, number, halves, 0, 1, False).start()

            pump(4)

        pump(3)
        for rows_chunk, d, number, first, count in pieces:
            halves = halves_of(first, count)
            distance = lax.rem(rows_chunk - x + SIDE, SIDE)
            for way in range(2):

                @pl.when(distance == 1 + 2 * way)
                def _():
                    which = halves[way]
                    line_copy(rows_chunk, number, halves, way, way, True).wait_recv()
                    part[rows_chunk, core, which] = part[rows_chunk, core, which] + relay[way, which]
                    line_copy(rows_chunk, number, halves, way, way, False).start()

    pump(8)
    for step in range(len(STEPS)):
        own_copy(step).start()
    lax.fori_loop(0, GROUPS * SIDE, stage_end, 0)
    local_moments()
    copies = group_moments_begin()
    pump(8)
    copies = ring_moments_begin(copies)
    pump(8)
    ring_moments_end(copies)
    for step in range(len(STEPS)):
        pump((step + 1) * (GROUPS - 1) + AHEAD - started[0])
        swap_end(step)
        standardize(step)
        multiply(step)
        pump(2)
        if step:
            reduce([0, 1] if step == 1 else [step])
    for copy in swaps[-AHEAD:]:
        copy.wait_send()

    for step in range(len(STEPS)):
        for rows_chunk, d, number, first, count in pieces_of(step):
            halves = halves_of(first, count)

            @pl.when(x != rows_chunk)
            def _():
                for half in range(2):
                    line_copy(rows_chunk, number, halves, half, 0, False).wait_send()

            @pl.when(x == rows_chunk)
            def _():
                for way in range(2):
                    for half in range(2):
                        line_copy(rows_chunk, number, halves, half, way, False).wait_recv()

    for d in range(REACH + 1):
        for index, (p, q) in enumerate(PLACES[d]):
            tile = STARTS[d] + index
            out_ref[p, d * OWN + q - p] = part[x, core, tile] + (ring[0, tile] + ring[1, tile])


def tiles(dosages):
    half_tile = (PANEL // 2, PANEL)
    dma = pltpu.SemaphoreType.DMA
    return pl.pallas_call(
        tiles_kernel,
        out_shape=jax.ShapeDtypeStruct((OWN, WMAX + 1) + half_tile, jnp.float32),
        in_specs=[pl.BlockSpec(memory_space=pltpu.HBM)],
        out_specs=pl.BlockSpec(memory_space=pltpu.VMEM),
        scratch_shapes=[
            pltpu.VMEM((GROUPS * SIDE, ROWS, CHUNK), jnp.bfloat16),
            pltpu.VMEM((CHUNKS, GROUPS, ROWS, CHUNK), jnp.bfloat16),
            pltpu.VMEM((GROUPS * SIDE + REACH, 2 * OWN, PANEL), jnp.float32),
            pltpu.VMEM((GROUPS, CHUNKS, 2 * OWN, PANEL), jnp.float32),
            pltpu.VMEM((8, CHUNKS, 2 * OWN, PANEL), jnp.float32),
            pltpu.VMEM((CHUNKS, 2 * OWN, PANEL), jnp.float32),
            pltpu.VMEM((CHUNKS, LOCAL, CHUNK), jnp.bfloat16),
            pltpu.VMEM((SIDE, CHUNK, LOCAL), jnp.bfloat16),
            pltpu.VMEM((SIDE, 2, TILES) + half_tile, jnp.float32),
            pltpu.VMEM((SIDE, TILES) + half_tile, jnp.float32),
            pltpu.VMEM((2, TILES) + half_tile, jnp.float32),
            pltpu.VMEM((2, TILES) + half_tile, jnp.float32),
            dma((GROUPS * SIDE,)),
            dma((len(STEPS),)),
            dma((len(STEPS), GROUPS)),
            dma((len(STEPS), GROUPS)),
            dma((GROUPS,)),
            dma((GROUPS,)),
            dma((7,)),
            dma((7,)),
            dma((SIDE, REACH + 2)),
            dma((SIDE, REACH + 2)),
            dma((2, REACH + 2)),
            dma((SIDE, REACH + 2, 2)),
            dma((2, REACH + 2, 2)),
        ],
        compiler_params=pltpu.CompilerParams(
            collective_id=0, has_side_effects=True, vmem_limit_bytes=52 * 1024 * 1024
        ),
        name="tiles",
    )(dosages)


def per_device(dosages, band_width):
    band_tiles = tiles(dosages)
    offsets = jnp.arange(WMAX + 1, dtype=jnp.int32)
    panel_count = OWN * lax.axis_size("var")
    global_panel = lax.axis_index("var") * OWN + jnp.arange(OWN, dtype=jnp.int32)
    in_band = (offsets[None, :] <= band_width[:, None]) & (
        global_panel[:, None] + offsets[None, :] < panel_count
    )
    return jnp.where(in_band[:, :, None, None], band_tiles * (1.0 / SAMPLES), 0.0)


def solution(mesh):
    in_specs = (P(("var", "samp"), None), P("var"))
    out_specs = P("var", None, "samp", None)
    return jax.shard_map(
        per_device, mesh=mesh, in_specs=in_specs, out_specs=out_specs, check_vma=False
    )
```

```python
import jax
import jax.numpy as jnp
from jax import lax
from jax.experimental import pallas as pl
from jax.experimental.pallas import tpu as pltpu
from jax.sharding import PartitionSpec as P

MESH = pl.DeviceIdType.MESH
WMAX = 8
PANEL = 128
SIDE = 4
GROUPS = SIDE * SIDE
OWN = 4
CHUNK = OWN * PANEL
REACH = WMAX // OWN
CHUNKS = SIDE + REACH
ROWS = 64
LOCAL = GROUPS * ROWS
BLOCK = 2 * PANEL
STEPS = [(chunk, 0, CHUNK) for chunk in range(CHUNKS)]
AHEAD = 30
ORDER = [10, 15, 1, 4, 6, 3, 9, 12, 11, 14, 7, 13, 2, 8, 5]
PARTNER = [1, 0, 3, 2, 5, 4, 7, 6, 9, 8, 11, 10, 13, 12, 14]
SAMPLES = 8192
PLACES = [
    [(p, q) for q in range(OWN) for p in range(OWN) if 0 <= d * OWN + q - p <= WMAX] for d in range(REACH + 1)
]
STARTS = [sum(len(places) for places in PLACES[:d]) for d in range(REACH + 2)]
TILES = STARTS[-1]


def position():
    var = lax.axis_index("var")
    return var // SIDE, lax.rem(var, SIDE), lax.axis_index("samp")


def tiles_kernel(
    dos_ref, out_ref, staged, received, moments, gathered, sums, totals, standard, turned, part, twin, relay, ring,
    stage_sem, own_sem, swap_send, swap_recv, group_send, group_recv, stat_send, stat_recv, twin_send, twin_recv, relay_recv, ring_send, ring_recv,
):
    group, x, core = position()
    z, y = group // SIDE, lax.rem(group, SIDE)

    def stage(index):
        first = pl.multiple_of(index * CHUNK, CHUNK)
        return pltpu.make_async_copy(dos_ref.at[:, pl.ds(first, CHUNK)], staged.at[index], stage_sem.at[index])

    def stage_begin(index, carry):
        stage(index).start()
        return carry

    def stage_end(index, carry):
        stage(index).wait()
        return carry

    lax.fori_loop(0, GROUPS * SIDE, stage_begin, 0)

    peers = []
    for dx in range(SIDE):
        for dc in range(2):
            if dx or dc:
                peer_x, peer_c = lax.rem(x + dx, SIDE), lax.rem(core + dc, 2)
                peers.append((group * SIDE + peer_x, peer_c))

    def group_at(offset):
        return lax.rem(z + offset // SIDE, SIDE) * SIDE + lax.rem(y + lax.rem(offset, SIDE), SIDE)

    barrier = pltpu.get_barrier_semaphore()
    for offset in range(1, GROUPS):
        pl.semaphore_signal(
            barrier, inc=1, device_id=(group_at(offset) * SIDE + x, core), device_id_type=MESH
        )
    for peer in peers:
        pl.semaphore_signal(barrier, inc=1, device_id=peer, device_id_type=MESH)
    pl.semaphore_wait(barrier, GROUPS - 1 + len(peers))

    def columns_of(other, chunk, first, count):
        top = lax.rem(other * SIDE + chunk, GROUPS * SIDE) * CHUNK + first
        return dos_ref.at[:, pl.ds(pl.multiple_of(top, BLOCK), count)]

    def swap(index):
        step, turn = divmod(index, GROUPS - 1)
        chunk, first, count = STEPS[step]
        columns = pl.ds(first, count)
        offset = ORDER[turn] + core * (ORDER[PARTNER[turn]] - ORDER[turn])
        other = group_at(offset)
        return pltpu.make_async_remote_copy(
            src_ref=columns_of(other, chunk, first, count),
            dst_ref=received.at[chunk, offset, :, columns],
            send_sem=swap_send.at[step, offset],
            recv_sem=swap_recv.at[step, offset],
            device_id=(other * SIDE + x, core),
            device_id_type=MESH,
        )

    swaps = [swap(index) for index in range(len(STEPS) * (GROUPS - 1))]
    started = [0]

    def pump(count):
        for index in range(started[0], min(started[0] + count, len(swaps))):
            if index >= AHEAD:
                swaps[index - AHEAD].wait_send()
            swaps[index].start()
            started[0] = index + 1

    def own_copy(step):
        chunk, first, count = STEPS[step]
        columns = pl.ds(first, count)
        return pltpu.make_async_copy(
            columns_of(group, chunk, first, count),
            received.at[chunk, 0, :, columns],
            own_sem.at[step],
        )

    def swap_end(step):
        own_copy(step).wait()
        for copy in swaps[step * (GROUPS - 1):(step + 1) * (GROUPS - 1)]:
            copy.wait_recv()

    def local_moments():
        def chunk_moments(index, carry):
            values = staged[index].astype(jnp.float32).reshape(ROWS // 8, 8, CHUNK)
            for row, total in enumerate((jnp.sum(values, 0), jnp.sum(values * values, 0))):
                total = jnp.sum(total, 0, keepdims=True)
                for q in range(OWN):
                    moments[index, row * OWN + q:row * OWN + q + 1, :] = total[:, q * PANEL:(q + 1) * PANEL]
            return carry

        lax.fori_loop(0, GROUPS * SIDE, chunk_moments, 0)
        for extra in range(REACH):
            moments[GROUPS * SIDE + extra] = moments[extra]

    def group_moments_begin():
        gathered[0] = moments[pl.ds(group * SIDE, CHUNKS)]
        copies = []
        for offset in range(1, GROUPS):
            other = group_at(offset)
            copy = pltpu.make_async_remote_copy(
                src_ref=moments.at[pl.ds(other * SIDE, CHUNKS)],
                dst_ref=gathered.at[offset],
                send_sem=group_send.at[offset],
                recv_sem=group_recv.at[offset],
                device_id=(other * SIDE + x, core),
                device_id_type=MESH,
            )
            copy.start()
            copies.append(copy)
        return copies

    def ring_moments_begin(copies):
        for copy in copies:
            copy.wait()
        sums[0] = jnp.sum(gathered[...], 0)
        copies = []
        for index, peer in enumerate(peers):
            copy = pltpu.make_async_remote_copy(
                src_ref=sums.at[0],
                dst_ref=sums.at[index + 1],
                send_sem=stat_send.at[index],
                recv_sem=stat_recv.at[index],
                device_id=peer,
                device_id_type=MESH,
            )
            copy.start()
            copies.append(copy)
        return copies

    def ring_moments_end(copies):
        for copy in copies:
            copy.wait()
        totals[...] = jnp.sum(sums[...], 0)

    def standardize(step):
        chunk, start, count = STEPS[step]
        columns = pl.ds(start, count)
        panels = range(start // PANEL, (start + count) // PANEL)
        first, second = totals[chunk, 0:OWN], totals[chunk, OWN:2 * OWN]
        mean = first * (1.0 / SAMPLES)
        inv_scale = lax.rsqrt(second * (1.0 / SAMPLES) - mean * mean + 1e-05)
        mean = jnp.concatenate([mean[q:q + 1] for q in panels], axis=1)
        inv_scale = jnp.concatenate([inv_scale[q:q + 1] for q in panels], axis=1)

        def block_standard(block, carry):
            rows = pl.ds(pl.multiple_of(block * ROWS, ROWS), ROWS)
            values = received[chunk, block, :, columns].astype(jnp.float32)
            standard[chunk, rows, columns] = ((values - mean) * inv_scale).astype(jnp.bfloat16)
            return carry

        lax.fori_loop(0, GROUPS, block_standard, 0)
        if chunk < SIDE:
            turned[chunk] = standard[chunk].T

    def pieces_of(step):
        chunk, start, count = STEPS[step]
        pieces = []
        for d in range(REACH + 1):
            if 0 <= chunk - d < SIDE:
                inside = [
                    index for index, (p, q) in enumerate(PLACES[d])
                    if start // PANEL <= q < (start + count) // PANEL
                ]
                pieces.append((chunk - d, d, d + (start > 0), STARTS[d] + inside[0], len(inside)))
        return pieces

    def twin_copy(rows_chunk, number, first, count):
        which = pl.ds(first, count)
        return pltpu.make_async_remote_copy(
            src_ref=part.at[rows_chunk, 1 - core, which],
            dst_ref=twin.at[rows_chunk, which],
            send_sem=twin_send.at[rows_chunk, number],
            recv_sem=twin_recv.at[rows_chunk, number],
            device_id=(group * SIDE + x, 1 - core),
            device_id_type=MESH,
        )

    def multiply(step):
        chunk, start, columns = STEPS[step]
        for rows_chunk, d, number, first, count in pieces_of(step):
            for pp in range(OWN // 2):
                for qq in range(start // BLOCK, (start + columns) // BLOCK):
                    inside = [
                        (p, q) for p in range(2) for q in range(2) if (2 * pp + p, 2 * qq + q) in PLACES[d]
                    ]
                    if not inside:
                        continue
                    block = jnp.dot(
                        turned[rows_chunk, pp * BLOCK:(pp + 1) * BLOCK, :],
                        standard[chunk, :, qq * BLOCK:(qq + 1) * BLOCK],
                        preferred_element_type=jnp.float32,
                    )
                    for p, q in inside:
                        tile = STARTS[d] + PLACES[d].index((2 * pp + p, 2 * qq + q))
                        for half in range(2):
                            top = p * PANEL + half * (PANEL // 2)
                            part[rows_chunk, half, tile] = block[
                                top:top + PANEL // 2, q * PANEL:(q + 1) * PANEL
                            ]
            twin_copy(rows_chunk, number, first, count).start()

    def halves_of(first, count):
        upper = (count + 1) // 2
        return pl.ds(first, upper), pl.ds(first + upper, count - upper)

    def line_copy(rows_chunk, number, halves, half, way, relayed):
        which = halves[half]
        return pltpu.make_async_remote_copy(
            src_ref=part.at[rows_chunk, core, which],
            dst_ref=(relay if relayed else ring).at[way, which],
            send_sem=ring_send.at[rows_chunk, number, half],
            recv_sem=relay_recv.at[way, number] if relayed else ring_recv.at[way, number, half],
            device_id=(group * SIDE + lax.rem(x + 1 + 2 * way, SIDE), core),
            device_id_type=MESH,
        )

    def reduce(step):
        for rows_chunk, d, number, first, count in pieces_of(step):
            which = pl.ds(first, count)
            halves = halves_of(first, count)
            twin_copy(rows_chunk, number, first, count).wait()
            part[rows_chunk, core, which] = part[rows_chunk, core, which] + twin[rows_chunk, which]
            distance = lax.rem(rows_chunk - x + SIDE, SIDE)

            @pl.when(distance == 2)
            def _():
                line_copy(rows_chunk, number, halves, 0, 0, True).start()
                line_copy(rows_chunk, number, halves, 1, 1, True).start()

            @pl.when(distance == 1)
            def _():
                line_copy(rows_chunk, number, halves, 1, 0, False).start()

            @pl.when(distance == 3)
            def _():
                line_copy(rows_chunk, number, halves, 0, 1, False).start()

            pump(4)

        pump(3)
        for rows_chunk, d, number, first, count in pieces_of(step):
            halves = halves_of(first, count)
            distance = lax.rem(rows_chunk - x + SIDE, SIDE)
            for way in range(2):

                @pl.when(distance == 1 + 2 * way)
                def _():
                    which = halves[way]
                    line_copy(rows_chunk, number, halves, way, way, True).wait_recv()
                    part[rows_chunk, core, which] = part[rows_chunk, core, which] + relay[way, which]
                    line_copy(rows_chunk, number, halves, way, way, False).start()

    pump(8)
    for step in range(len(STEPS)):
        own_copy(step).start()
    lax.fori_loop(0, GROUPS * SIDE, stage_end, 0)
    local_moments()
    copies = group_moments_begin()
    pump(8)
    copies = ring_moments_begin(copies)
    pump(8)
    ring_moments_end(copies)
    for step in range(len(STEPS)):
        pump((step + 1) * (GROUPS - 1) + AHEAD - started[0])
        swap_end(step)
        standardize(step)
        multiply(step)
        pump(2)
        reduce(step)
    for copy in swaps[-AHEAD:]:
        copy.wait_send()

    for step in range(len(STEPS)):
        for rows_chunk, d, number, first, count in pieces_of(step):
            halves = halves_of(first, count)

            @pl.when(x != rows_chunk)
            def _():
                for half in range(2):
                    line_copy(rows_chunk, number, halves, half, 0, False).wait_send()

            @pl.when(x == rows_chunk)
            def _():
                for way in range(2):
                    for half in range(2):
                        line_copy(rows_chunk, number, halves, half, way, False).wait_recv()

    for d in range(REACH + 1):
        for index, (p, q) in enumerate(PLACES[d]):
            tile = STARTS[d] + index
            out_ref[p, d * OWN + q - p] = part[x, core, tile] + (ring[0, tile] + ring[1, tile])


def tiles(dosages):
    half_tile = (PANEL // 2, PANEL)
    dma = pltpu.SemaphoreType.DMA
    return pl.pallas_call(
        tiles_kernel,
        out_shape=jax.ShapeDtypeStruct((OWN, WMAX + 1) + half_tile, jnp.float32),
        in_specs=[pl.BlockSpec(memory_space=pltpu.HBM)],
        out_specs=pl.BlockSpec(memory_space=pltpu.VMEM),
        scratch_shapes=[
            pltpu.VMEM((GROUPS * SIDE, ROWS, CHUNK), jnp.bfloat16),
            pltpu.VMEM((CHUNKS, GROUPS, ROWS, CHUNK), jnp.bfloat16),
            pltpu.VMEM((GROUPS * SIDE + REACH, 2 * OWN, PANEL), jnp.float32),
            pltpu.VMEM((GROUPS, CHUNKS, 2 * OWN, PANEL), jnp.float32),
            pltpu.VMEM((8, CHUNKS, 2 * OWN, PANEL), jnp.float32),
            pltpu.VMEM((CHUNKS, 2 * OWN, PANEL), jnp.float32),
            pltpu.VMEM((CHUNKS, LOCAL, CHUNK), jnp.bfloat16),
            pltpu.VMEM((SIDE, CHUNK, LOCAL), jnp.bfloat16),
            pltpu.VMEM((SIDE, 2, TILES) + half_tile, jnp.float32),
            pltpu.VMEM((SIDE, TILES) + half_tile, jnp.float32),
            pltpu.VMEM((2, TILES) + half_tile, jnp.float32),
            pltpu.VMEM((2, TILES) + half_tile, jnp.float32),
            dma((GROUPS * SIDE,)),
            dma((len(STEPS),)),
            dma((len(STEPS), GROUPS)),
            dma((len(STEPS), GROUPS)),
            dma((GROUPS,)),
            dma((GROUPS,)),
            dma((7,)),
            dma((7,)),
            dma((SIDE, REACH + 2)),
            dma((SIDE, REACH + 2)),
            dma((2, REACH + 2)),
            dma((SIDE, REACH + 2, 2)),
            dma((2, REACH + 2, 2)),
        ],
        compiler_params=pltpu.CompilerParams(
            collective_id=0, has_side_effects=True, vmem_limit_bytes=52 * 1024 * 1024
        ),
        name="tiles",
    )(dosages)


def per_device(dosages, band_width):
    band_tiles = tiles(dosages)
    offsets = jnp.arange(WMAX + 1, dtype=jnp.int32)
    panel_count = OWN * lax.axis_size("var")
    global_panel = lax.axis_index("var") * OWN + jnp.arange(OWN, dtype=jnp.int32)
    in_band = (offsets[None, :] <= band_width[:, None]) & (
        global_panel[:, None] + offsets[None, :] < panel_count
    )
    return jnp.where(in_band[:, :, None, None], band_tiles * (1.0 / SAMPLES), 0.0)


def solution(mesh):
    in_specs = (P(("var", "samp"), None), P("var"))
    out_specs = P("var", None, "samp", None)
    return jax.shard_map(
        per_device, mesh=mesh, in_specs=in_specs, out_specs=out_specs, check_vma=False
    )
```
